32 devices in a mesh: frame: 4 (over y, core), pack: 8 (over z, x).
Axes of the slice: x: 2, y: 2, z: 4, core: 2. Of those that a mesh axis runs over, the one named last changes fastest.
Arguments:
- tokens: bfloat16 [32, 8, 256, 384], P('pack', 'frame'), may hold values from -6 to 6
- condition: bfloat16 [32, 8, 384], P('pack', 'frame'), may hold values from -6 to 6
- clip_lengths: int32 [32, 4], P('pack'), may hold values from 0 to 8, as said below
- ada_weight: bfloat16 [384, 3456], replicated, may hold values from -0.3125 to 0.3125
- spatial_qkv: bfloat16 [384, 1152], replicated, may hold values from -0.3125 to 0.3125
- spatial_out: bfloat16 [384, 384], replicated, may hold values from -1.25 to 1.25
- temporal_qkv: bfloat16 [384, 1152], replicated, may hold values from -0.3125 to 0.3125
- temporal_out: bfloat16 [384, 384], replicated, may hold values from -0.875 to 0.875
- mlp_up: bfloat16 [384, 1536], replicated, may hold values from -0.3125 to 0.3125
- mlp_down: bfloat16 [1536, 384], replicated, may hold values from -0.15625 to 0.15625
- cotangent: bfloat16 [32, 8, 256, 384], P('pack', 'frame'), may hold values from -6 to 6
Outputs:
- output: bfloat16 [32, 8, 256, 384], P('pack', 'frame')
- tokens_grad: float32 [32, 8, 256, 384], P('pack', 'frame')
- condition_grad: float32 [32, 8, 384], P('pack', 'frame')
- ada_grad: float32 [384, 3456], replicated
- spatial_qkv_grad: float32 [384, 1152], replicated
- spatial_out_grad: float32 [384, 384], replicated
- temporal_qkv_grad: float32 [384, 1152], replicated
- temporal_out_grad: float32 [384, 384], replicated
- mlp_up_grad: float32 [384, 1536], replicated
- mlp_down_grad: float32 [1536, 384], replicated
The draws below stay inside these ranges and needn't reach their ends.
Inputs may be any that keep to these rules, and one draw needn't show every extreme that they name: `clip_lengths`: row b lists the lengths of the clips of pack b in frame order, each 2, 4 or 8, summing to 8, then zeros. Of the 4 consecutive packs that share an index of pack, at least one is a single clip of 8 frames.
All inputs are finite; a program needn't handle non-finite values.
Results may differ from the reference program's by a relative error of at most 0.02.
The reference program's roundings to bfloat16 on the way count: a program that leaves them out, or rounds other values in their place, can miss the bound.
Values may be sent and summed in bfloat16 or wider, within the bound.
No kernel may reach another device: no remote copies, remote signals or barrier semaphores. Data moves between devices by JAX's collectives and lax.ppermute only.
A program may use at most 192 MiB of HBM per device.

```python
import jax
import jax.numpy as jnp
from jax import lax

D = 384
HEADS = 6
HEAD_DIM = 64
MLP = 1536
PATCHES = 256
MICRO = 4
FRAMES = 8
PACKS = 32


def draw_clip_lengths(key, part):
    key = jax.random.fold_in(key, 7)
    patterns = jnp.array([[4, 0, 0, 0], [2, 2, 0, 0], [2, 1, 1, 0], [1, 2, 1, 0], [1, 1, 2, 0], [1, 1, 1, 1]], jnp.int32)
    pattern_key, single_key = jax.random.split(key)
    pattern_index = jax.random.randint(pattern_key, (PACKS,), 0, 6)
    groups = PACKS // MICRO
    single_slot = jax.random.randint(single_key, (groups,), 0, MICRO)
    forced = jnp.arange(PACKS, dtype=jnp.int32) % MICRO == jnp.repeat(single_slot, MICRO)
    pattern_index = jnp.where(forced, 0, pattern_index)
    return (patterns[pattern_index] * (FRAMES // 4)).astype(jnp.int32)


def steps_of(rng, dims, cuts, smallest, top_value):
    level = 1.0
    for dim, parts in cuts:
        draws = jax.random.uniform(jax.random.fold_in(jax.random.fold_in(rng, 6), dim), (parts,), jnp.float32, smallest / len(cuts), top_value / len(cuts))
        level = level * jnp.repeat(jnp.exp(draws), dims[dim] // parts).reshape((-1,) + (1,) * (len(dims) - 1 - dim))
    return level


def normal_values(own_key, extent, scale, bound, cuts=(), held_as=jnp.bfloat16):
    gain = steps_of(own_key, extent, cuts, -0.22, 0.18) if cuts else 1.0
    drawn = jax.random.normal(own_key, extent, jnp.float32) * scale * gain
    return jnp.minimum(jnp.maximum(drawn, -bound), bound).astype(held_as)


def setup_inputs(seed: int = 0) -> dict:
    arg_keys = jax.random.split(jax.random.key(seed), 12)
    tokens = normal_values(arg_keys[0], (PACKS, FRAMES, PATCHES, D), 1.0, 6.0, ((0, 8), (1, 4)))
    condition = normal_values(arg_keys[1], (PACKS, FRAMES, D), 1.0, 6.0, ((0, 8), (1, 4)))
    clip_lengths = draw_clip_lengths(jax.random.fold_in(arg_keys[11], 71), 0)
    ada_weight = normal_values(arg_keys[3], (D, 9 * D), D ** -0.5, 0.3125)
    spatial_qkv = normal_values(arg_keys[4], (D, 3 * D), D ** -0.5, 0.3125)
    spatial_out = normal_values(arg_keys[5], (D, D), (D // 16) ** -0.5, 1.25)
    temporal_qkv = normal_values(arg_keys[6], (D, 3 * D), D ** -0.5, 0.3125)
    temporal_out = normal_values(arg_keys[7], (D, D), (D // 8) ** -0.5, 0.875)
    mlp_up = normal_values(arg_keys[8], (D, MLP), D ** -0.5, 0.3125)
    mlp_down = normal_values(arg_keys[9], (MLP, D), MLP ** -0.5, 0.15625)
    cotangent = normal_values(arg_keys[10], (PACKS, FRAMES, PATCHES, D), 1.0, 6.0, ((0, 8), (1, 4)))
    return dict(tokens=tokens, condition=condition, clip_lengths=clip_lengths, ada_weight=ada_weight, spatial_qkv=spatial_qkv, spatial_out=spatial_out, temporal_qkv=temporal_qkv, temporal_out=temporal_out, mlp_up=mlp_up, mlp_down=mlp_down, cotangent=cotangent)


@jax.custom_vjp
def low(v):
    return lax.optimization_barrier(v.astype(jnp.bfloat16)).astype(jnp.float32)

@jax.custom_vjp
def low_back(v):
    return v

def low_keep(v):
    return (low(v), None)

def low_pass(kept, grad):
    return (grad,)

def back_keep(v):
    return (v, None)

def back_low(kept, grad):
    return (low(grad),)
low.defvjp(low_keep, low_pass)
low_back.defvjp(back_keep, back_low)

def product(left, right):
    return jnp.einsum('...i,ij->...j', left, right, precision=lax.Precision.HIGHEST)

def normalize(values, shift, scale):
    average = lax.optimization_barrier(jnp.mean(values, axis=-1, keepdims=True))
    centered = values - average
    variance = lax.optimization_barrier(jnp.mean(centered * centered, axis=-1, keepdims=True))
    return centered * lax.rsqrt(variance + 1e-06) * (1.0 + scale) + shift

def gelu_tanh(values):
    inner = 0.7978845608028654 * (values + 0.044715 * values * values * values)
    return 0.5 * values * (1.0 + jnp.tanh(inner))

def attend(query, keys, values, allowed):
    batch, length = (query.shape[0], query.shape[1])
    heads_query = query.reshape(batch, length, HEADS, HEAD_DIM)
    heads_keys = keys.reshape(batch, length, HEADS, HEAD_DIM)
    heads_values = values.reshape(batch, length, HEADS, HEAD_DIM)
    raw = jnp.einsum('blhe,bmhe->bhlm', heads_query, heads_keys, precision=lax.Precision.HIGHEST) * HEAD_DIM ** (-0.5)
    scores = low_back(jnp.where(allowed, raw, -1e+30))
    highest = lax.optimization_barrier(jnp.max(scores, axis=-1, keepdims=True))
    expanded = jnp.exp(scores - highest)
    weights = low(expanded / lax.optimization_barrier(jnp.sum(expanded, axis=-1, keepdims=True)))
    mixed = jnp.einsum('bhlm,bmhe->blhe', weights, heads_values, precision=lax.Precision.HIGHEST)
    return low(low_back(mixed.reshape(batch, length, HEADS * HEAD_DIM)))

def pack_forward(weights, inputs, condition, same_clip):
    ada_weight, spatial_qkv, spatial_out, temporal_qkv, temporal_out, mlp_up, mlp_down = weights
    modulation = low_back(product(low(jax.nn.silu(condition)), ada_weight))
    pieces = [modulation[:, None, index * D:(index + 1) * D] for index in range(9)]
    first = low(normalize(inputs, pieces[0], pieces[1]))
    qkv_first = low(low_back(product(first, spatial_qkv)))
    mixed_first = attend(qkv_first[..., :D], qkv_first[..., D:2 * D], qkv_first[..., 2 * D:], True)
    branch_first = low_back(product(mixed_first, spatial_out))
    after_first = inputs + pieces[2] * branch_first
    second = low(normalize(after_first, pieces[3], pieces[4]))
    qkv_second = jnp.swapaxes(low(low_back(product(second, temporal_qkv))), 0, 1)
    mixed_second = attend(qkv_second[..., :D], qkv_second[..., D:2 * D], qkv_second[..., 2 * D:], same_clip)
    mixed_second = jnp.swapaxes(mixed_second, 0, 1)
    branch_second = low_back(product(mixed_second, temporal_out))
    after_second = after_first + pieces[5] * branch_second
    third = low(normalize(after_second, pieces[6], pieces[7]))
    hidden = low(gelu_tanh(low_back(product(third, mlp_up))))
    branch_third = low_back(product(hidden, mlp_down))
    return after_second + pieces[8] * branch_third

def reference(tokens, condition, clip_lengths, ada_weight, spatial_qkv, spatial_out, temporal_qkv, temporal_out, mlp_up, mlp_down, cotangent):
    weights = tuple((matrix.astype(jnp.float32) for matrix in (ada_weight, spatial_qkv, spatial_out, temporal_qkv, temporal_out, mlp_up, mlp_down)))
    frame_ids = jnp.arange(FRAMES, dtype=jnp.int32)

    def one_pack(totals, slices):
        inputs, cond_row, lengths, cotan_row = slices
        ends = jnp.cumsum(lengths).astype(jnp.int32)
        segment = lax.optimization_barrier(jnp.sum((ends[None, :] <= frame_ids[:, None]).astype(jnp.int32), axis=1))
        same_clip = segment[:, None] == segment[None, :]

        def forward(values, cond_values, weight_values):
            return pack_forward(weight_values, values, cond_values, same_clip)
        result, pullback = jax.vjp(forward, inputs.astype(jnp.float32), cond_row.astype(jnp.float32), weights)
        grad_inputs, grad_cond, grad_weights = pullback(cotan_row.astype(jnp.float32))
        totals = jax.tree.map(jnp.add, totals, grad_weights)
        return (totals, (result.astype(jnp.bfloat16), grad_inputs, grad_cond))
    zeros = tuple((jnp.zeros_like(matrix) for matrix in weights))
    totals, stacked = lax.scan(one_pack, zeros, (tokens, condition, clip_lengths, cotangent))
    return (stacked[0], stacked[1], stacked[2], totals[0], totals[1], totals[2], totals[3], totals[4], totals[5], totals[6])
```

```python
import functools

import jax
import jax.numpy as jnp
from jax import lax
from jax.experimental import pallas as pl
from jax.experimental.pallas import tpu as pltpu
from jax.sharding import PartitionSpec as P

D = 384
HEADS = 6
HD = 64
MLP = 1536
F32 = jnp.float32
BF16 = jnp.bfloat16
CHUNKS = 2
GROUP = 16
VMEM = 58 * 2**20


def nn(a, b):
    return lax.dot_general(a, b, (((1,), (0,)), ((), ())), preferred_element_type=F32)


def nt(a, b):
    return lax.dot_general(a, b, (((1,), (1,)), ((), ())), preferred_element_type=F32)


def tn(a, b):
    return lax.dot_general(a, b, (((0,), (0,)), ((), ())), preferred_element_type=F32)


def norm_stats(x):
    c = x - jnp.mean(x, -1, keepdims=True)
    r = lax.rsqrt(jnp.mean(c * c, -1, keepdims=True) + 1e-6)
    return c * r, r


def norm_back(h, n, r):
    return r * (h - jnp.mean(h, -1, keepdims=True) - n * jnp.mean(h * n, -1, keepdims=True))


def spatial_fwd(idx, tok, mod, w_t, wo, qkv_o, mix_o, br_o, tot_o, *rest):
    slots, scr = rest[:-1], rest[-1]
    rows = slots[0].shape[2]
    x = tok[0, 0].astype(F32)
    n, _ = norm_stats(x)
    md = mod[0, 0]
    first = (n * (1.0 + md[1:2]) + md[0:1]).astype(BF16)
    qkv_o[0, 0] = nt(w_t[...], first).astype(BF16)
    for h in range(HEADS):
        a = h * HD
        q = qkv_o[0, 0, a : a + HD] * BF16(0.125)
        k = qkv_o[0, 0, D + a : D + a + HD]
        v = qkv_o[0, 0, 2 * D + a : 2 * D + a + HD]
        s = tn(k, q)
        mx = jnp.max(s, axis=0, keepdims=True)
        p = jnp.exp(s - mx)
        total = jnp.sum(p, axis=0, keepdims=True)
        o = nn(v, p.astype(BF16)) * (1.0 / total)
        tot_o[0, 0, h : h + 1] = mx + jnp.log(total)
        mix_o[0, 0, a : a + HD] = o.astype(BF16)
    br = tn(mix_o[0, 0], wo[...])
    br_o[0, 0] = br.astype(BF16)
    scr[...] = (x + md[2:3] * br).astype(BF16)
    i = idx[0]
    for k, slot in enumerate(slots):
        slot[0, 0] = scr[pl.ds(pl.multiple_of((i ^ k) * rows, GROUP), rows), :]


def call_spatial_fwd(idx, tok, mod, w_t, wo, start, count, n):
    f = tok.shape[1]
    p = tok.shape[2]
    whole = lambda *s: pl.BlockSpec((1, 1) + s, lambda b, f, i: (b + start, f) + (0,) * len(s))
    part = lambda *s: pl.BlockSpec((1, 1) + s, lambda b, f, i: (b, f) + (0,) * len(s))
    fixed = lambda *s: pl.BlockSpec(s, lambda b, f, i: (0,) * len(s))
    sd = lambda s, d: jax.ShapeDtypeStruct((count, f) + s, d)
    return pl.pallas_call(
        spatial_fwd,
        grid_spec=pltpu.PrefetchScalarGridSpec(
            num_scalar_prefetch=1,
            grid=(count, f),
            in_specs=[whole(p, D), whole(3, D), fixed(3 * D, D), fixed(D, D)],
            out_specs=[part(3 * D, p), part(D, p), part(p, D), part(HEADS, p)]
            + [part(p // n, D)] * n,
            scratch_shapes=[pltpu.VMEM((p, D), BF16)],
        ),
        out_shape=[sd((3 * D, p), BF16), sd((D, p), BF16), sd((p, D), BF16), sd((HEADS, p), F32)]
        + [sd((p // n, D), BF16)] * n,
        compiler_params=pltpu.CompilerParams(vmem_limit_bytes=VMEM),
        name="spatial_fwd",
    )(idx, tok, mod, w_t, wo)


def gather_tile(refs, groups):
    f = refs[0].shape[1]
    return jnp.concatenate(
        [
            r[0, j, g * GROUP : (g + 1) * GROUP, :]
            for g in range(groups)
            for r in refs
            for j in range(f)
        ],
        axis=0,
    )


def scatter_tile(refs, value, groups):
    f = refs[0].shape[1]
    at = 0
    for g in range(groups):
        for r in refs:
            for j in range(f):
                r[0, j, g * GROUP : (g + 1) * GROUP, :] = value[at : at + GROUP]
                at += GROUP


def middle(n, first_chunk, *refs):
    refs = list(refs)
    a1, refs = refs[:n], refs[n:]
    ct, refs = refs[:n], refs[n:]
    mod, bias, tq_t, tq, to, up, down = refs[:7]
    refs = refs[7:]
    if not first_chunk:
        inits, refs = refs[:3], refs[3:]
    dl, refs = refs[:n], refs[n:]
    ou, refs = refs[:n], refs[n:]
    gsum, acc_up, acc_down, acc_t = refs[:4]
    qkv_s, p_s, mix_s, dg_s, hid_s, dqkv_s = refs[4:]
    groups = a1[0].shape[2] // GROUP
    frames = n * a1[0].shape[1]
    span = frames * GROUP
    tokens = span * groups

    @pl.when(pl.program_id(0) == 0)
    def _():
        if first_chunk:
            acc_up[...] = jnp.zeros_like(acc_up)
            acc_down[...] = jnp.zeros_like(acc_down)
            acc_t[...] = jnp.zeros_like(acc_t)
        else:
            acc_up[...] = inits[0][...]
            acc_down[...] = inits[1][...]
            acc_t[...] = inits[2][...]

    def per_frame(piece, plus=0.0):
        m = mod[0, :, piece : piece + 1, :] + plus
        return jnp.broadcast_to(m[None], (groups, frames, GROUP, D)).reshape(tokens, D)

    def frame_sum(v):
        return jnp.sum(jnp.sum(v.reshape(groups, frames, GROUP, D), axis=0), axis=1)

    x1 = gather_tile(a1, groups).astype(F32)
    n2, r2 = norm_stats(x1)
    second = (n2 * per_frame(1, 1.0) + per_frame(0)).astype(BF16)
    qkv_s[...] = nt(tq_t[...], second).astype(BF16)
    for g in range(groups):
        cols = slice(g * span, (g + 1) * span)
        for h in range(HEADS):
            a = h * HD
            q = qkv_s[a : a + HD, cols] * BF16(0.125)
            k = qkv_s[D + a : D + a + HD, cols]
            v = qkv_s[2 * D + a : 2 * D + a + HD, cols]
            s = tn(k, q) + bias[0]
            p = jnp.exp(s - jnp.max(s, axis=0, keepdims=True))
            p = p * (1.0 / jnp.sum(p, axis=0, keepdims=True))
            p_s[g * HEADS + h] = p
            mix_s[a : a + HD, cols] = nn(v, p.astype(BF16)).astype(BF16)
    br2 = tn(mix_s[...], to[...])
    x2 = x1 + per_frame(2) * br2
    n3, r3 = norm_stats(x2)
    third = (n3 * per_frame(4, 1.0) + per_frame(3)).astype(BF16)
    step = 256
    br3 = jnp.zeros((tokens, D), F32)
    for c in range(0, MLP, step):
        pre = nn(third, up[:, c : c + step])
        sq = pre * pre
        t = jnp.tanh(pre * (0.7978845608028654 + (0.7978845608028654 * 0.044715) * sq))
        half = 0.5 + 0.5 * t
        hid = (pre * half).astype(BF16)
        hid_s[:, c : c + step] = hid
        inner = 0.7978845608028654 + (3 * 0.7978845608028654 * 0.044715) * sq
        dg_s[:, c : c + step] = half + 0.5 * pre * (1.0 - t * t) * inner
        br3 += nn(hid, down[c : c + step, :])
    gate3 = per_frame(5)
    scatter_tile(ou, (x2 + gate3 * br3).astype(BF16), groups)
    cot = gather_tile(ct, groups).astype(F32)
    gsum[0, :, 5] = frame_sum(cot * br3)
    gb3 = (gate3 * cot).astype(BF16)
    gb3_t = gb3.T
    third_t = third.T
    g3 = jnp.zeros((tokens, D), F32)
    for c in range(0, MLP, step):
        acc_down[:, c : c + step] += nn(gb3_t, hid_s[:, c : c + step])
        gp = (nt(gb3, down[c : c + step, :]) * dg_s[:, c : c + step]).astype(BF16)
        acc_up[:, c : c + step] += nn(third_t, gp)
        g3 += nt(gp, up[:, c : c + step])
    gsum[0, :, 3] = frame_sum(g3)
    gsum[0, :, 4] = frame_sum(g3 * n3)
    dx3 = norm_back(g3 * per_frame(4, 1.0), n3, r3)
    ga2 = cot + dx3
    gsum[0, :, 2] = frame_sum(ga2 * br2)
    gb2 = (per_frame(2) * ga2).astype(BF16)
    acc_t[:, 3 * D :] += nn(mix_s[...], gb2)
    gm_t = nt(to[...], gb2).astype(BF16)
    for g in range(groups):
        cols = slice(g * span, (g + 1) * span)
        for h in range(HEADS):
            a = h * HD
            q = qkv_s[a : a + HD, cols] * BF16(0.125)
            k = qkv_s[D + a : D + a + HD, cols]
            v = qkv_s[2 * D + a : 2 * D + a + HD, cols]
            go = gm_t[a : a + HD, cols]
            p = p_s[g * HEADS + h]
            dp = tn(v, go)
            ds = (p * (dp - jnp.sum(p * dp, axis=0, keepdims=True))).astype(BF16)
            dqkv_s[2 * D + a : 2 * D + a + HD, cols] = nt(go, p.astype(BF16)).astype(BF16)
            dqkv_s[D + a : D + a + HD, cols] = nt(q, ds).astype(BF16)
            dqkv_s[a : a + HD, cols] = (nn(k, ds) * 0.125).astype(BF16)
    dqkv = dqkv_s[...]
    acc_t[:, : 3 * D] += nt(second.T, dqkv)
    g2 = nn(tq[...], dqkv).T
    gsum[0, :, 0] = frame_sum(g2)
    gsum[0, :, 1] = frame_sum(g2 * n2)
    dx2 = norm_back(g2 * per_frame(1, 1.0), n2, r2)
    scatter_tile(dl, (dx3 + dx2).astype(BF16), groups)


def call_middle(a1, ct, mod, bias, tq_t, tq, to, up, down, inits, start):
    n = len(a1)
    count, f, rows = a1[0].shape[:3]
    frames = n * f
    span = frames * GROUP
    tokens = frames * rows
    groups = rows // GROUP
    part = lambda *s: pl.BlockSpec((1,) + s, lambda b: (b,) + (0,) * len(s))
    whole = lambda *s: pl.BlockSpec((1,) + s, lambda b: (b + start,) + (0,) * len(s))
    fixed = lambda *s: pl.BlockSpec(s, lambda b: (0,) * len(s), pipeline_mode=pl.Buffered(1))
    accs = [(D, MLP)] * 3
    sd = jax.ShapeDtypeStruct
    return pl.pallas_call(
        functools.partial(middle, n, not inits),
        grid=(count,),
        in_specs=[part(f, rows, D)] * n
        + [whole(f, rows, D)] * n
        + [whole(frames, 6, D), whole(span, span), fixed(3 * D, D), fixed(D, 3 * D)]
        + [fixed(D, D), fixed(D, MLP), fixed(MLP, D)]
        + [fixed(*s) for s in accs[: len(inits)]],
        out_specs=[part(f, rows, D)] * (2 * n)
        + [part(frames, 6, D)]
        + [pl.BlockSpec(s, lambda b: (0, 0)) for s in accs],
        out_shape=[sd((count, f, rows, D), BF16)] * (2 * n)
        + [sd((count, frames, 6, D), F32)]
        + [sd(s, F32) for s in accs],
        scratch_shapes=[
            pltpu.VMEM((3 * D, tokens), BF16),
            pltpu.VMEM((groups * HEADS, span, span), F32),
            pltpu.VMEM((D, tokens), BF16),
            pltpu.VMEM((tokens, MLP), F32),
            pltpu.VMEM((tokens, MLP), BF16),
            pltpu.VMEM((3 * D, tokens), BF16),
        ],
        compiler_params=pltpu.CompilerParams(vmem_limit_bytes=VMEM),
        name="middle",
    )(*a1, *ct, mod, bias, tq_t, tq, to, up, down, *inits)


def spatial_bwd(n, first_chunk, idx, tok, cot, mod, qkv, mix, br, tot, wo, *rest):
    rest = list(rest)
    if not first_chunk:
        init, rest = rest[0], rest[1:]
    dl, rest = rest[:n], rest[n:]
    dqkv_o, ga_o, gg_o, acc, scr = rest

    @pl.when((pl.program_id(0) == 0) & (pl.program_id(1) == 0))
    def _():
        acc[...] = jnp.zeros_like(acc) if first_chunk else init[...]

    rows = dl[0].shape[2]
    i = idx[0]
    for k in range(n):
        scr[pl.ds(pl.multiple_of((i ^ k) * rows, GROUP), rows), :] = dl[k][0, 0]
    ga = cot[0, 0].astype(F32) + scr[...].astype(F32)
    ga_o[0, 0] = ga
    md = mod[0, 0]
    gg_o[0, 0] = jnp.sum(ga * br[0, 0].astype(F32), axis=0, keepdims=True)
    gb = (md[2:3] * ga).astype(BF16)
    acc[:, 3 * D :] += nn(mix[0, 0], gb)
    gm = nt(wo[...], gb).astype(BF16)
    for h in range(HEADS):
        a = h * HD
        q = qkv[0, 0, a : a + HD] * BF16(0.125)
        k = qkv[0, 0, D + a : D + a + HD]
        v = qkv[0, 0, 2 * D + a : 2 * D + a + HD]
        go = gm[a : a + HD]
        p = jnp.exp(tn(k, q) - tot[0, 0, h : h + 1])
        dp = tn(v, go)
        ds = (p * (dp - jnp.sum(p * dp, axis=0, keepdims=True))).astype(BF16)
        dqkv_o[0, 0, 2 * D + a : 2 * D + a + HD] = nt(go, p.astype(BF16)).astype(BF16)
        dqkv_o[0, 0, D + a : D + a + HD] = nt(q, ds).astype(BF16)
        dqkv_o[0, 0, a : a + HD] = (nn(k, ds) * 0.125).astype(BF16)
    nrm, _ = norm_stats(tok[0, 0].astype(F32))
    first = (nrm * (1.0 + md[1:2]) + md[0:1]).astype(BF16)
    acc[:, : 3 * D] += nt(first.T, dqkv_o[0, 0])


def call_spatial_bwd(idx, tok, cot, mod, qkv, mix, br, tot, wo, init, dl, start):
    n = len(dl)
    count, f, rows = dl[0].shape[:3]
    p = tok.shape[2]
    whole = lambda *s: pl.BlockSpec((1, 1) + s, lambda b, f, i: (b + start, f) + (0,) * len(s))
    part = lambda *s: pl.BlockSpec((1, 1) + s, lambda b, f, i: (b, f) + (0,) * len(s))
    fixed = lambda *s: pl.BlockSpec(s, lambda b, f, i: (0,) * len(s), pipeline_mode=pl.Buffered(1))
    sd = lambda s, d: jax.ShapeDtypeStruct((count, f) + s, d)
    return pl.pallas_call(
        functools.partial(spatial_bwd, n, not init),
        grid_spec=pltpu.PrefetchScalarGridSpec(
            num_scalar_prefetch=1,
            grid=(count, f),
            in_specs=[whole(p, D), whole(p, D), whole(3, D), part(3 * D, p), part(D, p)]
            + [part(p, D), part(HEADS, p), fixed(D, D)]
            + [fixed(D, MLP)] * len(init)
            + [part(rows, D)] * n,
            out_specs=[part(3 * D, p), part(p, D), part(1, D)]
            + [pl.BlockSpec((D, MLP), lambda b, f, i: (0, 0))],
            scratch_shapes=[pltpu.VMEM((p, D), BF16)],
        ),
        out_shape=[sd((3 * D, p), BF16), sd((p, D), F32), sd((1, D), F32)]
        + [jax.ShapeDtypeStruct((D, MLP), F32)],
        compiler_params=pltpu.CompilerParams(vmem_limit_bytes=VMEM),
        name="spatial_bwd",
    )(idx, tok, cot, mod, qkv, mix, br, tot, wo, *init, *dl)


def last_step(n, idx, tok, mod, w_t, dqkv, ga, *rest):
    ou, rest = rest[:n], rest[n:]
    grad_o, out_o, gs_o = rest
    rows = ou[0].shape[2]
    i = idx[0]
    for k in range(n):
        out_o[0, 0, pl.ds(pl.multiple_of((i ^ k) * rows, GROUP), rows), :] = ou[k][0, 0]
    g = tn(dqkv[0, 0], w_t[...])
    nrm, r = norm_stats(tok[0, 0].astype(F32))
    md = mod[0, 0]
    gs_o[0, 0, 0:1] = jnp.sum(g, axis=0, keepdims=True)
    gs_o[0, 0, 1:2] = jnp.sum(g * nrm, axis=0, keepdims=True)
    grad_o[0, 0] = ga[0, 0] + norm_back(g * (1.0 + md[1:2]), nrm, r)


def call_last(idx, tok, mod, w_t, dqkv, ga, ou, start):
    n = len(ou)
    count, f, rows = ou[0].shape[:3]
    p = tok.shape[2]
    whole = lambda *s: pl.BlockSpec((1, 1) + s, lambda b, f, i: (b + start, f) + (0,) * len(s))
    part = lambda *s: pl.BlockSpec((1, 1) + s, lambda b, f, i: (b, f) + (0,) * len(s))
    fixed = lambda *s: pl.BlockSpec(s, lambda b, f, i: (0,) * len(s), pipeline_mode=pl.Buffered(1))
    sd = lambda s, d: jax.ShapeDtypeStruct((count, f) + s, d)
    return pl.pallas_call(
        functools.partial(last_step, n),
        grid_spec=pltpu.PrefetchScalarGridSpec(
            num_scalar_prefetch=1,
            grid=(count, f),
            in_specs=[whole(p, D), whole(3, D), fixed(3 * D, D), part(3 * D, p), part(p, D)]
            + [part(rows, D)] * n,
            out_specs=[part(p, D), part(p, D), part(2, D)],
        ),
        out_shape=[sd((p, D), F32), sd((p, D), BF16), sd((2, D), F32)],
        compiler_params=pltpu.CompilerParams(vmem_limit_bytes=VMEM),
        name="last_step",
    )(idx, tok, mod, w_t, dqkv, ga, *ou)


def swap(x, axis, mask):
    size = lax.axis_size(axis)
    return lax.ppermute(x, axis, [(s, s ^ mask) for s in range(size)])


def bits_of(axis):
    return [(axis, b) for b in range(lax.axis_size(axis).bit_length() - 1)]


def bit_of(axis, b):
    return (lax.axis_index(axis) >> b) & 1


def reduce_all(g):
    frame, pack = bits_of("frame"), bits_of("pack")
    steps = frame[:1] + pack + frame[1:]
    halved = []
    for axis, b in steps:
        rows = g.shape[0]
        if rows % 32 == 0:
            mine = bit_of(axis, b)
            half = rows // 2
            send = lax.dynamic_slice_in_dim(g, (1 - mine) * half, half, 0).astype(BF16)
            keep = lax.dynamic_slice_in_dim(g, mine * half, half, 0)
            g = keep.astype(F32) + swap(send, axis, 1 << b).astype(F32)
            halved.append((axis, b))
        else:
            send = g.astype(BF16)
            g = send.astype(F32) + swap(send, axis, 1 << b).astype(F32)
    g = g.astype(BF16)
    return spread(g, halved[::-1])


def spread(g, steps):
    for axis, b in steps:
        other = swap(g, axis, 1 << b)
        mine = bit_of(axis, b) == 1
        g = jnp.concatenate([jnp.where(mine, other, g), jnp.where(mine, g, other)], axis=0)
    return g


def local(
    tokens,
    condition,
    clip_lengths,
    ada_weight,
    spatial_qkv,
    spatial_out,
    temporal_qkv,
    temporal_out,
    mlp_up,
    mlp_down,
    cotangent,
):
    n = lax.axis_size("frame")
    i = lax.axis_index("frame")
    idx = i.reshape(1).astype(jnp.int32)
    packs, f, patches = tokens.shape[:3]
    rows = patches // n
    count = packs // CHUNKS
    every = bits_of("frame") + bits_of("pack")

    cut = lambda v, k: lax.dynamic_slice_in_dim(v, (i ^ k) * rows, rows, 2)
    send = lambda parts: [parts[0]] + [swap(parts[k], "frame", k) for k in range(1, n)]

    silu = lambda v: v / (1.0 + jnp.exp(-v))
    cond_slots = send([condition] * n)
    activated = silu(condition.astype(F32)).astype(BF16)
    act_slots = silu(jnp.stack(cond_slots, 1).astype(F32)).astype(BF16)
    dot = functools.partial(jnp.einsum, preferred_element_type=F32)
    mod_own = dot("bfi,ij->bfj", activated, ada_weight[:, : 3 * D]).reshape(packs, f, 3, D)
    mod_all = dot("bkfi,ij->bkfj", act_slots, ada_weight[:, 3 * D :])
    mod_all = mod_all.reshape(packs, n * f, 6, D)

    frame_ids = jnp.concatenate([(i ^ k) * f + jnp.arange(f, dtype=jnp.int32) for k in range(n)])
    width = clip_lengths.shape[1]
    ends = [jnp.sum(clip_lengths[:, : j + 1], axis=1) for j in range(width)]
    segment = sum((e[:, None] <= frame_ids[None, :]).astype(jnp.int32) for e in ends)
    segment = jnp.repeat(segment, GROUP, axis=1)
    patch = jnp.tile(jnp.arange(GROUP, dtype=jnp.int32), n * f)
    allowed = (segment[:, :, None] == segment[:, None, :]) & (patch[:, None] == patch[None, :])
    bias = jnp.where(allowed, 0.0, -1e30).astype(F32)

    sq_t = spatial_qkv.T
    tq_t = temporal_qkv.T
    ct = send([cut(cotangent, k) for k in range(n)])

    fwd = []
    for c in range(CHUNKS):
        res = call_spatial_fwd(idx, tokens, mod_own, sq_t, spatial_out, c * count, count, n)
        fwd.append((res[:4], send(list(res[4:]))))

    accs, mids = [], []
    for c in range(CHUNKS):
        res = call_middle(
            fwd[c][1], ct, mod_all, bias, tq_t, temporal_qkv, temporal_out, mlp_up, mlp_down,
            accs, c * count,
        )
        accs = list(res[2 * n + 1 :])
        sums = res[2 * n].reshape(count, n, f, 6, D)
        mids.append((send(list(res[:n])), send(list(res[n : 2 * n])), send([sums[:, k] for k in range(n)])))
    early = reduce_all(jnp.concatenate(accs, axis=0))

    acc, backs = [], []
    for c in range(CHUNKS):
        qkv, mix, br, tot = fwd[c][0]
        res = call_spatial_bwd(
            idx, tokens, cotangent, mod_own, qkv, mix, br, tot, spatial_out, acc, mids[c][0],
            c * count,
        )
        acc = [res[3]]
        backs.append(res)
    late = reduce_all(acc[0])

    lasts = []
    for c in range(CHUNKS):
        dqkv, ga, gate_sum, _ = backs[c]
        lasts.append(call_last(idx, tokens, mod_own, sq_t, dqkv, ga, mids[c][1], c * count))
    grad_tokens = jnp.concatenate([v[0] for v in lasts], 0)
    output = jnp.concatenate([v[1] for v in lasts], 0)

    grad_mod = jnp.concatenate(
        [
            jnp.concatenate([lasts[c][2], backs[c][2], sum(mids[c][2])], axis=2)
            for c in range(CHUNKS)
        ],
        axis=0,
    ).astype(BF16)
    grad_mod = grad_mod.reshape(packs * f, 9 * D)
    all_act = spread(activated.reshape(packs * f, D), every)
    all_mod = spread(grad_mod, every)
    grad_ada = dot("ti,tj->ij", all_act, all_mod)
    back = dot("tj,ij->ti", grad_mod, ada_weight).reshape(packs, f, D)
    cf = condition.astype(F32)
    sig = 1.0 / (1.0 + jnp.exp(-cf))
    grad_condition = back * (sig * (1.0 + cf * (1.0 - sig)))

    early = early.astype(F32)
    late = late.astype(F32)
    return (
        output,
        grad_tokens,
        grad_condition,
        grad_ada,
        late[:, : 3 * D],
        late[:, 3 * D :],
        early[2 * D :, : 3 * D],
        early[2 * D :, 3 * D :],
        early[:D],
        early[D : 2 * D].T,
    )


def solution(mesh):
    tok = P("pack", "frame", None, None)
    cond = P("pack", "frame", None)
    return jax.shard_map(
        local,
        mesh=mesh,
        in_specs=(tok, cond, P("pack", None), P(), P(), P(), P(), P(), P(), P(), tok),
        out_specs=(tok, tok, cond, P(), P(), P(), P(), P(), P(), P()),
        check_vma=False,
    )
```

```python
import functools

import jax
import jax.numpy as jnp
from jax import lax
from jax.experimental import pallas as pl
from jax.experimental.pallas import tpu as pltpu
from jax.sharding import PartitionSpec as P

D = 384
HEADS = 6
HD = 64
MLP = 1536
F32 = jnp.float32
BF16 = jnp.bfloat16
CHUNKS = 2
GROUP = 16
VMEM = 58 * 2**20


def nn(a, b):
    return lax.dot_general(a, b, (((1,), (0,)), ((), ())), preferred_element_type=F32)


def nt(a, b):
    return lax.dot_general(a, b, (((1,), (1,)), ((), ())), preferred_element_type=F32)


def tn(a, b):
    return lax.dot_general(a, b, (((0,), (0,)), ((), ())), preferred_element_type=F32)


def cost(us):
    return pl.CostEstimate(flops=int(us * 1.0e9), bytes_accessed=1000, transcendentals=0)


def on_diagonal(pair):
    none = jnp.zeros_like(pair[:HD])
    return jnp.concatenate(
        [
            jnp.concatenate([pair[:HD], none], axis=1),
            jnp.concatenate([none, pair[HD:]], axis=1),
        ],
        axis=0,
    )


def norm_stats(x):
    c = x - jnp.mean(x, -1, keepdims=True)
    r = lax.rsqrt(jnp.mean(c * c, -1, keepdims=True) + 1e-6)
    return c * r, r


def norm_back(h, n, r):
    return r * (h - jnp.mean(h, -1, keepdims=True) - n * jnp.mean(h * n, -1, keepdims=True))


def divide(mine, acc, sent, kept):
    half = sent.shape[0]
    for j in range(half):
        sent[j] = acc[(1 - mine) * half + j].astype(BF16)
        kept[j] = acc[mine * half + j].astype(BF16)


def silu_low(v):
    v = v.astype(F32)
    return (v / (1.0 + jnp.exp(-v))).astype(BF16)


def spatial_fwd(start, idx, tok, cond, ada, w_t, wo, qkv_o, mix_o, br_o, tot_o, mod_o, *rest):
    slots, (scr, mod_s) = rest[:-2], rest[-2:]
    rows = slots[0].shape[2]
    frames = pl.num_programs(1)
    at = pl.program_id(0) * frames + pl.program_id(1)

    @pl.when(at == 0)
    def _():
        mod_s[...] = nn(silu_low(cond[...]), ada[...])

    at = at + start * frames
    md = [mod_s[pl.ds(at, 1), j * D : (j + 1) * D] for j in range(3)]
    for j in range(3):
        mod_o[0, 0, j : j + 1] = md[j]
    x = tok[0, 0].astype(F32)
    n, _ = norm_stats(x)
    first = (n * (1.0 + md[1]) + md[0]).astype(BF16)
    qkv_o[0, 0] = nt(w_t[...], first).astype(BF16)
    for j in range(HEADS // 2):
        a = j * 2 * HD
        q = on_diagonal(qkv_o[0, 0, a : a + 2 * HD] * BF16(0.125))
        k = qkv_o[0, 0, D + a : D + a + 2 * HD]
        s = tn(k, q)
        mx = jnp.max(s, axis=0, keepdims=True)
        p = jnp.exp(s - mx)
        total = jnp.sum(p, axis=0, keepdims=True)
        tot_o[0, 0, j : j + 1] = mx + jnp.log(total)
        p = p.astype(BF16)
        scale = 1.0 / total
        cut = q.shape[1] // 2
        for e in range(2):
            v = qkv_o[0, 0, 2 * D + a + e * HD : 2 * D + a + (e + 1) * HD]
            cols = slice(e * cut, (e + 1) * cut)
            mix_o[0, 0, a + e * HD : a + (e + 1) * HD] = (nn(v, p[:, cols]) * scale[:, cols]).astype(BF16)
    br = tn(mix_o[0, 0], wo[...])
    br_o[0, 0] = br.astype(BF16)
    scr[...] = (x + md[2] * br).astype(BF16)
    i = idx[0]
    for k, slot in enumerate(slots):
        slot[0, 0] = scr[pl.ds(pl.multiple_of((i ^ k) * rows, GROUP), rows), :]


def call_spatial_fwd(idx, tok, cond, ada, w_t, wo, start, count, n):
    f = tok.shape[1]
    p = tok.shape[2]
    whole = lambda *s: pl.BlockSpec((1, 1) + s, lambda b, f, i: (b + start, f) + (0,) * len(s))
    part = lambda *s: pl.BlockSpec((1, 1) + s, lambda b, f, i: (b, f) + (0,) * len(s))
    fixed = lambda *s: pl.BlockSpec(s, lambda b, f, i: (0,) * len(s), pipeline_mode=pl.Buffered(1))
    sd = lambda s, d: jax.ShapeDtypeStruct((count, f) + s, d)
    return pl.pallas_call(
        functools.partial(spatial_fwd, start),
        grid_spec=pltpu.PrefetchScalarGridSpec(
            num_scalar_prefetch=1,
            grid=(count, f),
            in_specs=[whole(p, D), fixed(tok.shape[0] * f, D), fixed(D, 3 * D), fixed(3 * D, D), fixed(D, D)],
            out_specs=[part(3 * D, p), part(D, p), part(p, D), part(HEADS // 2, 2 * p), part(3, D)]
            + [part(p // n, D)] * n,
            scratch_shapes=[pltpu.VMEM((p, D), BF16), pltpu.VMEM((tok.shape[0] * f, 3 * D), F32)],
        ),
        out_shape=[sd((3 * D, p), BF16), sd((D, p), BF16), sd((p, D), BF16)]
        + [sd((HEADS // 2, 2 * p), F32), sd((3, D), F32)]
        + [sd((p // n, D), BF16)] * n,
        compiler_params=pltpu.CompilerParams(vmem_limit_bytes=VMEM),
        cost_estimate=cost(6 * count),
        name="spatial_fwd",
    )(idx, tok, cond.reshape(-1, D), ada, w_t, wo)


def gather_tile(refs, groups):
    f = refs[0].shape[1]
    return jnp.concatenate(
        [
            r[0, j, g * GROUP : (g + 1) * GROUP, :]
            for g in range(groups)
            for r in refs
            for j in range(f)
        ],
        axis=0,
    )


def scatter_tile(refs, value, groups, f):
    at = 0
    for g in range(groups):
        for r in refs:
            for j in range(f):
                r[0, j, g * GROUP : (g + 1) * GROUP, :] = value[at : at + GROUP]
                at += GROUP


def middle(n, start, first_chunk, last_chunk, idx, seg, *refs):
    refs = list(refs)
    a1, refs = refs[:n], refs[n:]
    ct, refs = refs[:n], refs[n:]
    cond, ada_a, ada_b, tq_t, tq, to, up, down = refs[:8]
    refs = refs[8:]
    if not first_chunk:
        init, refs = refs[0], refs[3:]
    dl, refs = refs[:n], refs[n:]
    ou = [refs[k // (n // 2)].at[k % (n // 2)] for k in range(n)]
    refs = refs[2:]
    gsum = refs[0]
    if last_chunk:
        sent, kept = refs[1:3]
        refs = refs[3:]
        acc = refs.pop()
    else:
        acc = refs[1]
        refs = refs[2:]
    mod_s, qkv_s, p_s, mix_s, dg_s, hid_s, dqkv_s = refs
    groups = a1[0].shape[2] // GROUP
    frames = n * a1[0].shape[1]
    span = frames * GROUP
    tokens = span * groups

    @pl.when(pl.program_id(0) == 0)
    def _():
        acc[...] = jnp.zeros_like(acc) if first_chunk else init[...]

    act = silu_low(cond[0])
    mod_s[:, : 3 * D] = nn(act, ada_a[...])
    mod_s[:, 3 * D :] = nn(act, ada_b[...])

    def per_frame(piece, plus=0.0):
        rows = [mod_s[t : t + 1, piece * D : (piece + 1) * D] + plus for t in range(frames)]
        one = jnp.concatenate([jnp.broadcast_to(r, (GROUP, D)) for r in rows], axis=0)
        return jnp.concatenate([one] * groups, axis=0)

    def frame_sum(v):
        return jnp.sum(jnp.sum(v.reshape(groups, frames, GROUP, D), axis=0), axis=1)

    def add(base, col, value):
        for j in range(value.shape[1] // D):
            acc[base + col // D + j] += value[:, j * D : (j + 1) * D]

    x1 = gather_tile(a1, groups).astype(F32)
    n2, r2 = norm_stats(x1)
    second = (n2 * per_frame(1, 1.0) + per_frame(0)).astype(BF16)
    qkv_s[...] = nt(tq_t[...], second).astype(BF16)
    lane = lax.broadcasted_iota(jnp.int32, (span, span), 0) % GROUP
    other = lax.broadcasted_iota(jnp.int32, (span, span), 1) % GROUP
    segs = [seg[pl.program_id(0) + start, t] for t in range(frames)]

    def segment_of(axis):
        at = lax.broadcasted_iota(jnp.int32, (span, span), axis) // GROUP
        value = jnp.zeros((span, span), jnp.int32)
        for t in range(frames):
            value = jnp.where(at == t, segs[t], value)
        return value

    allowed = (segment_of(0) == segment_of(1)) & (lane == other)
    bias = jnp.where(allowed, 0.0, -1e30)
    bias2 = jnp.concatenate([bias, bias], axis=1)
    for g in range(groups):
        cols = slice(g * span, (g + 1) * span)
        for j in range(HEADS // 2):
            a = j * 2 * HD
            q = on_diagonal(qkv_s[a : a + 2 * HD, cols] * BF16(0.125))
            k = qkv_s[D + a : D + a + 2 * HD, cols]
            v = qkv_s[2 * D + a : 2 * D + a + 2 * HD, cols]
            s = tn(k, q) + bias2
            p = jnp.exp(s - jnp.max(s, axis=0, keepdims=True))
            p = p * (1.0 / jnp.sum(p, axis=0, keepdims=True))
            p_s[g * (HEADS // 2) + j] = p
            o = nn(v, p.astype(BF16)).astype(BF16)
            mix_s[a : a + HD, cols] = o[:HD, :span]
            mix_s[a + HD : a + 2 * HD, cols] = o[HD:, span:]
    br2 = tn(mix_s[...], to[...])
    x2 = x1 + per_frame(2) * br2
    n3, r3 = norm_stats(x2)
    third = (n3 * per_frame(4, 1.0) + per_frame(3)).astype(BF16)
    step = 2 * D
    br3 = jnp.zeros((tokens, D), F32)
    for c in range(0, MLP, step):
        pre = nn(third, up[:, c : c + step])
        sq = pre * pre
        t = jnp.tanh(pre * (0.7978845608028654 + (0.7978845608028654 * 0.044715) * sq))
        half = 0.5 + 0.5 * t
        hid = (pre * half).astype(BF16)
        hid_s[:, c : c + step] = hid
        inner = 0.7978845608028654 + (3 * 0.7978845608028654 * 0.044715) * sq
        dg_s[:, c : c + step] = half + 0.5 * pre * (1.0 - t * t) * inner
        br3 += nn(hid, down[c : c + step, :])
    gate3 = per_frame(5)
    scatter_tile(ou, (x2 + gate3 * br3).astype(BF16), groups, a1[0].shape[1])
    cot = gather_tile(ct, groups).astype(F32)
    gsum[0, :, 5] = frame_sum(cot * br3)
    gb3 = (gate3 * cot).astype(BF16)
    gb3_t = gb3.T
    third_t = third.T
    g3 = jnp.zeros((tokens, D), F32)
    for c in range(0, MLP, step):
        add(4, c, nn(gb3_t, hid_s[:, c : c + step]))
        gp = (nt(gb3, down[c : c + step, :]) * dg_s[:, c : c + step]).astype(BF16)
        add(0, c, nn(third_t, gp))
        g3 += nt(gp, up[:, c : c + step])
    gsum[0, :, 3] = frame_sum(g3)
    gsum[0, :, 4] = frame_sum(g3 * n3)
    dx3 = norm_back(g3 * per_frame(4, 1.0), n3, r3)
    ga2 = cot + dx3
    gsum[0, :, 2] = frame_sum(ga2 * br2)
    gb2 = (per_frame(2) * ga2).astype(BF16)
    add(11, 0, nn(mix_s[...], gb2))
    gm_t = nt(to[...], gb2).astype(BF16)
    for g in range(groups):
        cols = slice(g * span, (g + 1) * span)
        for j in range(HEADS // 2):
            a = j * 2 * HD
            q = on_diagonal(qkv_s[a : a + 2 * HD, cols] * BF16(0.125))
            k = qkv_s[D + a : D + a + 2 * HD, cols]
            v = qkv_s[2 * D + a : 2 * D + a + 2 * HD, cols]
            go = on_diagonal(gm_t[a : a + 2 * HD, cols])
            p = p_s[g * (HEADS // 2) + j]
            dp = tn(v, go)
            ds = (p * (dp - jnp.sum(p * dp, axis=0, keepdims=True))).astype(BF16)
            dqkv_s[2 * D + a : 2 * D + a + 2 * HD, cols] = nt(go, p.astype(BF16)).astype(BF16)
            dqkv_s[D + a : D + a + 2 * HD, cols] = nt(q, ds).astype(BF16)
            dq = (nn(k, ds) * 0.125).astype(BF16)
            dqkv_s[a : a + HD, cols] = dq[:HD, :span]
            dqkv_s[a + HD : a + 2 * HD, cols] = dq[HD:, span:]
    dqkv = dqkv_s[...]
    add(8, 0, nt(second.T, dqkv))
    g2 = nn(tq[...], dqkv).T
    gsum[0, :, 0] = frame_sum(g2)
    gsum[0, :, 1] = frame_sum(g2 * n2)
    dx2 = norm_back(g2 * per_frame(1, 1.0), n2, r2)
    scatter_tile(dl, (dx3 + dx2).astype(BF16), groups, a1[0].shape[1])
    if last_chunk:

        @pl.when(pl.program_id(0) == pl.num_programs(0) - 1)
        def _():
            divide(idx[0] & 1, acc, sent, kept)


def sum_specs(last_chunk, blocks):
    const = lambda *s: pl.BlockSpec(s, lambda *g: (0,) * len(s))
    sd = jax.ShapeDtypeStruct
    if not last_chunk:
        return [const(blocks, D, D)], [sd((blocks, D, D), F32)], []
    half = (blocks // 2, D, D)
    return [const(*half)] * 2, [sd(half, BF16), sd(half, BF16)], [pltpu.VMEM((blocks, D, D), F32)]


def call_middle(idx, seg, a1, ct, cond, ada, tq_t, tq, to, up, down, init, start, last_chunk):
    n = len(a1)
    count, f, rows = a1[0].shape[:3]
    packs = cond.shape[0]
    frames = n * f
    span = frames * GROUP
    tokens = frames * rows
    groups = rows // GROUP
    part = lambda *s: pl.BlockSpec((1,) + s, lambda b, i, s_: (b,) + (0,) * len(s))
    whole = lambda *s: pl.BlockSpec((1,) + s, lambda b, i, s_: (b + start,) + (0,) * len(s))
    fixed = lambda *s: pl.BlockSpec(s, lambda b, i, s_: (0,) * len(s), pipeline_mode=pl.Buffered(1))
    column = lambda j: pl.BlockSpec((D, 3 * D), lambda b, i, s_: (0, j), pipeline_mode=pl.Buffered(1))
    sd = jax.ShapeDtypeStruct
    sum_out, sum_shape, sum_scratch = sum_specs(last_chunk, 12)
    stack = (n // 2, packs, f, rows, D)
    stacked = pl.BlockSpec((n // 2, 1, f, rows, D), lambda b, i, s_: (0, b + start, 0, 0, 0))
    return pl.pallas_call(
        functools.partial(middle, n, start, not init, last_chunk),
        grid_spec=pltpu.PrefetchScalarGridSpec(
            num_scalar_prefetch=2,
            grid=(count,),
            in_specs=[part(f, rows, D)] * n
            + [whole(f, rows, D)] * n
            + [whole(frames, D)]
            + [column(1), column(2), fixed(3 * D, D), fixed(D, 3 * D)]
            + [fixed(D, D), fixed(D, MLP), fixed(MLP, D)]
            + ([fixed(12, D, D)] + [pl.BlockSpec(memory_space=pl.ANY)] * 2 if init else []),
            out_specs=[part(f, rows, D)] * n + [stacked] * 2 + [part(frames, 6, D)] + sum_out,
            scratch_shapes=[
                pltpu.VMEM((frames, 6 * D), F32),
                pltpu.VMEM((3 * D, tokens), BF16),
                pltpu.VMEM((groups * HEADS // 2, span, 2 * span), F32),
                pltpu.VMEM((D, tokens), BF16),
                pltpu.VMEM((tokens, MLP), F32),
                pltpu.VMEM((tokens, MLP), BF16),
                pltpu.VMEM((3 * D, tokens), BF16),
            ]
            + sum_scratch,
        ),
        out_shape=[sd((count, f, rows, D), BF16)] * n
        + [sd(stack, BF16)] * 2
        + [sd((count, frames, 6, D), F32)]
        + sum_shape,
        input_output_aliases={2 + 2 * n + 9 + j: n + j for j in range(2)} if init else {},
        compiler_params=pltpu.CompilerParams(vmem_limit_bytes=VMEM),
        cost_estimate=cost(16 * count),
        name="middle",
    )(idx, seg, *a1, *ct, cond, ada, ada, tq_t, tq, to, up, down, *init)


def spatial_bwd(n, first_chunk, last_chunk, idx, tok, cot, mod, qkv, mix, br, tot, wo, *rest):
    rest = list(rest)
    if not first_chunk:
        init, rest = rest[0], rest[1:]
    dl, rest = rest[:n], rest[n:]
    dqkv_o, ga_o, gg_o = rest[:3]
    if last_chunk:
        sent, kept, scr, acc = rest[3:]
    else:
        acc, scr = rest[3:]

    @pl.when((pl.program_id(0) == 0) & (pl.program_id(1) == 0))
    def _():
        acc[...] = jnp.zeros_like(acc) if first_chunk else init[...]

    rows = dl[0].shape[2]
    i = idx[0]
    for k in range(n):
        scr[pl.ds(pl.multiple_of((i ^ k) * rows, GROUP), rows), :] = dl[k][0, 0]
    ga = cot[0, 0].astype(F32) + scr[...].astype(F32)
    ga_o[0, 0] = ga
    md = mod[0, 0]
    gg_o[0, 0] = jnp.sum(ga * br[0, 0].astype(F32), axis=0, keepdims=True)
    gb = (md[2:3] * ga).astype(BF16)
    acc[3] += nn(mix[0, 0], gb)
    gm = nt(wo[...], gb).astype(BF16)
    for j in range(HEADS // 2):
        a = j * 2 * HD
        q = qkv[0, 0, a : a + 2 * HD] * BF16(0.125)
        k = qkv[0, 0, D + a : D + a + 2 * HD]
        v = qkv[0, 0, 2 * D + a : 2 * D + a + 2 * HD]
        go = gm[a : a + 2 * HD]
        p = jnp.exp(tn(k, on_diagonal(q)) - tot[0, 0, j : j + 1])
        dp = tn(v, on_diagonal(go))
        ds = (p * (dp - jnp.sum(p * dp, axis=0, keepdims=True))).astype(BF16)
        p = p.astype(BF16)
        cut = q.shape[1]
        for e in range(2):
            cols = slice(e * cut, (e + 1) * cut)
            r = slice(e * HD, (e + 1) * HD)
            at = a + e * HD
            dqkv_o[0, 0, 2 * D + at : 2 * D + at + HD] = nt(go[r], p[:, cols]).astype(BF16)
            dqkv_o[0, 0, D + at : D + at + HD] = nt(q[r], ds[:, cols]).astype(BF16)
            dqkv_o[0, 0, at : at + HD] = (nn(k[r], ds[:, cols]) * 0.125).astype(BF16)
    nrm, _ = norm_stats(tok[0, 0].astype(F32))
    first = (nrm * (1.0 + md[1:2]) + md[0:1]).astype(BF16)
    value = nt(first.T, dqkv_o[0, 0])
    for j in range(3):
        acc[j] += value[:, j * D : (j + 1) * D]
    if last_chunk:
        end = (pl.program_id(0) == pl.num_programs(0) - 1) & (pl.program_id(1) == pl.num_programs(1) - 1)

        @pl.when(end)
        def _():
            divide(i & 1, acc, sent, kept)


def call_spatial_bwd(idx, tok, cot, mod, qkv, mix, br, tot, wo, init, dl, start, last_chunk):
    n = len(dl)
    count, f, rows = dl[0].shape[:3]
    p = tok.shape[2]
    whole = lambda *s: pl.BlockSpec((1, 1) + s, lambda b, f, i: (b + start, f) + (0,) * len(s))
    part = lambda *s: pl.BlockSpec((1, 1) + s, lambda b, f, i: (b, f) + (0,) * len(s))
    fixed = lambda *s: pl.BlockSpec(s, lambda b, f, i: (0,) * len(s), pipeline_mode=pl.Buffered(1))
    sd = lambda s, d: jax.ShapeDtypeStruct((count, f) + s, d)
    sum_out, sum_shape, sum_scratch = sum_specs(last_chunk, 4)
    return pl.pallas_call(
        functools.partial(spatial_bwd, n, not init, last_chunk),
        grid_spec=pltpu.PrefetchScalarGridSpec(
            num_scalar_prefetch=1,
            grid=(count, f),
            in_specs=[whole(p, D), whole(p, D), part(3, D), part(3 * D, p), part(D, p)]
            + [part(p, D), part(HEADS // 2, 2 * p), fixed(D, D)]
            + [fixed(4, D, D)] * len(init)
            + [part(rows, D)] * n,
            out_specs=[part(3 * D, p), part(p, D), part(1, D)]
            + sum_out,
            scratch_shapes=[pltpu.VMEM((p, D), BF16)] + sum_scratch,
        ),
        out_shape=[sd((3 * D, p), BF16), sd((p, D), F32), sd((1, D), F32)]
        + sum_shape,
        compiler_params=pltpu.CompilerParams(vmem_limit_bytes=VMEM),
        cost_estimate=cost(6 * count),
        name="spatial_bwd",
    )(idx, tok, cot, mod, qkv, mix, br, tot, wo, *init, *dl)


def last_step(masks, idx, tok, mod, w_t, dqkv, ga, *rest):
    grad_o, out_o, gs_o = rest[-3:]
    rows = rest[0].shape[3]
    i = idx[0]
    for k, piece in zip(masks, rest):
        out_o[0, 0, pl.ds(pl.multiple_of((i ^ k) * rows, GROUP), rows), :] = piece[0, 0, 0]
    g = tn(dqkv[0, 0], w_t[...])
    nrm, r = norm_stats(tok[0, 0].astype(F32))
    md = mod[0, 0]
    gs_o[0, 0, 0:1] = jnp.sum(g, axis=0, keepdims=True)
    gs_o[0, 0, 1:2] = jnp.sum(g * nrm, axis=0, keepdims=True)
    grad_o[0, 0] = ga[0, 0] + norm_back(g * (1.0 + md[1:2]), nrm, r)


def call_last(idx, tok, mod, w_t, dqkv, ga, ou, start, held):
    n = len(ou)
    arrays, offsets, masks = zip(*ou)
    count, f = dqkv.shape[:2]
    rows = arrays[0].shape[3]
    p = tok.shape[2]
    whole = lambda *s: pl.BlockSpec((1, 1) + s, lambda b, f, i: (b + start, f) + (0,) * len(s))
    part = lambda *s: pl.BlockSpec((1, 1) + s, lambda b, f, i: (b, f) + (0,) * len(s))
    fixed = lambda *s: pl.BlockSpec(s, lambda b, f, i: (0,) * len(s), pipeline_mode=pl.Buffered(1))
    piece = lambda j: pl.BlockSpec((1, 1, 1, rows, D), lambda b, f, i: (j, b + start, f, 0, 0))
    sd = lambda s, d: jax.ShapeDtypeStruct((count, f) + s, d)
    return pl.pallas_call(
        functools.partial(last_step, masks),
        grid_spec=pltpu.PrefetchScalarGridSpec(
            num_scalar_prefetch=1,
            grid=(count, f),
            in_specs=[whole(p, D), part(3, D), fixed(3 * D, D), part(3 * D, p), part(p, D)]
            + [piece(j) for j in offsets]
            + [pl.BlockSpec(memory_space=pl.ANY)] * len(held),
            out_specs=[whole(p, D), whole(p, D), part(2, D)],
        ),
        out_shape=[
            jax.ShapeDtypeStruct(tok.shape, F32),
            jax.ShapeDtypeStruct(tok.shape, BF16),
            sd((2, D), F32),
        ],
        input_output_aliases={6 + n + j: j for j in range(len(held))},
        compiler_params=pltpu.CompilerParams(vmem_limit_bytes=VMEM),
        cost_estimate=cost(3 * count),
        name="last_step",
    )(idx, tok, mod, w_t, dqkv, ga, *arrays, *held)


def pick(idx, own, other):
    mine = idx[0] & 1
    half = own.shape[0]
    return lambda k: jnp.where(k // half == mine, own[k % half], other[k % half]).astype(F32)


def finish_early(idx, own, other, up_o, down_o, qkv_o, out_o):
    block = pick(idx, own, other)
    for j in range(4):
        up_o[:, j * D : (j + 1) * D] = block(j)
        down_o[j * D : (j + 1) * D, :] = block(4 + j).T
    for j in range(3):
        qkv_o[:, j * D : (j + 1) * D] = block(8 + j)
    out_o[...] = block(11)


def call_finish_early(idx, own, other):
    sd = lambda *s: jax.ShapeDtypeStruct(s, F32)
    return pl.pallas_call(
        finish_early,
        in_specs=[pl.BlockSpec(memory_space=pltpu.SMEM)] + [pl.BlockSpec(memory_space=pltpu.VMEM)] * 2,
        out_specs=[pl.BlockSpec(memory_space=pltpu.VMEM)] * 4,
        out_shape=[sd(D, MLP), sd(MLP, D), sd(D, 3 * D), sd(D, D)],
        compiler_params=pltpu.CompilerParams(vmem_limit_bytes=VMEM),
        cost_estimate=cost(3),
        name="finish_early",
    )(idx, own, other)


def finish_late(idx, own, other, rest, mod, ada_o, qkv_o, out_o):
    block = pick(idx, own, other)
    act = silu_low(rest[:, 6 * D :]).T
    ada_o[:, : 3 * D] = nn(act, mod[...])
    ada_o[:, 3 * D :] = nn(act, rest[:, : 6 * D])
    for j in range(3):
        qkv_o[:, j * D : (j + 1) * D] = block(j)
    out_o[...] = block(3)


def call_finish_late(idx, own, other, rest, mod):
    sd = lambda *s: jax.ShapeDtypeStruct(s, F32)
    return pl.pallas_call(
        finish_late,
        in_specs=[pl.BlockSpec(memory_space=pltpu.SMEM)] + [pl.BlockSpec(memory_space=pltpu.VMEM)] * 4,
        out_specs=[pl.BlockSpec(memory_space=pltpu.VMEM)] * 3,
        out_shape=[sd(D, 9 * D), sd(D, 3 * D), sd(D, D)],
        compiler_params=pltpu.CompilerParams(vmem_limit_bytes=VMEM),
        cost_estimate=cost(4),
        name="finish_late",
    )(idx, own, other, rest, mod)


def swap(x, axis, mask):
    size = lax.axis_size(axis)
    return lax.ppermute(x, axis, [(s, s ^ mask) for s in range(size)])


def bits_of(axis):
    return [(axis, b) for b in range(lax.axis_size(axis).bit_length() - 1)]


def bit_of(axis, b):
    return (lax.axis_index(axis) >> b) & 1


def orders():
    path = bits_of("pack") + bits_of("frame")[1:]
    path = path[:1] + path[-1:] + path[1:-1]
    half = len(path) // 2
    return path, path[half:] + path[:half]


def swap_by_core(x, step):
    nf, npk = lax.axis_size("frame"), lax.axis_size("pack")
    perm = []
    for pack in range(npk):
        for frame in range(nf):
            axis, b = step[frame & 1]
            to = (pack ^ (1 << b), frame) if axis == "pack" else (pack, frame ^ (1 << b))
            perm.append((frame * npk + pack, to[1] * npk + to[0]))
    return lax.ppermute(x, ("frame", "pack"), perm)


def ar_steps():
    core = ("frame", 0)
    return [(core, core)] + list(zip(*orders()))


def bit_by_core(step):
    core = bit_of("frame", 0)
    return jnp.where(core == 0, bit_of(*step[0]), bit_of(*step[1]))


def split(g, step):
    mine = bit_by_core(step)
    half = g.shape[0] // 2
    send = lax.dynamic_slice_in_dim(g, (1 - mine) * half, half, 0)
    return send, lax.dynamic_slice_in_dim(g, mine * half, half, 0)


def double(g, step):
    other = swap_by_core(g, step)
    mine = bit_by_core(step) == 1
    return jnp.concatenate([jnp.where(mine, other, g), jnp.where(mine, g, other)], axis=0)


class Regroup:
    def __init__(self, lo, hi):
        self.count = lo.shape[0]
        self.pieces = [(lo, 0, 0)]
        self.start(hi)

    def start(self, send):
        self.moving = swap(send, "frame", self.count)

    def arrive(self, after=None):
        got = self.moving if after is None else tie(self.moving, after)
        k = self.count
        self.pieces += [(got, j * k, m ^ k) for j, (_, _, m) in enumerate(self.pieces)]
        if k > 1:
            half = k // 2
            send = jnp.concatenate([a[o + half : o + k] for a, o, _ in self.pieces], axis=0)
            self.count = half
            self.start(send)
            return False
        return True


def reduce_slots(v):
    while v.shape[1] > 1:
        half = v.shape[1] // 2
        v = v[:, :half] + swap(v[:, half:], "frame", half)
    return v[:, 0]


class Summing:
    def __init__(self, send, keep):
        self.todo = ar_steps()
        self.done = []
        self.send, self.keep = send, keep
        self.moving = None
        self.value = None

    def start(self):
        step = self.todo[0]
        if self.value is not None:
            self.send, self.keep = split(self.value, step)
        self.moving = swap_by_core(self.send, step)
        return self

    def add(self, after=None):
        moving = self.moving if after is None else tie(self.moving, after)
        self.value = (self.keep.astype(F32) + moving.astype(F32)).astype(BF16)
        self.done.append(self.todo.pop(0))
        return self.value

    def finish_halving(self):
        while self.todo:
            self.start()
            self.add()

    def finish_doubling(self):
        g = self.value
        for step in self.done[:0:-1]:
            g = double(g, step)
        return g, swap_by_core(g, self.done[0])


def spread(g, steps, after=None):
    for axis, b in steps:
        other = swap(g, axis, 1 << b)
        if after is not None:
            other = tie(other, after)
        mine = bit_of(axis, b) == 1
        g = jnp.concatenate([jnp.where(mine, other, g), jnp.where(mine, g, other)], axis=0)
    return g


def tie_all(values, *deps):
    return list(lax.optimization_barrier((*values, *deps))[: len(values)])


def tie(value, *deps):
    return lax.optimization_barrier((value, *deps))[0]


def local(
    tokens,
    condition,
    clip_lengths,
    ada_weight,
    spatial_qkv,
    spatial_out,
    temporal_qkv,
    temporal_out,
    mlp_up,
    mlp_down,
    cotangent,
):
    n = lax.axis_size("frame")
    i = lax.axis_index("frame")
    idx = i.reshape(1).astype(jnp.int32)
    packs, f, patches = tokens.shape[:3]
    rows = patches // n
    count = packs // CHUNKS
    every = bits_of("frame") + bits_of("pack")

    cut = lambda v, k: lax.dynamic_slice_in_dim(v, (i ^ k) * rows, rows, 2)
    send = lambda parts: [parts[0]] + [swap(parts[k], "frame", k) for k in range(1, n)]
    steps = ar_steps()

    sq_t = spatial_qkv.T
    tq_t = temporal_qkv.T
    ct = send([cut(cotangent, k) for k in range(n)])
    top = n // 2
    cond_slots, masks = condition[None], [0]
    cond_slots = jnp.concatenate([cond_slots, swap(cond_slots, "frame", top)], axis=0)
    masks = masks + [m ^ top for m in masks]
    frame_ids = jnp.concatenate([(i ^ k) * f + jnp.arange(f, dtype=jnp.int32) for k in range(n)])
    width = clip_lengths.shape[1]
    ends = [jnp.sum(clip_lengths[:, : j + 1], axis=1) for j in range(width)]
    segment = sum((e[:, None] <= frame_ids[None, :]).astype(jnp.int32) for e in ends)

    fwd = []
    source = tokens
    for c in range(CHUNKS):
        res = call_spatial_fwd(idx, source, condition, ada_weight, sq_t, spatial_out, c * count, count, n)
        slots = list(res[5:])
        if c:
            cond_slots = tie(cond_slots, res[4], fwd[-1][1][1])
            while top > 1:
                top //= 2
                cond_slots = jnp.concatenate([cond_slots, swap(cond_slots, "frame", top)], axis=0)
                masks = masks + [m ^ top for m in masks]
            cond_slots = jnp.stack([cond_slots[masks.index(k)] for k in range(n)], axis=1)
            cond_slots = cond_slots.reshape(packs, n * f, D)
            slots = tie_all(slots, *fwd[-1][1][1:], *ct[1:], cond_slots)
        fwd.append((res[:5], send(slots)))
        if c == 0:
            source = tie(tokens, cond_slots, segment, tq_t, ct[1])

    init, mids = [], []
    for c in range(CHUNKS):
        last = c == CHUNKS - 1
        res = call_middle(
            idx, segment, fwd[c][1], ct, cond_slots, ada_weight, tq_t, temporal_qkv, temporal_out,
            mlp_up, mlp_down, init, c * count, last,
        )
        init = [res[n + 3], res[n], res[n + 1]]
        res = list(res)
        if c:
            res = tie_all(res, *mids[-1][0][1:])
        mids.append((send(res[:n]), res[n + 2]))
    flat = lambda v: v.reshape(-1, D)
    early = Summing(flat(res[n + 3]), flat(res[n + 4])).start()
    outs = Regroup(res[n], res[n + 1])

    acc, backs = [], []
    for c in range(CHUNKS):
        last = c == CHUNKS - 1
        qkv, mix, br, tot, mod = fwd[c][0]
        dl = mids[c][0]
        if c:
            early.add(after=backs[-1][2])
            early.start()
            dl = [tie(v, early.send) for v in dl]
        res = call_spatial_bwd(
            idx, tokens, cotangent, mod, qkv, mix, br, tot, spatial_out, acc, dl, c * count, last
        )
        acc = list(res[3:])
        backs.append(res)
    sums = jnp.concatenate([m[1] for m in mids], 0).reshape(packs, n, f, 6, D)
    sums = reduce_slots(tie(sums, backs[0][2]))
    late = Summing(flat(acc[0]), flat(acc[1])).start()
    early.add(after=backs[-1][2])
    early.start()
    every = bits_of("pack") + bits_of("frame")[::-1]
    low = tie(sums, backs[-1][2]).astype(BF16).reshape(packs * f, 6 * D)
    while not outs.arrive(after=backs[-1][2]):
        pass
    rest_all = jnp.concatenate([low, condition.reshape(packs * f, D)], axis=1)
    lasts, held = [], []
    for c in range(CHUNKS):
        dqkv, ga, gate_sum = backs[c][:3]
        ga = tie(ga, early.send) if c == 0 else tie(ga, early.send, late.send)
        res = call_last(idx, tokens, fwd[c][0][4], sq_t, dqkv, ga, outs.pieces, c * count, held)
        held = list(res[:2])
        lasts.append(res)
        rest_all = spread(rest_all, every[c : c + 1], after=res[2])
        late.add(after=res[2])
        late.start()
        early.add(after=res[2])
        if early.todo:
            early.start()
    if early.todo and early.moving is not None:
        early.add()
    late.add()
    early.finish_halving()
    late.finish_halving()
    grad_tokens, output = held

    rest_all = spread(rest_all, every[CHUNKS:])
    own = jnp.concatenate(
        [jnp.concatenate([lasts[c][2], backs[c][2]], axis=2) for c in range(CHUNKS)], axis=0
    ).astype(BF16)
    own = own.reshape(packs * f, 3 * D)
    mod_all = spread(own, every)
    dot = functools.partial(jnp.einsum, preferred_element_type=F32)
    grad_mod = jnp.concatenate([own, low], axis=1)
    back = dot("tj,ij->ti", grad_mod, ada_weight).reshape(packs, f, D)
    cf = condition.astype(F32)
    sig = 1.0 / (1.0 + jnp.exp(-cf))
    grad_condition = back * (sig * (1.0 + cf * (1.0 - sig)))

    blocks = lambda v: v.reshape(-1, D, D)
    e_own, e_other = early.finish_doubling()
    l_own, l_other = late.finish_doubling()
    up, down, t_qkv, t_out = call_finish_early(idx, blocks(e_own), blocks(e_other))
    ada, s_qkv, s_out = call_finish_late(idx, blocks(l_own), blocks(l_other), rest_all, mod_all)
    return (output, grad_tokens, grad_condition, ada, s_qkv, s_out, t_qkv, t_out, up, down)


def solution(mesh):
    tok = P("pack", "frame", None, None)
    cond = P("pack", "frame", None)
    return jax.shard_map(
        local,
        mesh=mesh,
        in_specs=(tok, cond, P("pack", None), P(), P(), P(), P(), P(), P(), P(), tok),
        out_specs=(tok, tok, cond, P(), P(), P(), P(), P(), P(), P()),
        check_vma=False,
    )
```

```python
import functools

import jax
import jax.numpy as jnp
from jax import lax
from jax.experimental import pallas as pl
from jax.experimental.pallas import tpu as pltpu
from jax.sharding import PartitionSpec as P

D = 384
HEADS = 6
HD = 64
MLP = 1536
F32 = jnp.float32
BF16 = jnp.bfloat16
CHUNKS = 2
GROUP = 16
VMEM = 58 * 2**20


def nn(a, b):
    return lax.dot_general(a, b, (((1,), (0,)), ((), ())), preferred_element_type=F32)


def nt(a, b):
    return lax.dot_general(a, b, (((1,), (1,)), ((), ())), preferred_element_type=F32)


def tn(a, b):
    return lax.dot_general(a, b, (((0,), (0,)), ((), ())), preferred_element_type=F32)


def cost(us):
    return pl.CostEstimate(flops=int(us * 1.0e9), bytes_accessed=1000, transcendentals=0)


def silu_low(v):
    v = v.astype(F32)
    return (v / (1.0 + jnp.exp(-v))).astype(BF16)


def on_diagonal(pair):
    none = jnp.zeros_like(pair[:HD])
    return jnp.concatenate(
        [
            jnp.concatenate([pair[:HD], none], axis=1),
            jnp.concatenate([none, pair[HD:]], axis=1),
        ],
        axis=0,
    )


def norm_stats(x):
    c = x - jnp.mean(x, -1, keepdims=True)
    r = lax.rsqrt(jnp.mean(c * c, -1, keepdims=True) + 1e-6)
    return c * r, r


def norm_back(h, n, r):
    return r * (h - jnp.mean(h, -1, keepdims=True) - n * jnp.mean(h * n, -1, keepdims=True))


def pipelined(items, stages, ahead=1):
    held = [[] for _ in stages]
    last = len(stages) - 1
    for t in range(len(items) + ahead * last):
        for s, stage in enumerate(stages):
            at = t - s * ahead
            if 0 <= at < len(items):
                value = stage(*items[at], *(held[s - 1].pop(0) if s else ()))
                if s < last:
                    held[s].append(value)


def spatial_fwd(start, idx, tok, cond, ada, w_t, wo, qkv_o, mix_o, br_o, tot_o, mod_o, *rest):
    slots, (scr, mod_s) = rest[:-2], rest[-2:]
    rows = slots[0].shape[2]
    frames = tok.shape[1]
    b = pl.program_id(0)

    @pl.when(b == 0)
    def _():
        mod_s[...] = nn(silu_low(cond[...]), ada[...])

    i = idx[0]
    mds = []
    for f in range(frames):
        at = (b + start) * frames + f
        md = [mod_s[pl.ds(at, 1), j * D : (j + 1) * D] for j in range(3)]
        for j in range(3):
            mod_o[0, f, j : j + 1] = md[j]
        n, _ = norm_stats(tok[0, f].astype(F32))
        first = (n * (1.0 + md[1]) + md[0]).astype(BF16)
        qkv_o[0, f] = nt(w_t[...], first).astype(BF16)
        mds.append(md)

    def scores(j, f):
        a = j * 2 * HD
        q = on_diagonal(qkv_o[0, f, a : a + 2 * HD] * BF16(0.125))
        k = qkv_o[0, f, D + a : D + a + 2 * HD]
        return (nn(k.T, q),)

    def mix(j, f, s):
        a = j * 2 * HD
        mx = jnp.max(s, axis=0, keepdims=True)
        p = jnp.exp(s - mx)
        total = jnp.sum(p, axis=0, keepdims=True)
        tot_o[0, f, j : j + 1] = mx + jnp.log(total)
        p = p.astype(BF16)
        scale = 1.0 / total
        cut = p.shape[1] // 2
        for e in range(2):
            v = qkv_o[0, f, 2 * D + a + e * HD : 2 * D + a + (e + 1) * HD]
            cols = slice(e * cut, (e + 1) * cut)
            mix_o[0, f, a + e * HD : a + (e + 1) * HD] = (nn(v, p[:, cols]) * scale[:, cols]).astype(BF16)

    pipelined([(j, f) for j in range(HEADS // 2) for f in range(frames)], [scores, mix], 2)
    for f in range(frames):
        br = tn(mix_o[0, f], wo[...])
        br_o[0, f] = br.astype(BF16)
        scr[f] = (tok[0, f].astype(F32) + mds[f][2] * br).astype(BF16)
        for k, slot in enumerate(slots):
            slot[0, f] = scr[f, pl.ds(pl.multiple_of((i ^ k) * rows, GROUP), rows), :]


def call_spatial_fwd(idx, tok, cond, ada, w_t, wo, start, count, n):
    f = tok.shape[1]
    p = tok.shape[2]
    whole = lambda *s: pl.BlockSpec((1, f) + s, lambda b, i: (b + start, 0) + (0,) * len(s))
    part = lambda *s: pl.BlockSpec((1, f) + s, lambda b, i: (b, 0) + (0,) * len(s))
    fixed = lambda *s: pl.BlockSpec(s, lambda b, i: (0,) * len(s), pipeline_mode=pl.Buffered(1))
    sd = lambda s, d: jax.ShapeDtypeStruct((count, f) + s, d)
    own = tok.shape[0] * f
    return pl.pallas_call(
        functools.partial(spatial_fwd, start),
        grid_spec=pltpu.PrefetchScalarGridSpec(
            num_scalar_prefetch=1,
            grid=(count,),
            in_specs=[whole(p, D), fixed(own, D), fixed(D, 3 * D), fixed(3 * D, D), fixed(D, D)],
            out_specs=[part(3 * D, p), part(D, p), part(p, D), part(HEADS // 2, 2 * p), part(3, D)]
            + [part(p // n, D)] * n,
            scratch_shapes=[pltpu.VMEM((f, p, D), BF16), pltpu.VMEM((own, 3 * D), F32)],
        ),
        out_shape=[sd((3 * D, p), BF16), sd((D, p), BF16), sd((p, D), BF16)]
        + [sd((HEADS // 2, 2 * p), F32), sd((3, D), F32)]
        + [sd((p // n, D), BF16)] * n,
        compiler_params=pltpu.CompilerParams(vmem_limit_bytes=VMEM),
        cost_estimate=cost(4 * count),
        name="spatial_fwd",
    )(idx, tok, cond.reshape(-1, D), ada, w_t, wo)


def tile_places(n, f, rows):
    return [
        (k, j * rows + g * GROUP)
        for g in range(rows // GROUP)
        for k in range(n)
        for j in range(f)
    ]


def divide(mine, acc, sent, kept, kinds):
    at = 0
    base = 0
    for kind, blocks in kinds:
        for out, who in ((sent, 1 - mine), (kept, mine)):
            row = at
            if kind == "rows":
                half = D // 2
                for j in range(blocks):
                    part = acc[base + j, pl.ds(pl.multiple_of(who * half, GROUP), half), :]
                    out[row : row + half] = part.astype(BF16)
                    row += half
            else:
                for j in range(blocks // 2):
                    out[row : row + D] = acc[base + who * (blocks // 2) + j].astype(BF16)
                    row += D
        at = row
        base += blocks


EARLY = (("rows", 4), ("blocks", 4), ("rows", 4))
LATE = (("rows", 4),)


def sum_specs(last_chunk, kinds):
    const = lambda *s: pl.BlockSpec(s, lambda *g: (0,) * len(s))
    sd = jax.ShapeDtypeStruct
    blocks = sum(k[1] for k in kinds)
    if not last_chunk:
        return [const(blocks, D, D)], [sd((blocks, D, D), F32)], []
    half = (blocks * D // 2, D)
    return [const(*half)] * 2, [sd(half, BF16)] * 2, [pltpu.VMEM((blocks, D, D), F32)]


def middle(n, f, start, first_chunk, last_chunk, idx, seg, *refs):
    refs = list(refs)
    take = lambda c: [refs.pop(0) for _ in range(c)]
    a1, ct, conds = take(n), take(n), take(n)
    ada_a, ada_b, tq_t, tq, to, up, down = take(7)
    if not first_chunk:
        init = take(3)[0]
    dl = take(n)
    lo, hi, *sums = take(2 + (2 if last_chunk else 1))
    ou = [(lo, hi)[k // (n // 2)].at[k % (n // 2)] for k in range(n)]
    acc = refs.pop() if last_chunk else sums[0]
    init_sem = refs.pop()
    mod_s, sum_s, qkv_s, p_s, mix_s, dg_s, hid_s, dqkv_s = refs
    rows = a1[0].shape[2]
    groups = rows // GROUP
    frames = n * f
    span = frames * GROUP
    tokens = span * groups
    places = tile_places(n, f, rows)
    b = pl.program_id(0)

    @pl.when(b == 0)
    def _():
        if first_chunk:
            acc[...] = jnp.zeros_like(acc)
        else:
            pltpu.make_async_copy(init, acc, init_sem).start()
        sum_s[...] = jnp.zeros_like(sum_s)
        act = silu_low(jnp.concatenate([c[...] for c in conds], axis=0))
        mod_s[:, : 3 * D] = nn(act, ada_a[...])
        mod_s[:, 3 * D :] = nn(act, ada_b[...])

    pad = conds[0].shape[0]

    def per_frame(piece, plus=0.0):
        cols = slice(piece * D, (piece + 1) * D)
        at = [k * pad + (b + start) * f + j for k in range(n) for j in range(f)]
        rows_ = [mod_s[pl.ds(t, 1), cols] + plus for t in at]
        one = jnp.concatenate([jnp.broadcast_to(r, (GROUP, D)) for r in rows_], axis=0)
        return jnp.concatenate([one] * groups, axis=0)

    def frame_sum(piece, v):
        total = jnp.sum(jnp.sum(v.reshape(groups, frames, GROUP, D), axis=0), axis=1)
        for k in range(n):
            for j in range(f):
                sum_s[k, j * 6 + piece : j * 6 + piece + 1] = total[k * f + j : k * f + j + 1]

    def add(base, col, value):
        for j in range(value.shape[1] // D):
            acc[base + col // D + j] += value[:, j * D : (j + 1) * D]

    x1 = jnp.concatenate(
        [a1[k][0, r // rows, r % rows : r % rows + GROUP] for k, r in places], axis=0
    ).astype(F32)
    n2, r2 = norm_stats(x1)
    second = (n2 * per_frame(1, 1.0) + per_frame(0)).astype(BF16)
    qkv_s[...] = nt(tq_t[...], second).astype(BF16)
    lane = lax.broadcasted_iota(jnp.int32, (span, span), 0) % GROUP
    other = lax.broadcasted_iota(jnp.int32, (span, span), 1) % GROUP
    segs = [seg[b + start, t] for t in range(frames)]

    def segment_of(axis):
        at = lax.broadcasted_iota(jnp.int32, (span, span), axis) // GROUP
        value = jnp.zeros((span, span), jnp.int32)
        for t in range(frames):
            value = jnp.where(at == t, segs[t], value)
        return value

    allowed = (segment_of(0) == segment_of(1)) & (lane == other)
    bias = jnp.where(allowed, 0.0, -1e30)
    bias = jnp.concatenate([bias, bias], axis=1)
    items = [(g, j) for g in range(groups) for j in range(HEADS // 2)]

    def pair(ref, kind, g, j):
        a = kind * D + j * 2 * HD
        return ref[a : a + 2 * HD, g * span : (g + 1) * span]

    def scores(g, j):
        q = on_diagonal(pair(qkv_s, 0, g, j) * BF16(0.125))
        return (nn(pair(qkv_s, 1, g, j).T, q),)

    def mix(g, j, s):
        s = s + bias
        p = jnp.exp(s - jnp.max(s, axis=0, keepdims=True))
        p = p * (1.0 / jnp.sum(p, axis=0, keepdims=True))
        p_s[g * (HEADS // 2) + j] = p
        o = nn(pair(qkv_s, 2, g, j), p.astype(BF16)).astype(BF16)
        a, cols = j * 2 * HD, slice(g * span, (g + 1) * span)
        mix_s[a : a + HD, cols] = o[:HD, :span]
        mix_s[a + HD : a + 2 * HD, cols] = o[HD:, span:]

    pipelined(items, [scores, mix], 2 if span <= 256 else 0)
    br2 = tn(mix_s[...], to[...])
    x2 = x1 + per_frame(2) * br2
    n3, r3 = norm_stats(x2)
    third = (n3 * per_frame(4, 1.0) + per_frame(3)).astype(BF16)
    step = STEP
    br3 = []

    def mlp_in(c):
        return (nn(third, up[:, c : c + step]),)

    def mlp_out(c, pre):
        sq = pre * pre
        t = jnp.tanh(pre * (0.7978845608028654 + (0.7978845608028654 * 0.044715) * sq))
        half = 0.5 + 0.5 * t
        hid = (pre * half).astype(BF16)
        hid_s[:, c : c + step] = hid
        inner = 0.7978845608028654 + (3 * 0.7978845608028654 * 0.044715) * sq
        dg_s[:, c : c + step] = half + 0.5 * pre * (1.0 - t * t) * inner
        br3[:] = [sum(br3, nn(hid, down[c : c + step, :]))]

    pipelined([(c,) for c in range(0, MLP, step)], [mlp_in, mlp_out], 1)
    br3 = br3[0]
    gate3 = per_frame(5)
    value = (x2 + gate3 * br3).astype(BF16)
    for t, (k, r) in enumerate(places):
        ou[k][0, r // rows, r % rows : r % rows + GROUP] = value[t * GROUP : (t + 1) * GROUP]
    cot = jnp.concatenate([ct[k][r : r + GROUP] for k, r in places], axis=0).astype(F32)
    frame_sum(5, cot * br3)
    gb3 = (gate3 * cot).astype(BF16)
    if not first_chunk:

        @pl.when(b == 0)
        def _():
            pltpu.make_async_copy(init, acc, init_sem).wait()

    gb3_t = gb3.T
    third_t = third.T
    g3 = []

    def back_in(c):
        return (nt(gb3, down[c : c + step, :]),)

    def back_out(c, gh):
        gp = (gh * dg_s[:, c : c + step]).astype(BF16)
        add(4, c, nn(gb3_t, hid_s[:, c : c + step]))
        add(0, c, nn(third_t, gp))
        g3[:] = [sum(g3, nt(gp, up[:, c : c + step]))]

    pipelined([(c,) for c in range(0, MLP, step)], [back_in, back_out], 1)
    g3 = g3[0]
    frame_sum(3, g3)
    frame_sum(4, g3 * n3)
    dx3 = norm_back(g3 * per_frame(4, 1.0), n3, r3)
    ga2 = cot + dx3
    frame_sum(2, ga2 * br2)
    gb2 = (per_frame(2) * ga2).astype(BF16)
    add(11, 0, nn(mix_s[...], gb2))
    gm_t = nt(to[...], gb2).astype(BF16)

    def grads_in(g, j):
        go = on_diagonal(gm_t[j * 2 * HD : (j + 1) * 2 * HD, g * span : (g + 1) * span])
        return (go, nn(pair(qkv_s, 2, g, j).T, go))

    def grads_mid(g, j, go, dp):
        p = p_s[g * (HEADS // 2) + j]
        ds = (p * (dp - jnp.sum(p * dp, axis=0, keepdims=True))).astype(BF16)
        return (go, p.astype(BF16), ds)

    def grads_out(g, j, go, p, ds):
        a, cols = j * 2 * HD, slice(g * span, (g + 1) * span)
        q = on_diagonal(pair(qkv_s, 0, g, j) * BF16(0.125))
        dqkv_s[2 * D + a : 2 * D + a + 2 * HD, cols] = nt(go, p).astype(BF16)
        dqkv_s[D + a : D + a + 2 * HD, cols] = nt(q, ds).astype(BF16)
        dq = (nn(pair(qkv_s, 1, g, j), ds) * 0.125).astype(BF16)
        dqkv_s[a : a + HD, cols] = dq[:HD, :span]
        dqkv_s[a + HD : a + 2 * HD, cols] = dq[HD:, span:]

    pipelined(items, [grads_in, grads_mid, grads_out], 1 if span <= 256 else 0)
    dqkv = dqkv_s[...]
    add(8, 0, nt(second.T, dqkv))
    g2 = nn(tq[...], dqkv).T
    frame_sum(0, g2)
    frame_sum(1, g2 * n2)
    dx2 = norm_back(g2 * per_frame(1, 1.0), n2, r2)
    value = (dx3 + dx2).astype(BF16)
    for t, (k, r) in enumerate(places):
        dl[k][0, r : r + GROUP] = value[t * GROUP : (t + 1) * GROUP]
    for k in range(n):
        dl[k][0, f * rows :] = sum_s[k].astype(BF16)
    if last_chunk:

        @pl.when(b == pl.num_programs(0) - 1)
        def _():
            divide(idx[0] & 1, acc, sums[0], sums[1], EARLY)


STEP = 2 * D


def sum_rows(f):
    return -(-6 * f // GROUP) * GROUP


def call_middle(idx, seg, a1, ct, ada, tq_t, tq, to, up, down, init, start, last_chunk, packs):
    n = len(a1)
    count, f, rows = a1[0].shape[:3]
    frames = n * f
    span = frames * GROUP
    tokens = frames * rows
    groups = rows // GROUP
    pad = ct[0].shape[0] - packs * f * rows
    extra = sum_rows(f)
    part = lambda *s: pl.BlockSpec((1,) + s, lambda b, *i: (b,) + (0,) * len(s))
    fixed = lambda *s: pl.BlockSpec(s, lambda b, *i: (0,) * len(s), pipeline_mode=pl.Buffered(1))
    column = lambda j: pl.BlockSpec((D, 3 * D), lambda b, *i: (0, j), pipeline_mode=pl.Buffered(1))
    sd = jax.ShapeDtypeStruct
    sum_out, sum_shape, sum_scratch = sum_specs(last_chunk, EARLY)
    stack = (n // 2, packs, f, rows, D)
    stacked = pl.BlockSpec((n // 2, 1, f, rows, D), lambda b, *i: (0, b + start, 0, 0, 0))
    return pl.pallas_call(
        functools.partial(middle, n, f, start, not init, last_chunk),
        grid_spec=pltpu.PrefetchScalarGridSpec(
            num_scalar_prefetch=2,
            grid=(count,),
            in_specs=[part(f, rows, D)] * n
            + [pl.BlockSpec((f * rows, D), lambda b, *i: (b + start, 0))] * n
            + [pl.BlockSpec((pad, D), lambda b, *i: (packs * f * rows // pad, 0))] * n
            + [column(1), column(2), fixed(3 * D, D), fixed(D, 3 * D)]
            + [fixed(D, D), fixed(D, MLP), fixed(MLP, D)]
            + [pl.BlockSpec(memory_space=pl.ANY)] * len(init),
            out_specs=[part(f * rows + extra, D)] * n + [stacked] * 2 + sum_out,
            scratch_shapes=[
                pltpu.VMEM((n * pad, 6 * D), F32),
                pltpu.VMEM((n, extra, D), F32),
                pltpu.VMEM((3 * D, tokens), BF16),
                pltpu.VMEM((groups * HEADS // 2, span, 2 * span), F32),
                pltpu.VMEM((D, tokens), BF16),
                pltpu.VMEM((tokens, MLP), F32),
                pltpu.VMEM((tokens, MLP), BF16),
                pltpu.VMEM((3 * D, tokens), BF16),
                pltpu.SemaphoreType.DMA,
            ]
            + sum_scratch,
        ),
        out_shape=[sd((count, f * rows + extra, D), BF16)] * n + [sd(stack, BF16)] * 2 + sum_shape,
        input_output_aliases={2 + 3 * n + 8 + j: n + j for j in range(2)} if init else {},
        compiler_params=pltpu.CompilerParams(vmem_limit_bytes=VMEM),
        cost_estimate=cost(14 * count),
        name="middle",
    )(idx, seg, *a1, *ct, *ct, ada, ada, tq_t, tq, to, up, down, *init)


def spatial_bwd(n, first_chunk, last_chunk, idx, tok, cot, mod, qkv, mix, br, tot, wo, *rest):
    rest = list(rest)
    take = lambda c: [rest.pop(0) for _ in range(c)]
    if not first_chunk:
        init = take(1)[0]
    dl = take(n)
    dqkv_o, ga_o, gm_o, *sums = take(3 + (2 if last_chunk else 1))
    scr = rest.pop(0)
    acc = rest.pop() if last_chunk else sums[0]
    b = pl.program_id(0)

    @pl.when(b == 0)
    def _():
        acc[...] = jnp.zeros_like(acc) if first_chunk else init[...]
        gm_o[...] = jnp.zeros_like(gm_o)

    frames = tok.shape[1]
    rows = tok.shape[2] // n
    i = idx[0]
    total = sum(d[0, frames * rows :].astype(F32) for d in dl)
    gms = []
    for f in range(frames):
        for k in range(n):
            scr[pl.ds(pl.multiple_of((i ^ k) * rows, GROUP), rows), :] = dl[k][0, f * rows : (f + 1) * rows]
        ga = cot[0, f].astype(F32) + scr[...].astype(F32)
        ga_o[0, f] = ga
        gm_o[0, f * 7 : f * 7 + 1] = jnp.sum(ga * br[0, f].astype(F32), axis=0, keepdims=True)
        gm_o[0, f * 7 + 1 : f * 7 + 7] = total[f * 6 : f * 6 + 6]
        gb = (mod[0, f, 2:3] * ga).astype(BF16)
        acc[3] += nn(mix[0, f], gb)
        gms.append(nt(wo[...], gb).astype(BF16))

    def products(j, f):
        a = j * 2 * HD
        q = on_diagonal(qkv[0, f, a : a + 2 * HD] * BF16(0.125))
        go = on_diagonal(gms[f][a : a + 2 * HD])
        s = nn(qkv[0, f, D + a : D + a + 2 * HD].T, q)
        return s, nn(qkv[0, f, 2 * D + a : 2 * D + a + 2 * HD].T, go)

    def weights(j, f, s, dp):
        p = jnp.exp(s - tot[0, f, j : j + 1])
        ds = (p * (dp - jnp.sum(p * dp, axis=0, keepdims=True))).astype(BF16)
        return p.astype(BF16), ds

    def grads(j, f, p, ds):
        cut = p.shape[1] // 2
        for e in range(2):
            cols = slice(e * cut, (e + 1) * cut)
            at = j * 2 * HD + e * HD
            q = qkv[0, f, at : at + HD] * BF16(0.125)
            k = qkv[0, f, D + at : D + at + HD]
            dqkv_o[0, f, 2 * D + at : 2 * D + at + HD] = nt(gms[f][at : at + HD], p[:, cols]).astype(BF16)
            dqkv_o[0, f, D + at : D + at + HD] = nt(q, ds[:, cols]).astype(BF16)
            dqkv_o[0, f, at : at + HD] = (nn(k, ds[:, cols]) * 0.125).astype(BF16)

    pipelined([(j, f) for j in range(HEADS // 2) for f in range(frames)], [products, weights, grads], 1)
    for f in range(frames):
        nrm, _ = norm_stats(tok[0, f].astype(F32))
        first = (nrm * (1.0 + mod[0, f, 1:2]) + mod[0, f, 0:1]).astype(BF16)
        value = nt(first.T, dqkv_o[0, f])
        for j in range(3):
            acc[j] += value[:, j * D : (j + 1) * D]
    if last_chunk:

        @pl.when(b == pl.num_programs(0) - 1)
        def _():
            divide(i & 1, acc, sums[0], sums[1], LATE)


def call_spatial_bwd(idx, tok, cot, mod, qkv, mix, br, tot, wo, init, dl, start, last_chunk):
    n = len(dl)
    count = dl[0].shape[0]
    f, p = tok.shape[1:3]
    whole = lambda *s: pl.BlockSpec((1, f) + s, lambda b, i: (b + start, 0) + (0,) * len(s))
    part = lambda *s: pl.BlockSpec((1, f) + s, lambda b, i: (b, 0) + (0,) * len(s))
    pack = lambda *s: pl.BlockSpec((1,) + s, lambda b, i: (b,) + (0,) * len(s))
    fixed = lambda *s: pl.BlockSpec(s, lambda b, i: (0,) * len(s), pipeline_mode=pl.Buffered(1))
    sd = lambda s, d: jax.ShapeDtypeStruct((count,) + s, d)
    sum_out, sum_shape, sum_scratch = sum_specs(last_chunk, LATE)
    gm_rows = -(-7 * f // 8) * 8
    return pl.pallas_call(
        functools.partial(spatial_bwd, n, not init, last_chunk),
        grid_spec=pltpu.PrefetchScalarGridSpec(
            num_scalar_prefetch=1,
            grid=(count,),
            in_specs=[whole(p, D), whole(p, D), part(3, D), part(3 * D, p), part(D, p)]
            + [part(p, D), part(HEADS // 2, 2 * p), fixed(D, D)]
            + [fixed(4, D, D)] * len(init)
            + [pack(*dl[0].shape[1:])] * n,
            out_specs=[part(3 * D, p), part(p, D), pack(gm_rows, D)] + sum_out,
            scratch_shapes=[pltpu.VMEM((p, D), BF16)] + sum_scratch,
        ),
        out_shape=[sd((f, 3 * D, p), BF16), sd((f, p, D), F32), sd((gm_rows, D), F32)] + sum_shape,
        compiler_params=pltpu.CompilerParams(vmem_limit_bytes=VMEM),
        cost_estimate=cost(5 * count),
        name="spatial_bwd",
    )(idx, tok, cot, mod, qkv, mix, br, tot, wo, *init, *dl)


def last_step(masks, idx, tok, mod, w, dqkv, ga, *rest):
    grad_o, out_o, gs_o = rest[-3:]
    rows = rest[0].shape[3]
    frames = tok.shape[1]
    i = idx[0]
    gs_o[...] = jnp.zeros_like(gs_o)

    def product(f):
        for k, piece in zip(masks, rest):
            out_o[0, f, pl.ds(pl.multiple_of((i ^ k) * rows, GROUP), rows), :] = piece[0, 0, f]
        return (nt(dqkv[0, f].T, w[...]),)

    def finish(f, g):
        nrm, r = norm_stats(tok[0, f].astype(F32))
        gs_o[0, f * 2 : f * 2 + 1] = jnp.sum(g, axis=0, keepdims=True)
        gs_o[0, f * 2 + 1 : f * 2 + 2] = jnp.sum(g * nrm, axis=0, keepdims=True)
        grad_o[0, f] = ga[0, f] + norm_back(g * (1.0 + mod[0, f, 1:2]), nrm, r)

    pipelined([(f,) for f in range(frames)], [product, finish], 1)


def call_last(idx, tok, mod, w, dqkv, ga, ou, start, held):
    n = len(ou)
    arrays, offsets, masks = zip(*ou)
    count, f = dqkv.shape[:2]
    rows = arrays[0].shape[3]
    p = tok.shape[2]
    gs_rows = -(-2 * f // 8) * 8
    whole = lambda *s: pl.BlockSpec((1, f) + s, lambda b, i: (b + start, 0) + (0,) * len(s))
    part = lambda *s: pl.BlockSpec((1, f) + s, lambda b, i: (b, 0) + (0,) * len(s))
    fixed = lambda *s: pl.BlockSpec(s, lambda b, i: (0,) * len(s), pipeline_mode=pl.Buffered(1))
    piece = lambda j: pl.BlockSpec((1, 1, f, rows, D), lambda b, i: (j, b + start, 0, 0, 0))
    sd = jax.ShapeDtypeStruct
    return pl.pallas_call(
        functools.partial(last_step, masks),
        grid_spec=pltpu.PrefetchScalarGridSpec(
            num_scalar_prefetch=1,
            grid=(count,),
            in_specs=[whole(p, D), part(3, D), fixed(D, 3 * D), part(3 * D, p), part(p, D)]
            + [piece(j) for j in offsets]
            + [pl.BlockSpec(memory_space=pl.ANY)] * len(held),
            out_specs=[whole(p, D), whole(p, D), pl.BlockSpec((1, gs_rows, D), lambda b, i: (b, 0, 0))],
        ),
        out_shape=[sd(tok.shape, F32), sd(tok.shape, BF16), sd((count, gs_rows, D), F32)],
        input_output_aliases={6 + n + j: j for j in range(len(held))},
        compiler_params=pltpu.CompilerParams(vmem_limit_bytes=VMEM),
        cost_estimate=cost(3 * count),
        name="last_step",
    )(idx, tok, mod, w, dqkv, ga, *arrays, *held)


def finish_early(idx, data, *refs):
    up_o, down_o, qkv_o, out_o = refs[-4:]
    half = D // 2
    for j in range(4):
        cols = slice(j * D, (j + 1) * D)
        up_o[:, cols] = data[j * half : (j + 1) * half].astype(F32)
        if j < 3:
            qkv_o[:, cols] = data[4 * D + j * half : 4 * D + (j + 1) * half].astype(F32)
    out_o[...] = data[4 * D + 3 * half :].astype(F32)
    for j in range(2):
        down_o[j * D : (j + 1) * D] = data[2 * D + j * D : 2 * D + (j + 1) * D].T.astype(F32)


def finish_late(idx, data, *refs):
    qkv_o, out_o = refs[-2:]
    half = D // 2
    for j in range(3):
        qkv_o[:, j * D : (j + 1) * D] = data[j * half : (j + 1) * half].astype(F32)
    out_o[...] = data[3 * half :].astype(F32)


def call_finish(kernel, shapes, idx, data, flip, held):
    spec = lambda s: pl.BlockSpec((s[0] // 2, s[1]), lambda j, i: ((i[0] & 1) ^ flip, 0))
    return pl.pallas_call(
        kernel,
        grid_spec=pltpu.PrefetchScalarGridSpec(
            num_scalar_prefetch=1,
            grid=(1,),
            in_specs=[pl.BlockSpec(data.shape, lambda j, i: (0, 0))]
            + [pl.BlockSpec(memory_space=pl.ANY)] * len(held),
            out_specs=[spec(s) for s in shapes],
        ),
        out_shape=[jax.ShapeDtypeStruct(s, F32) for s in shapes],
        input_output_aliases={2 + j: j for j in range(len(held))},
        compiler_params=pltpu.CompilerParams(vmem_limit_bytes=VMEM),
        cost_estimate=cost(2),
        name=kernel.__name__,
    )(idx, data, *held)


def ada_grad(act, mod, out):
    out[...] = nn(silu_low(act[...]).T, mod[...])


def call_ada_grad(rows):
    width = 9 * D
    step = 3 * D
    return pl.pallas_call(
        ada_grad,
        grid=(3,),
        in_specs=[
            pl.BlockSpec((rows.shape[0], D), lambda j: (0, 9)),
            pl.BlockSpec((rows.shape[0], step), lambda j: (0, j)),
        ],
        out_specs=pl.BlockSpec((D, step), lambda j: (0, j)),
        out_shape=jax.ShapeDtypeStruct((D, width), F32),
        compiler_params=pltpu.CompilerParams(vmem_limit_bytes=VMEM),
        cost_estimate=cost(3),
        name="ada_grad",
    )(rows, rows)


def swap(x, axis, mask):
    size = lax.axis_size(axis)
    return lax.ppermute(x, axis, [(s, s ^ mask) for s in range(size)])


def bits_of(axis):
    return [(axis, b) for b in range(lax.axis_size(axis).bit_length() - 1)]


def bit_of(axis, b):
    return (lax.axis_index(axis) >> b) & 1


def orders():
    pack, frame = bits_of("pack"), bits_of("frame")[1:]
    path = pack[:2]
    pack = pack[2:]
    while pack or frame:
        path += frame[:1] + pack[:1]
        pack, frame = pack[1:], frame[1:]
    turned = []
    for j in range(0, len(path), 2):
        turned += path[j : j + 2][::-1]
    return path, turned


def swap_by_core(x, step):
    nf, npk = lax.axis_size("frame"), lax.axis_size("pack")
    perm = []
    for pack in range(npk):
        for frame in range(nf):
            axis, b = step[frame & 1]
            to = (pack ^ (1 << b), frame) if axis == "pack" else (pack, frame ^ (1 << b))
            perm.append((frame * npk + pack, to[1] * npk + to[0]))
    return lax.ppermute(x, ("frame", "pack"), perm)


def bit_by_core(step):
    core = bit_of("frame", 0)
    return jnp.where(core == 0, bit_of(*step[0]), bit_of(*step[1]))


def doubled(g, other, mine):
    return jnp.concatenate([jnp.where(mine, other, g), jnp.where(mine, g, other)], axis=0)


def tie_all(values, *deps):
    return list(lax.optimization_barrier((*values, *deps))[: len(values)])


def tie(value, *deps):
    return lax.optimization_barrier((value, *deps))[0]


class Summing:
    def __init__(self, send, keep, halvings):
        self.keep = keep
        self.steps = list(zip(*orders()))
        self.halvings = halvings
        self.at = 0
        self.back = []
        self.moving = swap(send, "frame", 1)
        self.value = None

    def advance(self, after=None):
        moving = self.moving if after is None else tie(self.moving, after)
        if self.at <= len(self.steps):
            self.value = (self.keep.astype(F32) + moving.astype(F32)).astype(BF16)
        else:
            self.value = doubled(self.value, moving, bit_by_core(self.back.pop()) == 1)
        if self.at < len(self.steps):
            step = self.steps[self.at]
            self.at += 1
            if self.at <= self.halvings:
                mine = bit_by_core(step)
                half = self.value.shape[0] // 2
                send = lax.dynamic_slice_in_dim(self.value, (1 - mine) * half, half, 0)
                self.keep = lax.dynamic_slice_in_dim(self.value, mine * half, half, 0)
                self.back.append(step)
            else:
                send = self.keep = self.value
        else:
            self.at += 1
            send = self.value
            if not self.back:
                return False
            step = self.back[-1]
        self.sent = send
        self.moving = swap_by_core(send, step)
        return True


class Regroup:
    def __init__(self, lo, hi):
        self.count = lo.shape[0]
        self.pieces = [(lo, 0, 0)]
        self.start(hi)

    def start(self, send):
        self.moving = swap(send, "frame", self.count)

    def arrive(self, after=None):
        got = self.moving if after is None else tie(self.moving, after)
        k = self.count
        self.pieces += [(got, j * k, m ^ k) for j, (_, _, m) in enumerate(self.pieces)]
        if k > 1:
            half = k // 2
            send = jnp.concatenate([a[o + half : o + k] for a, o, _ in self.pieces], axis=0)
            self.count = half
            self.start(send)
            return False
        return True


def local(
    tokens,
    condition,
    clip_lengths,
    ada_weight,
    spatial_qkv,
    spatial_out,
    temporal_qkv,
    temporal_out,
    mlp_up,
    mlp_down,
    cotangent,
):
    n = lax.axis_size("frame")
    i = lax.axis_index("frame")
    idx = i.reshape(1).astype(jnp.int32)
    packs, f, patches = tokens.shape[:3]
    rows = patches // n
    count = packs // CHUNKS
    send = lambda parts: [parts[0]] + [swap(parts[k], "frame", k) for k in range(1, n)]

    own_cond = condition.reshape(packs * f, D)
    pad = -(-packs * f // GROUP) * GROUP
    cond_rows = jnp.concatenate([own_cond, jnp.zeros((pad - packs * f, D), BF16)], axis=0)

    def cut(k):
        v = lax.dynamic_slice_in_dim(cotangent, (i ^ k) * rows, rows, 2)
        return jnp.concatenate([v.reshape(-1, D), cond_rows], axis=0)

    ct = send([cut(k) for k in range(n)])
    sq_t = spatial_qkv.T
    tq_t = temporal_qkv.T
    frame_ids = jnp.concatenate([(i ^ k) * f + jnp.arange(f, dtype=jnp.int32) for k in range(n)])
    ends = [jnp.sum(clip_lengths[:, : j + 1], axis=1) for j in range(clip_lengths.shape[1])]
    segment = sum((e[:, None] <= frame_ids[None, :]).astype(jnp.int32) for e in ends)

    fwd = []
    source = tokens
    for c in range(CHUNKS):
        res = call_spatial_fwd(idx, source, condition, ada_weight, sq_t, spatial_out, c * count, count, n)
        slots = list(res[5:])
        if c:
            slots = tie_all(slots, *fwd[-1][1][1:])
        fwd.append((res[:5], send(slots)))
        if c == 0:
            source = tie(tokens, segment, tq_t, *ct[1:])

    init, mids = [], []
    for c in range(CHUNKS):
        last = c == CHUNKS - 1
        res = call_middle(
            idx, segment, fwd[c][1], ct, ada_weight, tq_t, temporal_qkv, temporal_out, mlp_up, mlp_down,
            init, c * count, last, packs,
        )
        init = [res[n + 2], res[n], res[n + 1]]
        res = list(res)
        if c:
            res = tie_all(res, *mids[-1][1:])
        mids.append(send(res[:n]))
    early = Summing(res[n + 2], res[n + 3], 3)
    outs = Regroup(res[n], res[n + 1])

    acc, backs = [], []
    for c in range(CHUNKS):
        last = c == CHUNKS - 1
        qkv, mix, br, tot, mod = fwd[c][0]
        dl = mids[c]
        if c:
            early.advance(after=backs[-1][2])
            dl = tie_all(dl, early.sent)
        res = call_spatial_bwd(
            idx, tokens, cotangent, mod, qkv, mix, br, tot, spatial_out, acc, dl, c * count, last
        )
        acc = list(res[3:])
        backs.append(res)
    late = Summing(acc[0], acc[1], 2)
    early.advance(after=backs[-1][2])
    while not outs.arrive(after=backs[-1][2]):
        pass
    lasts, held = [], []
    for c in range(CHUNKS):
        dqkv, ga = backs[c][:2]
        if c:
            late.advance(after=lasts[-1][2])
            early.advance(after=lasts[-1][2])
            ga = tie(ga, early.sent, late.sent)
        else:
            ga = tie(ga, early.sent)
        res = call_last(idx, tokens, fwd[c][0][4], spatial_qkv, dqkv, ga, outs.pieces, c * count, held)
        held = list(res[:2])
        lasts.append(res)
    grad_tokens, output = held

    gates = jnp.concatenate([b[2] for b in backs], 0)[:, : 7 * f].reshape(packs, f, 7 * D)
    norms = jnp.concatenate([v[2] for v in lasts], 0)[:, : 2 * f].reshape(packs, f, 2 * D)
    own = jnp.concatenate([norms, gates], axis=2).astype(BF16).reshape(packs * f, 9 * D)
    every = bits_of("pack")[::-1] + bits_of("frame")[::-1]
    all_rows = jnp.concatenate([own, own_cond], axis=1)
    late_going = early_going = True
    after = lasts[-1][2]
    for axis, b in every:
        other = swap(all_rows, axis, 1 << b)
        if late_going:
            late_going = late.advance(after)
        if early_going:
            early_going = early.advance(after)
        all_rows = doubled(all_rows, other, bit_of(axis, b) == 1)
        after = None
    while late_going:
        late_going = late.advance()
    while early_going:
        early_going = early.advance()
    grad_ada = call_ada_grad(all_rows)
    back = jnp.einsum("tj,ij->ti", own, ada_weight, preferred_element_type=F32).reshape(packs, f, D)
    cf = condition.astype(F32)
    sig = 1.0 / (1.0 + jnp.exp(-cf))
    grad_condition = back * (sig * (1.0 + cf * (1.0 - sig)))

    made = []
    for kernel, summing, shapes in (
        (finish_late, late, [(D, 3 * D), (D, D)]),
        (finish_early, early, [(D, MLP), (MLP, D), (D, 3 * D), (D, D)]),
    ):
        other = swap(summing.value, "frame", 1)
        half = call_finish(kernel, shapes, idx, summing.value, 0, [])
        made.append(call_finish(kernel, shapes, idx, other, 1, list(half)))
    (s_qkv, s_out), (up, down, t_qkv, t_out) = made
    return (output, grad_tokens, grad_condition, grad_ada, s_qkv, s_out, t_qkv, t_out, up, down)


def solution(mesh):
    tok = P("pack", "frame", None, None)
    cond = P("pack", "frame", None)
    return jax.shard_map(
        local,
        mesh=mesh,
        in_specs=(tok, cond, P("pack", None), P(), P(), P(), P(), P(), P(), P(), tok),
        out_specs=(tok, tok, cond, P(), P(), P(), P(), P(), P(), P()),
        check_vma=False,
    )
```

```python
import functools

import jax
import jax.numpy as jnp
from jax import lax
from jax.experimental import pallas as pl
from jax.experimental.pallas import tpu as pltpu
from jax.sharding import PartitionSpec as P

D = 384
HEADS = 6
HD = 64
MLP = 1536
F32 = jnp.float32
BF16 = jnp.bfloat16
CHUNKS = 2
GROUP = 16
VMEM = 58 * 2**20


def nn(a, b):
    return lax.dot_general(a, b, (((1,), (0,)), ((), ())), preferred_element_type=F32)


def nt(a, b):
    return lax.dot_general(a, b, (((1,), (1,)), ((), ())), preferred_element_type=F32)


def tn(a, b):
    return lax.dot_general(a, b, (((0,), (0,)), ((), ())), preferred_element_type=F32)


def cost(us):
    return pl.CostEstimate(flops=int(us * 1.0e9), bytes_accessed=1000, transcendentals=0)


def silu_low(v):
    v = v.astype(F32)
    return (v / (1.0 + jnp.exp(-v))).astype(BF16)


def on_diagonal(pair):
    none = jnp.zeros_like(pair[:HD])
    return jnp.concatenate(
        [
            jnp.concatenate([pair[:HD], none], axis=1),
            jnp.concatenate([none, pair[HD:]], axis=1),
        ],
        axis=0,
    )


def norm_stats(x):
    c = x - jnp.mean(x, -1, keepdims=True)
    r = lax.rsqrt(jnp.mean(c * c, -1, keepdims=True) + 1e-6)
    return c * r, r


def norm_back(h, n, r):
    return r * (h - jnp.mean(h, -1, keepdims=True) - n * jnp.mean(h * n, -1, keepdims=True))


def pipelined(items, stages, ahead=1):
    held = [[] for _ in stages]
    last = len(stages) - 1
    for t in range(len(items) + ahead * last):
        for s, stage in enumerate(stages):
            at = t - s * ahead
            if 0 <= at < len(items):
                value = stage(*items[at], *(held[s - 1].pop(0) if s else ()))
                if s < last:
                    held[s].append(value)


def spatial_fwd(start, idx, tok, cond, ada, w_t, wo, qkv_o, mix_o, br_o, tot_o, mod_o, *rest):
    slots, (scr, mod_s) = rest[:-2], rest[-2:]
    rows = slots[0].shape[2]
    frames = tok.shape[1]
    b = pl.program_id(0)

    @pl.when(b == 0)
    def _():
        mod_s[...] = nn(silu_low(cond[...]), ada[...])

    i = idx[0]
    mds = []
    for f in range(frames):
        at = (b + start) * frames + f
        md = [mod_s[pl.ds(at, 1), j * D : (j + 1) * D] for j in range(3)]
        for j in range(3):
            mod_o[0, f, j : j + 1] = md[j]
        n, _ = norm_stats(tok[0, f].astype(F32))
        first = (n * (1.0 + md[1]) + md[0]).astype(BF16)
        qkv_o[0, f] = nt(w_t[...], first).astype(BF16)
        mds.append(md)

    def scores(j, f):
        a = j * 2 * HD
        q = on_diagonal(qkv_o[0, f, a : a + 2 * HD] * BF16(0.125))
        k = qkv_o[0, f, D + a : D + a + 2 * HD]
        return (nn(k.T, q),)

    def mix(j, f, s):
        a = j * 2 * HD
        mx = jnp.max(s, axis=0, keepdims=True)
        p = jnp.exp(s - mx)
        total = jnp.sum(p, axis=0, keepdims=True)
        tot_o[0, f, j : j + 1] = mx + jnp.log(total)
        p = p.astype(BF16)
        scale = 1.0 / total
        cut = p.shape[1] // 2
        for e in range(2):
            v = qkv_o[0, f, 2 * D + a + e * HD : 2 * D + a + (e + 1) * HD]
            cols = slice(e * cut, (e + 1) * cut)
            mix_o[0, f, a + e * HD : a + (e + 1) * HD] = (nn(v, p[:, cols]) * scale[:, cols]).astype(BF16)

    pipelined([(j, f) for j in range(HEADS // 2) for f in range(frames)], [scores, mix], 2)
    for f in range(frames):
        br = tn(mix_o[0, f], wo[...])
        br_o[0, f] = br.astype(BF16)
        scr[f] = (tok[0, f].astype(F32) + mds[f][2] * br).astype(BF16)
        for k, slot in enumerate(slots):
            slot[0, f] = scr[f, pl.ds(pl.multiple_of((i ^ k) * rows, GROUP), rows), :]


def call_spatial_fwd(idx, tok, cond, ada, w_t, wo, start, count, n):
    f = tok.shape[1]
    p = tok.shape[2]
    whole = lambda *s: pl.BlockSpec((1, f) + s, lambda b, i: (b + start, 0) + (0,) * len(s))
    part = lambda *s: pl.BlockSpec((1, f) + s, lambda b, i: (b, 0) + (0,) * len(s))
    fixed = lambda *s: pl.BlockSpec(s, lambda b, i: (0,) * len(s), pipeline_mode=pl.Buffered(1))
    sd = lambda s, d: jax.ShapeDtypeStruct((count, f) + s, d)
    own = tok.shape[0] * f
    return pl.pallas_call(
        functools.partial(spatial_fwd, start),
        grid_spec=pltpu.PrefetchScalarGridSpec(
            num_scalar_prefetch=1,
            grid=(count,),
            in_specs=[whole(p, D), fixed(own, D), fixed(D, 3 * D), fixed(3 * D, D), fixed(D, D)],
            out_specs=[part(3 * D, p), part(D, p), part(p, D), part(HEADS // 2, 2 * p), part(3, D)]
            + [part(p // n, D)] * n,
            scratch_shapes=[pltpu.VMEM((f, p, D), BF16), pltpu.VMEM((own, 3 * D), F32)],
        ),
        out_shape=[sd((3 * D, p), BF16), sd((D, p), BF16), sd((p, D), BF16)]
        + [sd((HEADS // 2, 2 * p), F32), sd((3, D), F32)]
        + [sd((p // n, D), BF16)] * n,
        compiler_params=pltpu.CompilerParams(vmem_limit_bytes=VMEM),
        cost_estimate=cost(4 * count),
        name="spatial_fwd",
    )(idx, tok, cond.reshape(-1, D), ada, w_t, wo)


def tile_places(n, f, rows):
    return [
        (k, j * rows + g * GROUP)
        for g in range(rows // GROUP)
        for k in range(n)
        for j in range(f)
    ]


def divide(mine, acc, sent, kept, kinds):
    at = 0
    base = 0
    for kind, blocks in kinds:
        for out, who in ((sent, 1 - mine), (kept, mine)):
            row = at
            if kind == "rows":
                half = D // 2
                for j in range(blocks):
                    part = acc[base + j, pl.ds(pl.multiple_of(who * half, GROUP), half), :]
                    out[row : row + half] = part.astype(BF16)
                    row += half
            else:
                for j in range(blocks // 2):
                    out[row : row + D] = acc[base + who * (blocks // 2) + j].astype(BF16)
                    row += D
        at = row
        base += blocks


EARLY = (("rows", 4), ("blocks", 4), ("rows", 4))
LATE = (("rows", 4),)


def sum_specs(last_chunk, kinds):
    const = lambda *s: pl.BlockSpec(s, lambda *g: (0,) * len(s))
    sd = jax.ShapeDtypeStruct
    blocks = sum(k[1] for k in kinds)
    if not last_chunk:
        return [const(blocks, D, D)], [sd((blocks, D, D), F32)], []
    half = (blocks * D // 2, D)
    return [const(*half)] * 2, [sd(half, BF16)] * 2, [pltpu.VMEM((blocks, D, D), F32)]


def middle(n, f, start, first_chunk, last_chunk, once, idx, seg, *refs):
    refs = list(refs)
    take = lambda c: [refs.pop(0) for _ in range(c)]
    a1, ct, conds = take(n), take(n), take(n)
    ada_a, ada_b, tq_t, tq, to, up, down = take(7)
    if not first_chunk:
        init = take(1 + n)[0]
    dl = take(n)
    ou = take(n)
    sums = take(2 if last_chunk else 1)
    acc, init_sem = refs.pop(), refs.pop()
    mod_s, sum_s, qkv_s, p_s, mix_s, dg_s, hid_s, dqkv_s = refs
    rows = a1[0].shape[2]
    groups = rows // GROUP
    frames = n * f
    span = frames * GROUP
    tokens = span * groups
    places = tile_places(n, f, rows)
    b = pl.program_id(0)
    fresh = first_chunk and once

    @pl.when(b == 0)
    def _():
        if not first_chunk:
            pltpu.make_async_copy(init, acc, init_sem).start()
        elif not fresh:
            acc[...] = jnp.zeros_like(acc)
        sum_s[...] = jnp.zeros_like(sum_s)
        act = silu_low(jnp.concatenate([c[...] for c in conds], axis=0))
        mod_s[:, : 3 * D] = nn(act, ada_a[...])
        mod_s[:, 3 * D :] = nn(act, ada_b[...])

    pad = conds[0].shape[0]
    units = a1[0].shape[0]

    def tile(u):
        pack = b * units + u

        def per_frame(piece, plus=0.0):
            cols = slice(piece * D, (piece + 1) * D)
            at = [k * pad + (pack + start) * f + j for k in range(n) for j in range(f)]
            rows_ = [mod_s[pl.ds(t, 1), cols] + plus for t in at]
            one = jnp.concatenate([jnp.broadcast_to(r, (GROUP, D)) for r in rows_], axis=0)
            return jnp.concatenate([one] * groups, axis=0)

        def frame_sum(piece, v):
            total = jnp.sum(jnp.sum(v.reshape(groups, frames, GROUP, D), axis=0), axis=1)
            for k in range(n):
                for j in range(f):
                    sum_s[u, k, j * 6 + piece : j * 6 + piece + 1] = total[k * f + j : k * f + j + 1]

        def add(base, col, value):
            for j in range(value.shape[1] // D):
                part = value[:, j * D : (j + 1) * D]
                at = base + col // D + j
                acc[at] = part if fresh and u == 0 else acc[at] + part

        x1 = jnp.concatenate(
            [a1[k][u, r // rows, r % rows : r % rows + GROUP] for k, r in places], axis=0
        ).astype(F32)
        n2, r2 = norm_stats(x1)
        second = (n2 * per_frame(1, 1.0) + per_frame(0)).astype(BF16)
        yield
        qkv_s[u] = nt(tq_t[...], second).astype(BF16)
        lane = lax.broadcasted_iota(jnp.int32, (span, span), 0) % GROUP
        other = lax.broadcasted_iota(jnp.int32, (span, span), 1) % GROUP
        segs = [seg[pack + start, t] for t in range(frames)]

        def segment_of(axis):
            at = lax.broadcasted_iota(jnp.int32, (span, span), axis) // GROUP
            value = jnp.zeros((span, span), jnp.int32)
            for t in range(frames):
                value = jnp.where(at == t, segs[t], value)
            return value

        allowed = (segment_of(0) == segment_of(1)) & (lane == other)
        bias = jnp.where(allowed, 0.0, -1e30)
        bias = jnp.concatenate([bias, bias], axis=1)
        items = [(g, j) for g in range(groups) for j in range(HEADS // 2)]

        def pair(ref, kind, g, j):
            a = kind * D + j * 2 * HD
            return ref[u, a : a + 2 * HD, g * span : (g + 1) * span]

        def scores(g, j):
            q = on_diagonal(pair(qkv_s, 0, g, j) * BF16(0.125))
            return (nn(pair(qkv_s, 1, g, j).T, q),)

        def mix(g, j, s):
            s = s + bias
            p = jnp.exp(s - jnp.max(s, axis=0, keepdims=True))
            p = p * (1.0 / jnp.sum(p, axis=0, keepdims=True))
            p_s[u, g * (HEADS // 2) + j] = p
            o = nn(pair(qkv_s, 2, g, j), p.astype(BF16)).astype(BF16)
            a, cols = j * 2 * HD, slice(g * span, (g + 1) * span)
            mix_s[u, a : a + HD, cols] = o[:HD, :span]
            mix_s[u, a + HD : a + 2 * HD, cols] = o[HD:, span:]

        pipelined(items, [scores, mix], 2 if span <= 256 else 0)
        yield
        br2 = tn(mix_s[u], to[...])
        x2 = x1 + per_frame(2) * br2
        n3, r3 = norm_stats(x2)
        third = (n3 * per_frame(4, 1.0) + per_frame(3)).astype(BF16)
        yield
        step = STEP
        br3 = []

        def mlp_in(c):
            return (nn(third, up[:, c : c + step]),)

        def mlp_out(c, pre):
            sq = pre * pre
            t = jnp.tanh(pre * (0.7978845608028654 + (0.7978845608028654 * 0.044715) * sq))
            half = 0.5 + 0.5 * t
            hid = (pre * half).astype(BF16)
            hid_s[u, :, c : c + step] = hid
            inner = 0.7978845608028654 + (3 * 0.7978845608028654 * 0.044715) * sq
            dg_s[u, :, c : c + step] = (half + 0.5 * pre * (1.0 - t * t) * inner).astype(BF16)
            br3[:] = [sum(br3, nn(hid, down[c : c + step, :]))]

        pipelined([(c,) for c in range(0, MLP, step)], [mlp_in, mlp_out], 1)
        br3 = br3[0]
        yield
        gate3 = per_frame(5)
        value = (x2 + gate3 * br3).astype(BF16)
        for t, (k, r) in enumerate(places):
            ou[k][u, r // rows, r % rows : r % rows + GROUP] = value[t * GROUP : (t + 1) * GROUP]
        cot = jnp.concatenate([ct[k][u * f * rows + r : u * f * rows + r + GROUP] for k, r in places], axis=0).astype(F32)
        frame_sum(5, cot * br3)
        gb3 = (gate3 * cot).astype(BF16)
        if not first_chunk and u == 0:

            @pl.when(b == 0)
            def _():
                pltpu.make_async_copy(init, acc, init_sem).wait()

        gb3_t = gb3.T
        third_t = third.T
        yield
        g3 = []

        def back_in(c):
            return (nt(gb3, down[c : c + step, :]),)

        def back_out(c, gh):
            gp = (gh * dg_s[u, :, c : c + step]).astype(BF16)
            add(4, c, nn(gb3_t, hid_s[u, :, c : c + step]))
            add(0, c, nn(third_t, gp))
            g3[:] = [sum(g3, nt(gp, up[:, c : c + step]))]

        pipelined([(c,) for c in range(0, MLP, step)], [back_in, back_out], 1)
        g3 = g3[0]
        yield
        frame_sum(3, g3)
        frame_sum(4, g3 * n3)
        dx3 = norm_back(g3 * per_frame(4, 1.0), n3, r3)
        ga2 = cot + dx3
        frame_sum(2, ga2 * br2)
        gb2 = (per_frame(2) * ga2).astype(BF16)
        add(11, 0, nn(mix_s[u], gb2))
        gm_t = nt(to[...], gb2).astype(BF16)
        yield

        def grads_in(g, j):
            go = on_diagonal(gm_t[j * 2 * HD : (j + 1) * 2 * HD, g * span : (g + 1) * span])
            return (go, nn(pair(qkv_s, 2, g, j).T, go))

        def grads_mid(g, j, go, dp):
            p = p_s[u, g * (HEADS // 2) + j]
            ds = (p * (dp - jnp.sum(p * dp, axis=0, keepdims=True))).astype(BF16)
            return (go, p.astype(BF16), ds)

        def grads_out(g, j, go, p, ds):
            a, cols = j * 2 * HD, slice(g * span, (g + 1) * span)
            q = on_diagonal(pair(qkv_s, 0, g, j) * BF16(0.125))
            dqkv_s[u, 2 * D + a : 2 * D + a + 2 * HD, cols] = nt(go, p).astype(BF16)
            dqkv_s[u, D + a : D + a + 2 * HD, cols] = nt(q, ds).astype(BF16)
            dq = (nn(pair(qkv_s, 1, g, j), ds) * 0.125).astype(BF16)
            dqkv_s[u, a : a + HD, cols] = dq[:HD, :span]
            dqkv_s[u, a + HD : a + 2 * HD, cols] = dq[HD:, span:]

        pipelined(items, [grads_in, grads_mid, grads_out], 1 if span <= 256 else 0)
        yield
        dqkv = dqkv_s[u]
        add(8, 0, nt(second.T, dqkv))
        g2 = nn(tq[...], dqkv).T
        yield
        frame_sum(0, g2)
        frame_sum(1, g2 * n2)
        dx2 = norm_back(g2 * per_frame(1, 1.0), n2, r2)
        value = (dx3 + dx2).astype(BF16)
        for t, (k, r) in enumerate(places):
            dl[k][u, r : r + GROUP] = value[t * GROUP : (t + 1) * GROUP]
        for k in range(n):
            dl[k][u, f * rows :] = sum_s[u, k].astype(BF16)

    tiles = [tile(u) for u in range(units)]
    turn = 0
    while tiles:
        for t in list(tiles[: turn + 1]):
            if next(t, True):
                tiles.remove(t)
                turn -= 1
        turn += 1
    if last_chunk:

        @pl.when(b == pl.num_programs(0) - 1)
        def _():
            divide(idx[0] & 1, acc, sums[0], sums[1], EARLY)

    else:

        @pl.when(b == pl.num_programs(0) - 1)
        def _():
            copy = pltpu.make_async_copy(acc, sums[0], init_sem)
            copy.start()
            copy.wait()


STEP = 2 * D


def sum_rows(f):
    return -(-6 * f // GROUP) * GROUP


def call_middle(idx, seg, a1, ct, ada, tq_t, tq, to, up, down, init, start, last_chunk, packs):
    n = len(a1)
    count, f, rows = a1[0].shape[:3]
    frames = n * f
    span = frames * GROUP
    tokens = frames * rows
    groups = rows // GROUP
    pad = ct[0].shape[0] - packs * f * rows
    extra = sum_rows(f)
    units = count if span <= 256 else 1
    at = start // units
    part = lambda *s: pl.BlockSpec((units,) + s, lambda b, *i: (b,) + (0,) * len(s))
    fixed = lambda *s: pl.BlockSpec(s, lambda b, *i: (0,) * len(s), pipeline_mode=pl.Buffered(1))
    column = lambda j: pl.BlockSpec((D, 3 * D), lambda b, *i: (0, j), pipeline_mode=pl.Buffered(1))
    sd = jax.ShapeDtypeStruct
    sum_out, sum_shape, sum_scratch = sum_specs(last_chunk, EARLY)
    if not last_chunk:
        sum_out, sum_scratch = [pl.BlockSpec(memory_space=pl.ANY)], [pltpu.VMEM((12, D, D), F32)]
    whole = pl.BlockSpec((units, f, rows, D), lambda b, *i: (b + at, 0, 0, 0))
    return pl.pallas_call(
        functools.partial(middle, n, f, start, not init, last_chunk, units == count),
        grid_spec=pltpu.PrefetchScalarGridSpec(
            num_scalar_prefetch=2,
            grid=(count // units,),
            in_specs=[part(f, rows, D)] * n
            + [pl.BlockSpec((units * f * rows, D), lambda b, *i: (b + at, 0))] * n
            + [pl.BlockSpec((pad, D), lambda b, *i: (packs * f * rows // pad, 0))] * n
            + [column(1), column(2), fixed(3 * D, D), fixed(D, 3 * D)]
            + [fixed(D, D), fixed(D, MLP), fixed(MLP, D)]
            + [pl.BlockSpec(memory_space=pl.ANY)] * len(init),
            out_specs=[part(f * rows + extra, D)] * n + [whole] * n + sum_out,
            scratch_shapes=[
                pltpu.VMEM((n * pad, 6 * D), F32),
                pltpu.VMEM((units, n, extra, D), F32),
                pltpu.VMEM((units, 3 * D, tokens), BF16),
                pltpu.VMEM((units, groups * HEADS // 2, span, 2 * span), F32),
                pltpu.VMEM((units, D, tokens), BF16),
                pltpu.VMEM((units, tokens, MLP), BF16),
                pltpu.VMEM((units, tokens, MLP), BF16),
                pltpu.VMEM((units, 3 * D, tokens), BF16),
                pltpu.SemaphoreType.DMA,
            ]
            + sum_scratch,
        ),
        out_shape=[sd((count, f * rows + extra, D), BF16)] * n
        + [sd((packs, f, rows, D), BF16)] * n
        + sum_shape,
        input_output_aliases={2 + 3 * n + 8 + j: n + j for j in range(n)} if init else {},
        compiler_params=pltpu.CompilerParams(vmem_limit_bytes=VMEM),
        cost_estimate=cost(14 * count),
        name="middle",
    )(idx, seg, *a1, *ct, *ct, ada, ada, tq_t, tq, to, up, down, *init)


def spatial_bwd(n, first_chunk, last_chunk, idx, tok, cot, mod, qkv, mix, br, tot, wo, *rest):
    rest = list(rest)
    take = lambda c: [rest.pop(0) for _ in range(c)]
    if not first_chunk:
        init = take(1)[0]
    dl = take(n)
    dqkv_o, ga_o, gm_o, *sums = take(3 + (2 if last_chunk else 1))
    scr = rest.pop(0)
    acc = rest.pop() if last_chunk else sums[0]
    b = pl.program_id(0)

    @pl.when(b == 0)
    def _():
        acc[...] = jnp.zeros_like(acc) if first_chunk else init[...]
        gm_o[...] = jnp.zeros_like(gm_o)

    frames = tok.shape[1]
    rows = tok.shape[2] // n
    i = idx[0]
    total = sum(d[0, frames * rows :].astype(F32) for d in dl)
    gms = []
    for f in range(frames):
        for k in range(n):
            scr[pl.ds(pl.multiple_of((i ^ k) * rows, GROUP), rows), :] = dl[k][0, f * rows : (f + 1) * rows]
        ga = cot[0, f].astype(F32) + scr[...].astype(F32)
        ga_o[0, f] = ga
        gm_o[0, f * 7 : f * 7 + 1] = jnp.sum(ga * br[0, f].astype(F32), axis=0, keepdims=True)
        gm_o[0, f * 7 + 1 : f * 7 + 7] = total[f * 6 : f * 6 + 6]
        gb = (mod[0, f, 2:3] * ga).astype(BF16)
        acc[3] += nn(mix[0, f], gb)
        gms.append(nt(wo[...], gb).astype(BF16))

    def products(j, f):
        a = j * 2 * HD
        q = on_diagonal(qkv[0, f, a : a + 2 * HD] * BF16(0.125))
        go = on_diagonal(gms[f][a : a + 2 * HD])
        s = nn(qkv[0, f, D + a : D + a + 2 * HD].T, q)
        return s, nn(qkv[0, f, 2 * D + a : 2 * D + a + 2 * HD].T, go)

    def weights(j, f, s, dp):
        p = jnp.exp(s - tot[0, f, j : j + 1])
        ds = (p * (dp - jnp.sum(p * dp, axis=0, keepdims=True))).astype(BF16)
        return p.astype(BF16), ds

    def grads(j, f, p, ds):
        cut = p.shape[1] // 2
        for e in range(2):
            cols = slice(e * cut, (e + 1) * cut)
            at = j * 2 * HD + e * HD
            q = qkv[0, f, at : at + HD] * BF16(0.125)
            k = qkv[0, f, D + at : D + at + HD]
            dqkv_o[0, f, 2 * D + at : 2 * D + at + HD] = nt(gms[f][at : at + HD], p[:, cols]).astype(BF16)
            dqkv_o[0, f, D + at : D + at + HD] = nt(q, ds[:, cols]).astype(BF16)
            dqkv_o[0, f, at : at + HD] = (nn(k, ds[:, cols]) * 0.125).astype(BF16)

    pipelined([(j, f) for j in range(HEADS // 2) for f in range(frames)], [products, weights, grads], 1)
    for f in range(frames):
        nrm, _ = norm_stats(tok[0, f].astype(F32))
        first = (nrm * (1.0 + mod[0, f, 1:2]) + mod[0, f, 0:1]).astype(BF16)
        value = nt(first.T, dqkv_o[0, f])
        for j in range(3):
            acc[j] += value[:, j * D : (j + 1) * D]
    if last_chunk:

        @pl.when(b == pl.num_programs(0) - 1)
        def _():
            divide(i & 1, acc, sums[0], sums[1], LATE)


def call_spatial_bwd(idx, tok, cot, mod, qkv, mix, br, tot, wo, init, dl, start, last_chunk):
    n = len(dl)
    count = dl[0].shape[0]
    f, p = tok.shape[1:3]
    whole = lambda *s: pl.BlockSpec((1, f) + s, lambda b, i: (b + start, 0) + (0,) * len(s))
    part = lambda *s: pl.BlockSpec((1, f) + s, lambda b, i: (b, 0) + (0,) * len(s))
    pack = lambda *s: pl.BlockSpec((1,) + s, lambda b, i: (b,) + (0,) * len(s))
    fixed = lambda *s: pl.BlockSpec(s, lambda b, i: (0,) * len(s), pipeline_mode=pl.Buffered(1))
    sd = lambda s, d: jax.ShapeDtypeStruct((count,) + s, d)
    sum_out, sum_shape, sum_scratch = sum_specs(last_chunk, LATE)
    gm_rows = -(-7 * f // 8) * 8
    return pl.pallas_call(
        functools.partial(spatial_bwd, n, not init, last_chunk),
        grid_spec=pltpu.PrefetchScalarGridSpec(
            num_scalar_prefetch=1,
            grid=(count,),
            in_specs=[whole(p, D), whole(p, D), part(3, D), part(3 * D, p), part(D, p)]
            + [part(p, D), part(HEADS // 2, 2 * p), fixed(D, D)]
            + [fixed(4, D, D)] * len(init)
            + [pack(*dl[0].shape[1:])] * n,
            out_specs=[part(3 * D, p), part(p, D), pack(gm_rows, D)] + sum_out,
            scratch_shapes=[pltpu.VMEM((p, D), BF16)] + sum_scratch,
        ),
        out_shape=[sd((f, 3 * D, p), BF16), sd((f, p, D), F32), sd((gm_rows, D), F32)] + sum_shape,
        compiler_params=pltpu.CompilerParams(vmem_limit_bytes=VMEM),
        cost_estimate=cost(5 * count),
        name="spatial_bwd",
    )(idx, tok, cot, mod, qkv, mix, br, tot, wo, *init, *dl)


def last_step(n, start, last_chunk, idx, tok, mod, w, dqkv, ga, *rest):
    rest = list(rest)
    take = lambda c: [rest.pop(0) for _ in range(c)]
    pieces = take(n)
    rows = pieces[0].shape[2]
    frames = tok.shape[1]
    b = pl.program_id(0)
    i = idx[0]
    if last_chunk:
        cond = take(1)[0]
        gates = take(start // pl.num_programs(0) + 1)
        norms = take(len(gates) - 1)
        take(2)
        grad_o, out_o, gs_o, all_s = rest
        count = gates[0].shape[0]

        @pl.when(b == 0)
        def _():
            all_s[:, 9 * D :] = cond[...].astype(F32)
            for c, gate in enumerate(gates):
                for p in range(count):
                    for f in range(frames):
                        at = (c * count + p) * frames + f
                        for j in range(7):
                            all_s[at : at + 1, (2 + j) * D : (3 + j) * D] = gate[p, f * 7 + j : f * 7 + j + 1]
                        if c < len(norms):
                            for j in range(2):
                                all_s[at : at + 1, j * D : (j + 1) * D] = norms[c][p, f * 2 + j : f * 2 + j + 1]

    else:
        grad_o, out_o, gs_o = rest
        gs_o[...] = jnp.zeros_like(gs_o)

    def product(f):
        for k, piece in enumerate(pieces):
            out_o[0, f, pl.ds(pl.multiple_of((i ^ k) * rows, GROUP), rows), :] = piece[0, f]
        return (nt(dqkv[0, f].T, w[...]),)

    def finish(f, g):
        nrm, r = norm_stats(tok[0, f].astype(F32))
        for j, v in enumerate((g, g * nrm)):
            total = jnp.sum(v, axis=0, keepdims=True)
            if last_chunk:
                all_s[pl.ds((start + b) * frames + f, 1), j * D : (j + 1) * D] = total
            else:
                gs_o[0, f * 2 + j : f * 2 + j + 1] = total
        grad_o[0, f] = ga[0, f] + norm_back(g * (1.0 + mod[0, f, 1:2]), nrm, r)

    pipelined([(f,) for f in range(frames)], [product, finish], 1)
    if last_chunk:

        @pl.when(b == pl.num_programs(0) - 1)
        def _():
            gs_o[...] = all_s[...].astype(BF16)


def call_last(idx, tok, mod, w, dqkv, ga, ou, start, more, held):
    n = len(ou)
    count, f = dqkv.shape[:2]
    rows = ou[0].shape[2]
    packs, _, p = tok.shape[:3]
    gs_rows = -(-2 * f // 8) * 8
    whole = lambda *s: pl.BlockSpec((1, f) + s, lambda b, i: (b + start, 0) + (0,) * len(s))
    part = lambda *s: pl.BlockSpec((1, f) + s, lambda b, i: (b, 0) + (0,) * len(s))
    fixed = lambda *s: pl.BlockSpec(s, lambda b, i: (0,) * len(s), pipeline_mode=pl.Buffered(1))
    sd = jax.ShapeDtypeStruct
    more = more or []
    sums = sd((packs * f, 10 * D), BF16) if more else sd((count, gs_rows, D), F32)
    return pl.pallas_call(
        functools.partial(last_step, n, start, bool(more)),
        grid_spec=pltpu.PrefetchScalarGridSpec(
            num_scalar_prefetch=1,
            grid=(count,),
            in_specs=[whole(p, D), part(3, D), fixed(D, 3 * D), part(3 * D, p), part(p, D)]
            + [whole(rows, D)] * n
            + [fixed(*m.shape) for m in more]
            + [pl.BlockSpec(memory_space=pl.ANY)] * len(held),
            out_specs=[whole(p, D), whole(p, D)]
            + [
                pl.BlockSpec(sums.shape, lambda b, i: (0, 0))
                if more
                else pl.BlockSpec((1, gs_rows, D), lambda b, i: (b, 0, 0))
            ],
            scratch_shapes=[pltpu.VMEM(sums.shape, F32)] if more else [],
        ),
        out_shape=[sd(tok.shape, F32), sd(tok.shape, BF16), sums],
        input_output_aliases={6 + n + len(more) + j: j for j in range(len(held))},
        compiler_params=pltpu.CompilerParams(vmem_limit_bytes=VMEM),
        cost_estimate=cost(3 * count),
        name="last_step",
    )(idx, tok, mod, w, dqkv, ga, *ou, *more, *held)


def finish_early(idx, data, *refs):
    up_o, down_o, qkv_o, out_o = refs[-4:]
    half = D // 2
    for j in range(4):
        cols = slice(j * D, (j + 1) * D)
        up_o[:, cols] = data[j * half : (j + 1) * half].astype(F32)
        if j < 3:
            qkv_o[:, cols] = data[4 * D + j * half : 4 * D + (j + 1) * half].astype(F32)
    out_o[...] = data[4 * D + 3 * half :].astype(F32)
    for j in range(2):
        down_o[j * D : (j + 1) * D] = data[2 * D + j * D : 2 * D + (j + 1) * D].T.astype(F32)


def finish_late(idx, data, *refs):
    qkv_o, out_o = refs[-2:]
    half = D // 2
    for j in range(3):
        qkv_o[:, j * D : (j + 1) * D] = data[j * half : (j + 1) * half].astype(F32)
    out_o[...] = data[3 * half :].astype(F32)


def call_finish(kernel, shapes, idx, data, flip, held):
    spec = lambda s: pl.BlockSpec((s[0] // 2, s[1]), lambda j, i: ((i[0] & 1) ^ flip, 0))
    return pl.pallas_call(
        kernel,
        grid_spec=pltpu.PrefetchScalarGridSpec(
            num_scalar_prefetch=1,
            grid=(1,),
            in_specs=[pl.BlockSpec(data.shape, lambda j, i: (0, 0))]
            + [pl.BlockSpec(memory_space=pl.ANY)] * len(held),
            out_specs=[spec(s) for s in shapes],
        ),
        out_shape=[jax.ShapeDtypeStruct(s, F32) for s in shapes],
        input_output_aliases={2 + j: j for j in range(len(held))},
        compiler_params=pltpu.CompilerParams(vmem_limit_bytes=VMEM),
        cost_estimate=cost(2),
        name=kernel.__name__,
    )(idx, data, *held)


def ada_grad(turn, idx, own_act, other_act, own, other, out, act):
    first = (idx[0] & 1) == 0
    size = own.shape[0] // len(turn)
    block = lambda v, j: v[j * size : (j + 1) * size]

    def join(a, b):
        zero = [jnp.where(first, block(a, j), block(b, j)) for j in range(len(turn))]
        one = [jnp.where(first, block(b, j), block(a, j)) for j in turn]
        return jnp.concatenate(zero + one, axis=0)

    @pl.when(pl.program_id(0) == 0)
    def _():
        act[...] = silu_low(join(own_act, other_act)).T

    out[...] = nn(act[...], join(own, other))


def call_ada_grad(turn, idx, own, other):
    step = 3 * D
    act = pl.BlockSpec((own.shape[0], D), lambda j, i: (0, 9))
    mod = pl.BlockSpec((own.shape[0], step), lambda j, i: (0, j))
    return pl.pallas_call(
        functools.partial(ada_grad, turn),
        grid_spec=pltpu.PrefetchScalarGridSpec(
            num_scalar_prefetch=1,
            grid=(3,),
            in_specs=[act, act, mod, mod],
            out_specs=pl.BlockSpec((D, step), lambda j, i: (0, j)),
            scratch_shapes=[pltpu.VMEM((D, 2 * own.shape[0]), BF16)],
        ),
        out_shape=jax.ShapeDtypeStruct((D, 9 * D), F32),
        compiler_params=pltpu.CompilerParams(vmem_limit_bytes=VMEM),
        cost_estimate=cost(3),
        name="ada_grad",
    )(idx, own, other, own, other)


def swap(x, axis, mask):
    size = lax.axis_size(axis)
    return lax.ppermute(x, axis, [(s, s ^ mask) for s in range(size)])


def bits_of(axis):
    return [(axis, b) for b in range(lax.axis_size(axis).bit_length() - 1)]


def bit_of(axis, b):
    return (lax.axis_index(axis) >> b) & 1


def orders():
    pack, frame = bits_of("pack"), bits_of("frame")[1:]
    path = pack[:2]
    pack = pack[2:]
    while pack or frame:
        path += frame[:1] + pack[:1]
        pack, frame = pack[1:], frame[1:]
    turned = []
    for j in range(0, len(path), 2):
        turned += path[j : j + 2][::-1]
    return path, turned


def swap_by_core(x, step):
    nf, npk = lax.axis_size("frame"), lax.axis_size("pack")
    perm = []
    for pack in range(npk):
        for frame in range(nf):
            axis, b = step[frame & 1]
            to = (pack ^ (1 << b), frame) if axis == "pack" else (pack, frame ^ (1 << b))
            perm.append((frame * npk + pack, to[1] * npk + to[0]))
    return lax.ppermute(x, ("frame", "pack"), perm)


def bit_by_core(step):
    core = bit_of("frame", 0)
    return jnp.where(core == 0, bit_of(*step[0]), bit_of(*step[1]))


def doubled(g, other, mine):
    first = jnp.arange(2).reshape(2, 1, 1) == mine.astype(jnp.int32)
    return jnp.where(first, g[None], other[None]).reshape(-1, g.shape[1])


def tie_all(values, *deps):
    return list(lax.optimization_barrier((*values, *deps))[: len(values)])


def tie(value, *deps):
    return lax.optimization_barrier((value, *deps))[0]


class Order:
    def __init__(self):
        self.last = []

    def start(self, x):
        return tie(x, *self.last) if self.last else x

    def waited(self, x):
        self.last = [x]
        return x


class Gathering:
    def __init__(self, rows, steps):
        self.rows = rows
        self.steps = steps

    def start(self, step):
        self.moving = swap_by_core(self.rows, step)

    def end(self, step, after):
        self.rows = doubled(self.rows, tie(self.moving, after), bit_by_core(step))

    def sort(self, turn):
        size = self.rows.shape[0] // len(turn)
        turned = jnp.concatenate([self.rows[j * size : (j + 1) * size] for j in turn], axis=0)
        self.rows = jnp.where(bit_of("frame", 0) == 0, self.rows, turned)


def turned_blocks(steps):
    turn = []
    for j in range(1 << len(steps)):
        at = {s[0]: (j >> b) & 1 for b, s in enumerate(steps)}
        turn.append(sum(at[s[1]] << b for b, s in enumerate(steps)))
    return turn


class Summing:
    def __init__(self, order, send, keep, halvings):
        self.order = order
        self.keep = keep
        self.steps = list(zip(*orders()))
        self.halvings = halvings
        self.at = 0
        self.back = []
        self.beside = self.beside_step = None
        self.moving = swap(order.start(send), "frame", 1)

    def advance(self, after=None):
        moving = self.moving if after is None else tie(self.moving, after)
        moving = self.order.waited(moving)
        keep = self.keep
        if self.beside and self.beside_step:
            self.beside.end(self.beside_step, moving)
            if self.at == len(self.steps):
                self.beside.sort(turned_blocks(self.steps[self.halvings :]))
        total = lambda a, b: (a.astype(F32) + b.astype(F32)).astype(BF16)
        if self.at < len(self.steps):
            step = self.steps[self.at]
            if self.at < self.halvings:
                mine = bit_by_core(step)
                half = keep.shape[0] // 2
                part = lambda v, m: lax.dynamic_slice_in_dim(v, m * half, half, 0)
                send = total(part(keep, 1 - mine), part(moving, 1 - mine))
                self.keep = total(part(keep, mine), part(moving, mine))
                self.back.append(step)
            else:
                send = self.keep = total(keep, moving)
        else:
            if self.at == len(self.steps):
                self.keep = total(keep, moving)
            else:
                self.keep = doubled(keep, moving, bit_by_core(self.back.pop()))
            send = self.keep
            step = self.back[-1] if self.back else None
        self.at += 1
        send = self.order.start(send)
        self.sent = send
        if step is None:
            self.other = swap(send, "frame", 1)
            if self.beside:
                self.beside.other = swap(self.beside.rows, "frame", 1)
            return False
        self.moving = swap_by_core(send, step)
        if self.beside and self.at > self.halvings:
            self.beside.start(step)
            self.beside_step = step
        return True


def local(
    tokens,
    condition,
    clip_lengths,
    ada_weight,
    spatial_qkv,
    spatial_out,
    temporal_qkv,
    temporal_out,
    mlp_up,
    mlp_down,
    cotangent,
):
    n = lax.axis_size("frame")
    i = lax.axis_index("frame")
    idx = i.reshape(1).astype(jnp.int32)
    packs, f, patches = tokens.shape[:3]
    rows = patches // n
    count = packs // CHUNKS
    top = n // 2
    send = lambda parts: [parts[0]] + [swap(parts[k], "frame", k) for k in range(1, n)]

    own_cond = condition.reshape(packs * f, D)
    pad = -(-packs * f // GROUP) * GROUP
    cond_rows = jnp.concatenate([own_cond, jnp.zeros((pad - packs * f, D), BF16)], axis=0)

    def cut(k):
        v = lax.dynamic_slice_in_dim(cotangent, (i ^ k) * rows, rows, 2)
        return jnp.concatenate([v.reshape(-1, D), cond_rows], axis=0)

    ct = send([cut(k) for k in range(n)])
    sq_t = spatial_qkv.T
    tq_t = temporal_qkv.T
    frame_ids = jnp.concatenate([(i ^ k) * f + jnp.arange(f, dtype=jnp.int32) for k in range(n)])
    ends = [jnp.sum(clip_lengths[:, : j + 1], axis=1) for j in range(clip_lengths.shape[1])]
    segment = sum((e[:, None] <= frame_ids[None, :]).astype(jnp.int32) for e in ends)

    fwd = []
    source = tokens
    for c in range(CHUNKS):
        res = call_spatial_fwd(idx, source, condition, ada_weight, sq_t, spatial_out, c * count, count, n)
        slots = list(res[5:])
        if c:
            slots = tie_all(slots, *fwd[-1][1][1:])
        fwd.append((res[:5], send(slots)))
        if c == 0:
            source = tie(tokens, segment, tq_t, *ct[1:-1])

    init, mids = [], []
    for c in range(CHUNKS):
        last = c == CHUNKS - 1
        res = call_middle(
            idx, segment, fwd[c][1], ct, ada_weight, tq_t, temporal_qkv, temporal_out, mlp_up, mlp_down,
            init, c * count, last, packs,
        )
        init = [res[2 * n], *res[n : 2 * n]]
        res = list(res)
        if c:
            res = tie_all(res, *mids[-1][1:])
        mids.append(send(res[:n]))
    order = Order()
    early = Summing(order, res[2 * n], res[2 * n + 1], 3)
    outs = res[n : 2 * n]
    outs[top] = swap(outs[top], "frame", top)

    acc, backs = [], []
    for c in range(CHUNKS):
        last = c == CHUNKS - 1
        qkv, mix, br, tot, mod = fwd[c][0]
        dl = mids[c]
        if c:
            early.advance(after=backs[-1][2])
            dl = tie_all(dl, early.sent)
            for k in range(1, n):
                if k != top:
                    outs[k] = swap(tie(outs[k], early.sent), "frame", k)
        res = call_spatial_bwd(
            idx, tokens, cotangent, mod, qkv, mix, br, tot, spatial_out, acc, dl, c * count, last
        )
        acc = list(res[3:])
        backs.append(res)
    early.advance(after=backs[-1][2])
    late = Summing(order, acc[0], acc[1], 2)
    lasts, held = [], []
    for c in range(CHUNKS):
        last = c == CHUNKS - 1
        dqkv, ga = backs[c][:2]
        if c:
            early.advance(after=lasts[-1][2])
            late.advance(after=lasts[-1][2])
        ga = tie(ga, early.sent, late.moving if c == 0 else late.sent) if c else tie(ga, early.sent)
        more = [own_cond, *[b[2] for b in backs], *[v[2] for v in lasts]] if last else None
        res = call_last(idx, tokens, fwd[c][0][4], spatial_qkv, dqkv, ga, outs, c * count, more, held)
        held = list(res[:2])
        lasts.append(res)
    grad_tokens, output = held
    rows_of = lasts[-1][2]
    early.advance(after=rows_of)
    late.advance(after=rows_of)
    gather = late.beside = Gathering(rows_of, late.steps)
    live = {"late": late, "early": early}
    skipped = False
    while live:
        for name in list(live):
            if name == "early" and len(early.back) == 0 and not skipped:
                skipped = True
            elif not live[name].advance():
                del live[name]
    own = rows_of[:, : 9 * D]
    back = jnp.einsum("tj,ij->ti", own, ada_weight, preferred_element_type=F32).reshape(packs, f, D)
    cf = condition.astype(F32)
    sig = 1.0 / (1.0 + jnp.exp(-cf))
    grad_condition = back * (sig * (1.0 + cf * (1.0 - sig)))

    early_shapes = [(D, MLP), (MLP, D), (D, 3 * D), (D, D)]
    late_shapes = [(D, 3 * D), (D, D)]
    half = call_finish(finish_early, early_shapes, idx, early.keep, 0, [])
    late_half = call_finish(finish_late, late_shapes, idx, tie(late.keep, half[3]), 0, [])
    turn = turned_blocks(late.steps[: late.halvings][::-1])
    grad_ada = call_ada_grad(turn, idx, gather.rows, tie(gather.other, late_half[1]))
    late_other = tie(late.other, grad_ada)
    s_qkv, s_out = call_finish(finish_late, late_shapes, idx, late_other, 1, list(late_half))
    early_other = tie(early.other, s_out)
    up, down, t_qkv, t_out = call_finish(finish_early, early_shapes, idx, early_other, 1, list(half))
    return (output, grad_tokens, grad_condition, grad_ada, s_qkv, s_out, t_qkv, t_out, up, down)


def solution(mesh):
    tok = P("pack", "frame", None, None)
    cond = P("pack", "frame", None)
    return jax.shard_map(
        local,
        mesh=mesh,
        in_specs=(tok, cond, P("pack", None), P(), P(), P(), P(), P(), P(), P(), tok),
        out_specs=(tok, tok, cond, P(), P(), P(), P(), P(), P(), P()),
        check_vma=False,
    )
```

```python
import functools

import jax
import jax.numpy as jnp
from jax import lax
from jax.experimental import pallas as pl
from jax.experimental.pallas import tpu as pltpu
from jax.sharding import PartitionSpec as P

D = 384
HEADS = 6
HD = 64
MLP = 1536
F32 = jnp.float32
BF16 = jnp.bfloat16
CHUNKS = 2
GROUP = 16
VMEM = 58 * 2**20


def nn(a, b):
    return lax.dot_general(a, b, (((1,), (0,)), ((), ())), preferred_element_type=F32)


def nt(a, b):
    return lax.dot_general(a, b, (((1,), (1,)), ((), ())), preferred_element_type=F32)


def tn(a, b):
    return lax.dot_general(a, b, (((0,), (0,)), ((), ())), preferred_element_type=F32)


def cost(us):
    return pl.CostEstimate(flops=int(us * 1.0e10), bytes_accessed=1000, transcendentals=0)


def silu_low(v):
    v = v.astype(F32)
    return (v / (1.0 + jnp.exp(-v))).astype(BF16)


def on_diagonal(pair):
    none = jnp.zeros_like(pair[:HD])
    return jnp.concatenate(
        [
            jnp.concatenate([pair[:HD], none], axis=1),
            jnp.concatenate([none, pair[HD:]], axis=1),
        ],
        axis=0,
    )


def norm_stats(x):
    c = x - jnp.mean(x, -1, keepdims=True)
    r = lax.rsqrt(jnp.mean(c * c, -1, keepdims=True) + 1e-6)
    return c * r, r


def norm_back(h, n, r):
    return r * (h - jnp.mean(h, -1, keepdims=True) - n * jnp.mean(h * n, -1, keepdims=True))


def pipelined(items, stages, ahead=1):
    held = [[] for _ in stages]
    last = len(stages) - 1
    for t in range(len(items) + ahead * last):
        for s, stage in enumerate(stages):
            at = t - s * ahead
            if 0 <= at < len(items):
                value = stage(*items[at], *(held[s - 1].pop(0) if s else ()))
                if s < last:
                    held[s].append(value)


def spatial_fwd(start, idx, tok, cond, ada, w_t, wo, qkv_o, mix_o, br_o, tot_o, mod_o, *rest):
    slots, (scr, mod_s) = rest[:-2], rest[-2:]
    rows = slots[0].shape[2]
    frames = tok.shape[1]
    b = pl.program_id(0)

    @pl.when(b == 0)
    def _():
        mod_s[...] = nn(silu_low(cond[...]), ada[...])

    i = idx[0]
    mds = []
    for f in range(frames):
        at = (b + start) * frames + f
        md = [mod_s[pl.ds(at, 1), j * D : (j + 1) * D] for j in range(3)]
        for j in range(3):
            mod_o[0, f, j : j + 1] = md[j]
        n, _ = norm_stats(tok[0, f].astype(F32))
        first = (n * (1.0 + md[1]) + md[0]).astype(BF16)
        qkv_o[0, f] = nt(w_t[...], first).astype(BF16)
        mds.append(md)

    def scores(j, f):
        a = j * 2 * HD
        q = on_diagonal(qkv_o[0, f, a : a + 2 * HD] * BF16(0.125))
        k = qkv_o[0, f, D + a : D + a + 2 * HD]
        return (nn(k.T, q),)

    def mix(j, f, s):
        a = j * 2 * HD
        mx = jnp.max(s, axis=0, keepdims=True)
        p = jnp.exp(s - mx)
        total = jnp.sum(p, axis=0, keepdims=True)
        tot_o[0, f, j : j + 1] = mx + jnp.log(total)
        p = p.astype(BF16)
        scale = 1.0 / total
        cut = p.shape[1] // 2
        for e in range(2):
            v = qkv_o[0, f, 2 * D + a + e * HD : 2 * D + a + (e + 1) * HD]
            cols = slice(e * cut, (e + 1) * cut)
            mix_o[0, f, a + e * HD : a + (e + 1) * HD] = (nn(v, p[:, cols]) * scale[:, cols]).astype(BF16)

    pipelined([(j, f) for j in range(HEADS // 2) for f in range(frames)], [scores, mix], 2)
    for f in range(frames):
        br = tn(mix_o[0, f], wo[...])
        br_o[0, f] = br.astype(BF16)
        scr[f] = (tok[0, f].astype(F32) + mds[f][2] * br).astype(BF16)
        for k, slot in enumerate(slots):
            slot[0, f] = scr[f, pl.ds(pl.multiple_of((i ^ k) * rows, GROUP), rows), :]


def call_spatial_fwd(idx, tok, cond, ada, w_t, wo, start, count, n):
    f = tok.shape[1]
    p = tok.shape[2]
    whole = lambda *s: pl.BlockSpec((1, f) + s, lambda b, i: (b + start, 0) + (0,) * len(s))
    part = lambda *s: pl.BlockSpec((1, f) + s, lambda b, i: (b, 0) + (0,) * len(s))
    fixed = lambda *s: pl.BlockSpec(s, lambda b, i: (0,) * len(s), pipeline_mode=pl.Buffered(1))
    sd = lambda s, d: jax.ShapeDtypeStruct((count, f) + s, d)
    own = tok.shape[0] * f
    return pl.pallas_call(
        functools.partial(spatial_fwd, start),
        grid_spec=pltpu.PrefetchScalarGridSpec(
            num_scalar_prefetch=1,
            grid=(count,),
            in_specs=[whole(p, D), fixed(own, D), fixed(D, 3 * D), fixed(3 * D, D), fixed(D, D)],
            out_specs=[part(3 * D, p), part(D, p), part(p, D), part(HEADS // 2, 2 * p), part(3, D)]
            + [part(p // n, D)] * n,
            scratch_shapes=[pltpu.VMEM((f, p, D), BF16), pltpu.VMEM((own, 3 * D), F32)],
        ),
        out_shape=[sd((3 * D, p), BF16), sd((D, p), BF16), sd((p, D), BF16)]
        + [sd((HEADS // 2, 2 * p), F32), sd((3, D), F32)]
        + [sd((p // n, D), BF16)] * n,
        compiler_params=pltpu.CompilerParams(vmem_limit_bytes=VMEM),
        cost_estimate=cost(4 * count),
        name="spatial_fwd",
    )(idx, tok, cond.reshape(-1, D), ada, w_t, wo)


def tile_places(n, f, rows):
    return [
        (k, j * rows + g * GROUP)
        for g in range(rows // GROUP)
        for k in range(n)
        for j in range(f)
    ]


def divide(mine, acc, sent, kept, kinds):
    at = 0
    base = 0
    for kind, blocks in kinds:
        for out, who in ((sent, 1 - mine), (kept, mine)):
            row = at
            if kind == "rows":
                half = D // 2
                for j in range(blocks):
                    part = acc[base + j, pl.ds(pl.multiple_of(who * half, GROUP), half), :]
                    out[row : row + half] = part.astype(BF16)
                    row += half
            else:
                for j in range(blocks // 2):
                    out[row : row + D] = acc[base + who * (blocks // 2) + j].astype(BF16)
                    row += D
        at = row
        base += blocks


EARLY = (("rows", 4), ("blocks", 4), ("rows", 4))
LATE = (("rows", 4),)


def sum_specs(last_chunk, kinds):
    const = lambda *s: pl.BlockSpec(s, lambda *g: (0,) * len(s))
    sd = jax.ShapeDtypeStruct
    blocks = sum(k[1] for k in kinds)
    if not last_chunk:
        return [const(blocks, D, D)], [sd((blocks, D, D), F32)], []
    half = (blocks * D // 2, D)
    return [const(*half)] * 2, [sd(half, BF16)] * 2, [pltpu.VMEM((blocks, D, D), F32)]


def middle(n, f, start, first_chunk, last_chunk, once, idx, seg, *refs):
    refs = list(refs)
    take = lambda c: [refs.pop(0) for _ in range(c)]
    a1, ct, conds = take(n), take(n), take(n)
    ada_a, ada_b, tq_t, tq, to, up, down = take(7)
    if not first_chunk:
        init = take(1 + n)[0]
    dl = take(n)
    ou = take(n)
    sums = take(2 if last_chunk else 1)
    acc, init_sem = refs.pop(), refs.pop()
    mod_s, sum_s, qkv_s, p_s, mix_s, dg_s, hid_s, dqkv_s = refs
    rows = a1[0].shape[2]
    groups = rows // GROUP
    frames = n * f
    span = frames * GROUP
    tokens = span * groups
    places = tile_places(n, f, rows)
    b = pl.program_id(0)
    fresh = first_chunk and once

    @pl.when(b == 0)
    def _():
        if not first_chunk:
            pltpu.make_async_copy(init, acc, init_sem).start()
        elif not fresh:
            acc[...] = jnp.zeros_like(acc)
        sum_s[...] = jnp.zeros_like(sum_s)
        act = silu_low(jnp.concatenate([c[...] for c in conds], axis=0))
        mod_s[:, : 3 * D] = nn(act, ada_a[...])
        mod_s[:, 3 * D :] = nn(act, ada_b[...])

    pad = conds[0].shape[0]
    units = a1[0].shape[0]

    def tile(u):
        pack = b * units + u

        def per_frame(piece, plus=0.0):
            cols = slice(piece * D, (piece + 1) * D)
            at = [k * pad + (pack + start) * f + j for k in range(n) for j in range(f)]
            rows_ = [mod_s[pl.ds(t, 1), cols] + plus for t in at]
            one = jnp.concatenate([jnp.broadcast_to(r, (GROUP, D)) for r in rows_], axis=0)
            return jnp.concatenate([one] * groups, axis=0)

        def frame_sum(piece, v):
            total = jnp.sum(jnp.sum(v.reshape(groups, frames, GROUP, D), axis=0), axis=1)
            for k in range(n):
                for j in range(f):
                    sum_s[u, k, j * 6 + piece : j * 6 + piece + 1] = total[k * f + j : k * f + j + 1]

        def add(base, col, value):
            for j in range(value.shape[1] // D):
                part = value[:, j * D : (j + 1) * D]
                at = base + col // D + j
                acc[at] = part if fresh and u == 0 else acc[at] + part

        x1 = jnp.concatenate(
            [a1[k][u, r // rows, r % rows : r % rows + GROUP] for k, r in places], axis=0
        ).astype(F32)
        n2, r2 = norm_stats(x1)
        second = (n2 * per_frame(1, 1.0) + per_frame(0)).astype(BF16)
        yield
        qkv_s[u] = nt(tq_t[...], second).astype(BF16)
        lane = lax.broadcasted_iota(jnp.int32, (span, span), 0) % GROUP
        other = lax.broadcasted_iota(jnp.int32, (span, span), 1) % GROUP
        segs = [seg[pack + start, t] for t in range(frames)]

        def segment_of(axis):
            at = lax.broadcasted_iota(jnp.int32, (span, span), axis) // GROUP
            value = jnp.zeros((span, span), jnp.int32)
            for t in range(frames):
                value = jnp.where(at == t, segs[t], value)
            return value

        allowed = (segment_of(0) == segment_of(1)) & (lane == other)
        bias = jnp.where(allowed, 0.0, -1e30)
        bias = jnp.concatenate([bias, bias], axis=1)
        items = [(g, j) for g in range(groups) for j in range(HEADS // 2)]

        def pair(ref, kind, g, j):
            a = kind * D + j * 2 * HD
            return ref[u, a : a + 2 * HD, g * span : (g + 1) * span]

        def scores(g, j):
            q = on_diagonal(pair(qkv_s, 0, g, j) * BF16(0.125))
            return (nn(pair(qkv_s, 1, g, j).T, q),)

        def mix(g, j, s):
            s = s + bias
            p = jnp.exp(s - jnp.max(s, axis=0, keepdims=True))
            p = p * (1.0 / jnp.sum(p, axis=0, keepdims=True))
            p_s[u, g * (HEADS // 2) + j] = p
            o = nn(pair(qkv_s, 2, g, j), p.astype(BF16)).astype(BF16)
            a, cols = j * 2 * HD, slice(g * span, (g + 1) * span)
            mix_s[u, a : a + HD, cols] = o[:HD, :span]
            mix_s[u, a + HD : a + 2 * HD, cols] = o[HD:, span:]

        pipelined(items, [scores, mix], 2 if span <= 256 else 0)
        yield
        br2 = tn(mix_s[u], to[...])
        x2 = x1 + per_frame(2) * br2
        n3, r3 = norm_stats(x2)
        third = (n3 * per_frame(4, 1.0) + per_frame(3)).astype(BF16)
        yield
        step = STEP
        br3 = []

        def mlp_in(c):
            return (nn(third, up[:, c : c + step]),)

        def mlp_out(c, pre):
            sq = pre * pre
            t = jnp.tanh(pre * (0.7978845608028654 + (0.7978845608028654 * 0.044715) * sq))
            half = 0.5 + 0.5 * t
            hid = (pre * half).astype(BF16)
            hid_s[u, :, c : c + step] = hid
            inner = 0.7978845608028654 + (3 * 0.7978845608028654 * 0.044715) * sq
            dg_s[u, :, c : c + step] = (half + 0.5 * pre * (1.0 - t * t) * inner).astype(BF16)
            br3[:] = [sum(br3, nn(hid, down[c : c + step, :]))]

        pipelined([(c,) for c in range(0, MLP, step)], [mlp_in, mlp_out], 1)
        br3 = br3[0]
        yield
        gate3 = per_frame(5)
        value = (x2 + gate3 * br3).astype(BF16)
        for t, (k, r) in enumerate(places):
            ou[k][u, r // rows, r % rows : r % rows + GROUP] = value[t * GROUP : (t + 1) * GROUP]
        cot = jnp.concatenate([ct[k][u * f * rows + r : u * f * rows + r + GROUP] for k, r in places], axis=0).astype(F32)
        frame_sum(5, cot * br3)
        gb3 = (gate3 * cot).astype(BF16)
        if not first_chunk and u == 0:

            @pl.when(b == 0)
            def _():
                pltpu.make_async_copy(init, acc, init_sem).wait()

        gb3_t = gb3.T
        third_t = third.T
        yield
        g3 = []

        def back_in(c):
            return (nt(gb3, down[c : c + step, :]),)

        def back_out(c, gh):
            gp = (gh * dg_s[u, :, c : c + step]).astype(BF16)
            add(4, c, nn(gb3_t, hid_s[u, :, c : c + step]))
            add(0, c, nn(third_t, gp))
            g3[:] = [sum(g3, nt(gp, up[:, c : c + step]))]

        pipelined([(c,) for c in range(0, MLP, step)], [back_in, back_out], 1)
        g3 = g3[0]
        yield
        frame_sum(3, g3)
        frame_sum(4, g3 * n3)
        dx3 = norm_back(g3 * per_frame(4, 1.0), n3, r3)
        ga2 = cot + dx3
        frame_sum(2, ga2 * br2)
        gb2 = (per_frame(2) * ga2).astype(BF16)
        add(11, 0, nn(mix_s[u], gb2))
        gm_t = nt(to[...], gb2).astype(BF16)
        yield

        def grads_in(g, j):
            go = on_diagonal(gm_t[j * 2 * HD : (j + 1) * 2 * HD, g * span : (g + 1) * span])
            return (go, nn(pair(qkv_s, 2, g, j).T, go))

        def grads_mid(g, j, go, dp):
            p = p_s[u, g * (HEADS // 2) + j]
            ds = (p * (dp - jnp.sum(p * dp, axis=0, keepdims=True))).astype(BF16)
            return (go, p.astype(BF16), ds)

        def grads_out(g, j, go, p, ds):
            a, cols = j * 2 * HD, slice(g * span, (g + 1) * span)
            q = on_diagonal(pair(qkv_s, 0, g, j) * BF16(0.125))
            dqkv_s[u, 2 * D + a : 2 * D + a + 2 * HD, cols] = nt(go, p).astype(BF16)
            dqkv_s[u, D + a : D + a + 2 * HD, cols] = nt(q, ds).astype(BF16)
            dq = (nn(pair(qkv_s, 1, g, j), ds) * 0.125).astype(BF16)
            dqkv_s[u, a : a + HD, cols] = dq[:HD, :span]
            dqkv_s[u, a + HD : a + 2 * HD, cols] = dq[HD:, span:]

        pipelined(items, [grads_in, grads_mid, grads_out], 1 if span <= 256 else 0)
        yield
        dqkv = dqkv_s[u]
        add(8, 0, nt(second.T, dqkv))
        g2 = nn(tq[...], dqkv).T
        yield
        frame_sum(0, g2)
        frame_sum(1, g2 * n2)
        dx2 = norm_back(g2 * per_frame(1, 1.0), n2, r2)
        value = (dx3 + dx2).astype(BF16)
        for t, (k, r) in enumerate(places):
            dl[k][u, r : r + GROUP] = value[t * GROUP : (t + 1) * GROUP]
        for k in range(n):
            dl[k][u, f * rows :] = sum_s[u, k].astype(BF16)

    tiles = [tile(u) for u in range(units)]
    turn = 0
    while tiles:
        for t in list(tiles[: turn + 1]):
            if next(t, True):
                tiles.remove(t)
                turn -= 1
        turn += 1
    if last_chunk:

        @pl.when(b == pl.num_programs(0) - 1)
        def _():
            divide(idx[0] & 1, acc, sums[0], sums[1], EARLY)

    else:

        @pl.when(b == pl.num_programs(0) - 1)
        def _():
            copy = pltpu.make_async_copy(acc, sums[0], init_sem)
            copy.start()
            copy.wait()


STEP = 2 * D


def sum_rows(f):
    return -(-6 * f // GROUP) * GROUP


def call_middle(idx, seg, a1, ct, ada, tq_t, tq, to, up, down, init, start, last_chunk, packs):
    n = len(a1)
    count, f, rows = a1[0].shape[:3]
    frames = n * f
    span = frames * GROUP
    tokens = frames * rows
    groups = rows // GROUP
    pad = ct[0].shape[0] - packs * f * rows
    extra = sum_rows(f)
    units = count if span <= 256 else 1
    at = start // units
    part = lambda *s: pl.BlockSpec((units,) + s, lambda b, *i: (b,) + (0,) * len(s))
    fixed = lambda *s: pl.BlockSpec(s, lambda b, *i: (0,) * len(s), pipeline_mode=pl.Buffered(1))
    column = lambda j: pl.BlockSpec((D, 3 * D), lambda b, *i: (0, j), pipeline_mode=pl.Buffered(1))
    sd = jax.ShapeDtypeStruct
    sum_out, sum_shape, sum_scratch = sum_specs(last_chunk, EARLY)
    if not last_chunk:
        sum_out, sum_scratch = [pl.BlockSpec(memory_space=pl.ANY)], [pltpu.VMEM((12, D, D), F32)]
    whole = pl.BlockSpec((units, f, rows, D), lambda b, *i: (b + at, 0, 0, 0))
    return pl.pallas_call(
        functools.partial(middle, n, f, start, not init, last_chunk, units == count),
        grid_spec=pltpu.PrefetchScalarGridSpec(
            num_scalar_prefetch=2,
            grid=(count // units,),
            in_specs=[part(f, rows, D)] * n
            + [pl.BlockSpec((units * f * rows, D), lambda b, *i: (b + at, 0))] * n
            + [pl.BlockSpec((pad, D), lambda b, *i: (packs * f * rows // pad, 0))] * n
            + [column(1), column(2), fixed(3 * D, D), fixed(D, 3 * D)]
            + [fixed(D, D), fixed(D, MLP), fixed(MLP, D)]
            + [pl.BlockSpec(memory_space=pl.ANY)] * len(init),
            out_specs=[part(f * rows + extra, D)] * n + [whole] * n + sum_out,
            scratch_shapes=[
                pltpu.VMEM((n * pad, 6 * D), F32),
                pltpu.VMEM((units, n, extra, D), F32),
                pltpu.VMEM((units, 3 * D, tokens), BF16),
                pltpu.VMEM((units, groups * HEADS // 2, span, 2 * span), F32),
                pltpu.VMEM((units, D, tokens), BF16),
                pltpu.VMEM((units, tokens, MLP), BF16),
                pltpu.VMEM((units, tokens, MLP), BF16),
                pltpu.VMEM((units, 3 * D, tokens), BF16),
                pltpu.SemaphoreType.DMA,
            ]
            + sum_scratch,
        ),
        out_shape=[sd((count, f * rows + extra, D), BF16)] * n
        + [sd((packs, f, rows, D), BF16)] * n
        + sum_shape,
        input_output_aliases={2 + 3 * n + 8 + j: n + j for j in range(n)} if init else {},
        compiler_params=pltpu.CompilerParams(vmem_limit_bytes=VMEM),
        cost_estimate=cost(14 * count),
        name="middle",
    )(idx, seg, *a1, *ct, *ct, ada, ada, tq_t, tq, to, up, down, *init)


def spatial_bwd(n, first_chunk, last_chunk, idx, tok, cot, mod, qkv, mix, br, tot, wo, *rest):
    rest = list(rest)
    take = lambda c: [rest.pop(0) for _ in range(c)]
    if not first_chunk:
        init = take(1)[0]
    dl = take(n)
    dqkv_o, ga_o, gm_o, *sums = take(3 + (2 if last_chunk else 1))
    scr = rest.pop(0)
    acc = rest.pop() if last_chunk else sums[0]
    b = pl.program_id(0)

    @pl.when(b == 0)
    def _():
        acc[...] = jnp.zeros_like(acc) if first_chunk else init[...]
        gm_o[...] = jnp.zeros_like(gm_o)

    frames = tok.shape[1]
    rows = tok.shape[2] // n
    i = idx[0]
    total = sum(d[0, frames * rows :].astype(F32) for d in dl)
    gms = []
    for f in range(frames):
        for k in range(n):
            scr[pl.ds(pl.multiple_of((i ^ k) * rows, GROUP), rows), :] = dl[k][0, f * rows : (f + 1) * rows]
        ga = cot[0, f].astype(F32) + scr[...].astype(F32)
        ga_o[0, f] = ga
        gm_o[0, f * 7 : f * 7 + 1] = jnp.sum(ga * br[0, f].astype(F32), axis=0, keepdims=True)
        gm_o[0, f * 7 + 1 : f * 7 + 7] = total[f * 6 : f * 6 + 6]
        gb = (mod[0, f, 2:3] * ga).astype(BF16)
        acc[3] += nn(mix[0, f], gb)
        gms.append(nt(wo[...], gb).astype(BF16))

    def products(j, f):
        a = j * 2 * HD
        q = on_diagonal(qkv[0, f, a : a + 2 * HD] * BF16(0.125))
        go = on_diagonal(gms[f][a : a + 2 * HD])
        s = nn(qkv[0, f, D + a : D + a + 2 * HD].T, q)
        return s, nn(qkv[0, f, 2 * D + a : 2 * D + a + 2 * HD].T, go)

    def weights(j, f, s, dp):
        p = jnp.exp(s - tot[0, f, j : j + 1])
        ds = (p * (dp - jnp.sum(p * dp, axis=0, keepdims=True))).astype(BF16)
        return p.astype(BF16), ds

    def grads(j, f, p, ds):
        cut = p.shape[1] // 2
        for e in range(2):
            cols = slice(e * cut, (e + 1) * cut)
            at = j * 2 * HD + e * HD
            q = qkv[0, f, at : at + HD] * BF16(0.125)
            k = qkv[0, f, D + at : D + at + HD]
            dqkv_o[0, f, 2 * D + at : 2 * D + at + HD] = nt(gms[f][at : at + HD], p[:, cols]).astype(BF16)
            dqkv_o[0, f, D + at : D + at + HD] = nt(q, ds[:, cols]).astype(BF16)
            dqkv_o[0, f, at : at + HD] = (nn(k, ds[:, cols]) * 0.125).astype(BF16)

    pipelined([(j, f) for j in range(HEADS // 2) for f in range(frames)], [products, weights, grads], 1)
    for f in range(frames):
        nrm, _ = norm_stats(tok[0, f].astype(F32))
        first = (nrm * (1.0 + mod[0, f, 1:2]) + mod[0, f, 0:1]).astype(BF16)
        value = nt(first.T, dqkv_o[0, f])
        for j in range(3):
            acc[j] += value[:, j * D : (j + 1) * D]
    if last_chunk:

        @pl.when(b == pl.num_programs(0) - 1)
        def _():
            divide(i & 1, acc, sums[0], sums[1], LATE)


def call_spatial_bwd(idx, tok, cot, mod, qkv, mix, br, tot, wo, init, dl, start, last_chunk):
    n = len(dl)
    count = dl[0].shape[0]
    f, p = tok.shape[1:3]
    whole = lambda *s: pl.BlockSpec((1, f) + s, lambda b, i: (b + start, 0) + (0,) * len(s))
    part = lambda *s: pl.BlockSpec((1, f) + s, lambda b, i: (b, 0) + (0,) * len(s))
    pack = lambda *s: pl.BlockSpec((1,) + s, lambda b, i: (b,) + (0,) * len(s))
    fixed = lambda *s: pl.BlockSpec(s, lambda b, i: (0,) * len(s), pipeline_mode=pl.Buffered(1))
    sd = lambda s, d: jax.ShapeDtypeStruct((count,) + s, d)
    sum_out, sum_shape, sum_scratch = sum_specs(last_chunk, LATE)
    gm_rows = -(-7 * f // 8) * 8
    return pl.pallas_call(
        functools.partial(spatial_bwd, n, not init, last_chunk),
        grid_spec=pltpu.PrefetchScalarGridSpec(
            num_scalar_prefetch=1,
            grid=(count,),
            in_specs=[whole(p, D), whole(p, D), part(3, D), part(3 * D, p), part(D, p)]
            + [part(p, D), part(HEADS // 2, 2 * p), fixed(D, D)]
            + [fixed(4, D, D)] * len(init)
            + [pack(*dl[0].shape[1:])] * n,
            out_specs=[part(3 * D, p), part(p, D), pack(gm_rows, D)] + sum_out,
            scratch_shapes=[pltpu.VMEM((p, D), BF16)] + sum_scratch,
        ),
        out_shape=[sd((f, 3 * D, p), BF16), sd((f, p, D), F32), sd((gm_rows, D), F32)] + sum_shape,
        compiler_params=pltpu.CompilerParams(vmem_limit_bytes=VMEM),
        cost_estimate=cost(5 * count),
        name="spatial_bwd",
    )(idx, tok, cot, mod, qkv, mix, br, tot, wo, *init, *dl)


def last_step(n, start, last_chunk, idx, tok, mod, w, dqkv, ga, *rest):
    rest = list(rest)
    take = lambda c: [rest.pop(0) for _ in range(c)]
    pieces = take(n)
    rows = pieces[0].shape[2]
    frames = tok.shape[1]
    b = pl.program_id(0)
    i = idx[0]
    if last_chunk:
        cond = take(1)[0]
        gates = take(start // pl.num_programs(0) + 1)
        norms = take(len(gates) - 1)
        take(2)
        grad_o, out_o, gs_o, all_s = rest
        count = gates[0].shape[0]

        @pl.when(b == 0)
        def _():
            all_s[:, 9 * D :] = cond[...].astype(F32)
            for c, gate in enumerate(gates):
                for p in range(count):
                    for f in range(frames):
                        at = (c * count + p) * frames + f
                        for j in range(7):
                            all_s[at : at + 1, (2 + j) * D : (3 + j) * D] = gate[p, f * 7 + j : f * 7 + j + 1]
                        if c < len(norms):
                            for j in range(2):
                                all_s[at : at + 1, j * D : (j + 1) * D] = norms[c][p, f * 2 + j : f * 2 + j + 1]

    else:
        grad_o, out_o, gs_o = rest
        gs_o[...] = jnp.zeros_like(gs_o)

    def product(f):
        for k, piece in enumerate(pieces):
            out_o[0, f, pl.ds(pl.multiple_of((i ^ k) * rows, GROUP), rows), :] = piece[0, f]
        return (nt(dqkv[0, f].T, w[...]),)

    def finish(f, g):
        nrm, r = norm_stats(tok[0, f].astype(F32))
        for j, v in enumerate((g, g * nrm)):
            total = jnp.sum(v, axis=0, keepdims=True)
            if last_chunk:
                all_s[pl.ds((start + b) * frames + f, 1), j * D : (j + 1) * D] = total
            else:
                gs_o[0, f * 2 + j : f * 2 + j + 1] = total
        grad_o[0, f] = ga[0, f] + norm_back(g * (1.0 + mod[0, f, 1:2]), nrm, r)

    pipelined([(f,) for f in range(frames)], [product, finish], 1)
    if last_chunk:

        @pl.when(b == pl.num_programs(0) - 1)
        def _():
            gs_o[...] = all_s[...].astype(BF16)


def call_last(idx, tok, mod, w, dqkv, ga, ou, start, more, held):
    n = len(ou)
    count, f = dqkv.shape[:2]
    rows = ou[0].shape[2]
    packs, _, p = tok.shape[:3]
    gs_rows = -(-2 * f // 8) * 8
    whole = lambda *s: pl.BlockSpec((1, f) + s, lambda b, i: (b + start, 0) + (0,) * len(s))
    part = lambda *s: pl.BlockSpec((1, f) + s, lambda b, i: (b, 0) + (0,) * len(s))
    fixed = lambda *s: pl.BlockSpec(s, lambda b, i: (0,) * len(s), pipeline_mode=pl.Buffered(1))
    sd = jax.ShapeDtypeStruct
    more = more or []
    sums = sd((packs * f, 10 * D), BF16) if more else sd((count, gs_rows, D), F32)
    return pl.pallas_call(
        functools.partial(last_step, n, start, bool(more)),
        grid_spec=pltpu.PrefetchScalarGridSpec(
            num_scalar_prefetch=1,
            grid=(count,),
            in_specs=[whole(p, D), part(3, D), fixed(D, 3 * D), part(3 * D, p), part(p, D)]
            + [whole(rows, D)] * n
            + [fixed(*m.shape) for m in more]
            + [pl.BlockSpec(memory_space=pl.ANY)] * len(held),
            out_specs=[whole(p, D), whole(p, D)]
            + [
                pl.BlockSpec(sums.shape, lambda b, i: (0, 0))
                if more
                else pl.BlockSpec((1, gs_rows, D), lambda b, i: (b, 0, 0))
            ],
            scratch_shapes=[pltpu.VMEM(sums.shape, F32)] if more else [],
        ),
        out_shape=[sd(tok.shape, F32), sd(tok.shape, BF16), sums],
        input_output_aliases={6 + n + len(more) + j: j for j in range(len(held))},
        compiler_params=pltpu.CompilerParams(vmem_limit_bytes=VMEM),
        cost_estimate=cost(3 * count),
        name="last_step",
    )(idx, tok, mod, w, dqkv, ga, *ou, *more, *held)


def finish_early(idx, data, *refs):
    up_o, down_o, qkv_o, out_o = refs[-4:]
    half = D // 2
    for j in range(4):
        cols = slice(j * D, (j + 1) * D)
        up_o[:, cols] = data[j * half : (j + 1) * half].astype(F32)
        if j < 3:
            qkv_o[:, cols] = data[4 * D + j * half : 4 * D + (j + 1) * half].astype(F32)
    out_o[...] = data[4 * D + 3 * half :].astype(F32)
    for j in range(2):
        down_o[j * D : (j + 1) * D] = data[2 * D + j * D : 2 * D + (j + 1) * D].T.astype(F32)


def finish_late(idx, data, *refs):
    qkv_o, out_o = refs[-2:]
    half = D // 2
    for j in range(3):
        qkv_o[:, j * D : (j + 1) * D] = data[j * half : (j + 1) * half].astype(F32)
    out_o[...] = data[3 * half :].astype(F32)


def call_finish(kernel, shapes, idx, data, flip, held):
    spec = lambda s: pl.BlockSpec((s[0] // 2, s[1]), lambda j, i: ((i[0] & 1) ^ flip, 0))
    return pl.pallas_call(
        kernel,
        grid_spec=pltpu.PrefetchScalarGridSpec(
            num_scalar_prefetch=1,
            grid=(1,),
            in_specs=[pl.BlockSpec(data.shape, lambda j, i: (0, 0))]
            + [pl.BlockSpec(memory_space=pl.ANY)] * len(held),
            out_specs=[spec(s) for s in shapes],
        ),
        out_shape=[jax.ShapeDtypeStruct(s, F32) for s in shapes],
        input_output_aliases={2 + j: j for j in range(len(held))},
        compiler_params=pltpu.CompilerParams(vmem_limit_bytes=VMEM),
        cost_estimate=cost(2),
        name=kernel.__name__,
    )(idx, data, *held)


def ada_grad(turn, idx, own_act, other_act, own, other, out, act):
    first = (idx[0] & 1) == 0
    size = own.shape[0] // len(turn)
    block = lambda v, j: v[j * size : (j + 1) * size]

    def join(a, b):
        zero = [jnp.where(first, block(a, j), block(b, j)) for j in range(len(turn))]
        one = [jnp.where(first, block(b, j), block(a, j)) for j in turn]
        return jnp.concatenate(zero + one, axis=0)

    @pl.when(pl.program_id(0) == 0)
    def _():
        act[...] = silu_low(join(own_act, other_act)).T

    out[...] = nn(act[...], join(own, other))


def call_ada_grad(turn, idx, own, other):
    step = 3 * D
    act = pl.BlockSpec((own.shape[0], D), lambda j, i: (0, 9))
    mod = pl.BlockSpec((own.shape[0], step), lambda j, i: (0, j))
    return pl.pallas_call(
        functools.partial(ada_grad, turn),
        grid_spec=pltpu.PrefetchScalarGridSpec(
            num_scalar_prefetch=1,
            grid=(3,),
            in_specs=[act, act, mod, mod],
            out_specs=pl.BlockSpec((D, step), lambda j, i: (0, j)),
            scratch_shapes=[pltpu.VMEM((D, 2 * own.shape[0]), BF16)],
        ),
        out_shape=jax.ShapeDtypeStruct((D, 9 * D), F32),
        compiler_params=pltpu.CompilerParams(vmem_limit_bytes=VMEM),
        cost_estimate=cost(3),
        name="ada_grad",
    )(idx, own, other, own, other)


def swap(x, axis, mask):
    size = lax.axis_size(axis)
    return lax.ppermute(x, axis, [(s, s ^ mask) for s in range(size)])


def bits_of(axis):
    return [(axis, b) for b in range(lax.axis_size(axis).bit_length() - 1)]


def bit_of(axis, b):
    return (lax.axis_index(axis) >> b) & 1


def orders():
    pack, frame = bits_of("pack"), bits_of("frame")[1:]
    path = pack[:2]
    pack = pack[2:]
    while pack or frame:
        path += frame[:1] + pack[:1]
        pack, frame = pack[1:], frame[1:]
    turned = []
    for j in range(0, len(path), 2):
        turned += path[j : j + 2][::-1]
    return path, turned


def swap_by_core(x, step):
    nf, npk = lax.axis_size("frame"), lax.axis_size("pack")
    perm = []
    for pack in range(npk):
        for frame in range(nf):
            axis, b = step[frame & 1]
            to = (pack ^ (1 << b), frame) if axis == "pack" else (pack, frame ^ (1 << b))
            perm.append((frame * npk + pack, to[1] * npk + to[0]))
    return lax.ppermute(x, ("frame", "pack"), perm)


def bit_by_core(step):
    core = bit_of("frame", 0)
    return jnp.where(core == 0, bit_of(*step[0]), bit_of(*step[1]))


def doubled(g, other, mine):
    first = jnp.arange(2).reshape(2, 1, 1) == mine.astype(jnp.int32)
    return jnp.where(first, g[None], other[None]).reshape(-1, g.shape[1])


def tie_all(values, *deps):
    return list(lax.optimization_barrier((*values, *deps))[: len(values)])


def tie(value, *deps):
    return lax.optimization_barrier((value, *deps))[0]


class Order:
    def __init__(self):
        self.last = []

    def start(self, x):
        return tie(x, *self.last) if self.last else x

    def waited(self, x):
        self.last = [x]
        return x


class Gathering:
    def __init__(self, rows, steps):
        self.rows = rows
        self.steps = steps

    def start(self, step):
        self.moving = swap_by_core(self.rows, step)

    def end(self, step, after):
        self.rows = doubled(self.rows, tie(self.moving, after), bit_by_core(step))

    def sort(self, turn):
        size = self.rows.shape[0] // len(turn)
        turned = jnp.concatenate([self.rows[j * size : (j + 1) * size] for j in turn], axis=0)
        self.rows = jnp.where(bit_of("frame", 0) == 0, self.rows, turned)


def turned_blocks(steps):
    turn = []
    for j in range(1 << len(steps)):
        at = {s[0]: (j >> b) & 1 for b, s in enumerate(steps)}
        turn.append(sum(at[s[1]] << b for b, s in enumerate(steps)))
    return turn


class Summing:
    def __init__(self, order, send, keep, halvings):
        self.order = order
        self.keep = keep
        self.steps = list(zip(*orders()))
        self.halvings = halvings
        self.at = 0
        self.back = []
        self.beside = self.beside_step = None
        self.moving = swap(order.start(send), "frame", 1)

    def advance(self, after=None):
        moving = self.moving if after is None else tie(self.moving, after)
        moving = self.order.waited(moving)
        keep = self.keep
        if self.beside and self.beside_step:
            self.beside.end(self.beside_step, moving)
            if self.at == len(self.steps):
                self.beside.sort(turned_blocks(self.steps[self.halvings :]))
        total = lambda a, b: (a.astype(F32) + b.astype(F32)).astype(BF16)
        if self.at < len(self.steps):
            step = self.steps[self.at]
            if self.at < self.halvings:
                mine = bit_by_core(step)
                half = keep.shape[0] // 2
                part = lambda v, m: lax.dynamic_slice_in_dim(v, m * half, half, 0)
                send = total(part(keep, 1 - mine), part(moving, 1 - mine))
                self.keep = total(part(keep, mine), part(moving, mine))
                self.back.append(step)
            else:
                send = self.keep = total(keep, moving)
        else:
            if self.at == len(self.steps):
                self.keep = total(keep, moving)
            else:
                self.keep = doubled(keep, moving, bit_by_core(self.back.pop()))
            send = self.keep
            step = self.back[-1] if self.back else None
        self.at += 1
        send = self.order.start(send)
        self.sent = send
        if step is None:
            self.other = swap(send, "frame", 1)
            if self.beside:
                self.beside.other = swap(self.beside.rows, "frame", 1)
            return False
        self.moving = swap_by_core(send, step)
        if self.beside and self.at > self.halvings:
            self.beside.start(step)
            self.beside_step = step
        return True


def local(
    tokens,
    condition,
    clip_lengths,
    ada_weight,
    spatial_qkv,
    spatial_out,
    temporal_qkv,
    temporal_out,
    mlp_up,
    mlp_down,
    cotangent,
):
    n = lax.axis_size("frame")
    i = lax.axis_index("frame")
    idx = i.reshape(1).astype(jnp.int32)
    packs, f, patches = tokens.shape[:3]
    rows = patches // n
    count = packs // CHUNKS
    top = n // 2
    send = lambda parts: [parts[0]] + [swap(parts[k], "frame", k) for k in range(1, n)]

    own_cond = condition.reshape(packs * f, D)
    pad = -(-packs * f // GROUP) * GROUP
    cond_rows = jnp.concatenate([own_cond, jnp.zeros((pad - packs * f, D), BF16)], axis=0)

    def cut(k):
        v = lax.dynamic_slice_in_dim(cotangent, (i ^ k) * rows, rows, 2)
        return jnp.concatenate([v.reshape(-1, D), cond_rows], axis=0)

    ct = send([cut(k) for k in range(n)])
    sq_t = spatial_qkv.T
    tq_t = temporal_qkv.T
    frame_ids = jnp.concatenate([(i ^ k) * f + jnp.arange(f, dtype=jnp.int32) for k in range(n)])
    ends = [jnp.sum(clip_lengths[:, : j + 1], axis=1) for j in range(clip_lengths.shape[1])]
    segment = sum((e[:, None] <= frame_ids[None, :]).astype(jnp.int32) for e in ends)

    fwd = []
    source = tokens
    for c in range(CHUNKS):
        res = call_spatial_fwd(idx, source, condition, ada_weight, sq_t, spatial_out, c * count, count, n)
        slots = list(res[5:])
        if c:
            slots = tie_all(slots, *fwd[-1][1][1:])
        fwd.append((res[:5], send(slots)))
        if c == 0:
            source = tie(tokens, segment, tq_t, *ct[1:-1])

    init, mids = [], []
    for c in range(CHUNKS):
        last = c == CHUNKS - 1
        res = call_middle(
            idx, segment, fwd[c][1], ct, ada_weight, tq_t, temporal_qkv, temporal_out, mlp_up, mlp_down,
            init, c * count, last, packs,
        )
        init = [res[2 * n], *res[n : 2 * n]]
        res = list(res)
        if c:
            res = tie_all(res, *mids[-1][1:])
        mids.append(send(res[:n]))
    order = Order()
    early = Summing(order, res[2 * n], res[2 * n + 1], 3)
    outs = res[n : 2 * n]
    outs[top] = swap(outs[top], "frame", top)

    acc, backs = [], []
    for c in range(CHUNKS):
        last = c == CHUNKS - 1
        qkv, mix, br, tot, mod = fwd[c][0]
        dl = mids[c]
        if c:
            early.advance(after=backs[-1][2])
            dl = tie_all(dl, early.sent)
            for k in range(1, n):
                if k != top:
                    outs[k] = swap(tie(outs[k], early.sent), "frame", k)
        res = call_spatial_bwd(
            idx, tokens, cotangent, mod, qkv, mix, br, tot, spatial_out, acc, dl, c * count, last
        )
        acc = list(res[3:])
        backs.append(res)
    early.advance(after=backs[-1][2])
    late = Summing(order, acc[0], acc[1], 2)
    lasts, held = [], []
    for c in range(CHUNKS):
        last = c == CHUNKS - 1
        dqkv, ga = backs[c][:2]
        if c:
            early.advance(after=lasts[-1][2])
            late.advance(after=lasts[-1][2])
        ga = tie(ga, early.sent, late.moving if c == 0 else late.sent) if c else tie(ga, early.sent)
        more = [own_cond, *[b[2] for b in backs], *[v[2] for v in lasts]] if last else None
        res = call_last(idx, tokens, fwd[c][0][4], spatial_qkv, dqkv, ga, outs, c * count, more, held)
        held = list(res[:2])
        lasts.append(res)
    grad_tokens, output = held
    rows_of = lasts[-1][2]
    early.advance(after=rows_of)
    late.advance(after=rows_of)
    gather = late.beside = Gathering(rows_of, late.steps)
    early_shapes = [(D, MLP), (MLP, D), (D, 3 * D), (D, D)]
    late_shapes = [(D, 3 * D), (D, D)]
    half = None
    live = {"late": late, "early": early}
    skipped = False
    while live:
        for name in list(live):
            if name == "early" and len(early.back) == 0 and not skipped:
                skipped = True
            elif not live[name].advance():
                del live[name]
        if half is None and "early" not in live:
            half = call_finish(finish_early, early_shapes, idx, early.keep, 0, [])
            late.moving = tie(late.moving, half[3])
    own = rows_of[:, : 9 * D]
    back = jnp.einsum("tj,ij->ti", own, ada_weight, preferred_element_type=F32).reshape(packs, f, D)
    cf = condition.astype(F32)
    sig = 1.0 / (1.0 + jnp.exp(-cf))
    grad_condition = back * (sig * (1.0 + cf * (1.0 - sig)))

    late_half = call_finish(finish_late, late_shapes, idx, tie(late.keep, half[3]), 0, [])
    turn = turned_blocks(late.steps[: late.halvings][::-1])
    grad_ada = call_ada_grad(turn, idx, gather.rows, tie(gather.other, late_half[1]))
    late_other = tie(late.other, grad_ada)
    s_qkv, s_out = call_finish(finish_late, late_shapes, idx, late_other, 1, list(late_half))
    early_other = tie(early.other, s_out)
    up, down, t_qkv, t_out = call_finish(finish_early, early_shapes, idx, early_other, 1, list(half))
    return (output, grad_tokens, grad_condition, grad_ada, s_qkv, s_out, t_qkv, t_out, up, down)


def solution(mesh):
    tok = P("pack", "frame", None, None)
    cond = P("pack", "frame", None)
    return jax.shard_map(
        local,
        mesh=mesh,
        in_specs=(tok, cond, P("pack", None), P(), P(), P(), P(), P(), P(), P(), tok),
        out_specs=(tok, tok, cond, P(), P(), P(), P(), P(), P(), P()),
        check_vma=False,
    )
```

```python
import functools

import jax
import jax.numpy as jnp
from jax import lax
from jax.experimental import pallas as pl
from jax.experimental.pallas import tpu as pltpu
from jax.sharding import PartitionSpec as P

D = 384
HEADS = 6
HD = 64
MLP = 1536
F32 = jnp.float32
BF16 = jnp.bfloat16
CHUNKS = 2
GROUP = 16
VMEM = 58 * 2**20


def nn(a, b):
    return lax.dot_general(a, b, (((1,), (0,)), ((), ())), preferred_element_type=F32)


def nt(a, b):
    return lax.dot_general(a, b, (((1,), (1,)), ((), ())), preferred_element_type=F32)


def tn(a, b):
    return lax.dot_general(a, b, (((0,), (0,)), ((), ())), preferred_element_type=F32)


def cost(us):
    return pl.CostEstimate(flops=int(us * 5.0e9), bytes_accessed=1000, transcendentals=0)


def silu_low(v):
    v = v.astype(F32)
    return (v / (1.0 + jnp.exp(-v))).astype(BF16)


def on_diagonal(pair):
    none = jnp.zeros_like(pair[:HD])
    return jnp.concatenate(
        [
            jnp.concatenate([pair[:HD], none], axis=1),
            jnp.concatenate([none, pair[HD:]], axis=1),
        ],
        axis=0,
    )


def norm_stats(x):
    c = x - jnp.mean(x, -1, keepdims=True)
    r = lax.rsqrt(jnp.mean(c * c, -1, keepdims=True) + 1e-6)
    return c * r, r


def norm_back(h, n, r):
    return r * (h - jnp.mean(h, -1, keepdims=True) - n * jnp.mean(h * n, -1, keepdims=True))


def pipelined(items, stages, ahead=1):
    held = [[] for _ in stages]
    last = len(stages) - 1
    for t in range(len(items) + ahead * last):
        for s, stage in enumerate(stages):
            at = t - s * ahead
            if 0 <= at < len(items):
                value = stage(*items[at], *(held[s - 1].pop(0) if s else ()))
                if s < last:
                    held[s].append(value)


def spatial_fwd(start, idx, tok, cond, ada, w_t, wo, qkv_o, mix_o, br_o, tot_o, mod_o, *rest):
    slots, (scr, mod_s) = rest[:-2], rest[-2:]
    rows = slots[0].shape[2]
    frames = tok.shape[1]
    b = pl.program_id(0)

    @pl.when(b == 0)
    def _():
        mod_s[...] = nn(silu_low(cond[...]), ada[...])

    i = idx[0]
    mds = []
    for f in range(frames):
        at = (b + start) * frames + f
        md = [mod_s[pl.ds(at, 1), j * D : (j + 1) * D] for j in range(3)]
        for j in range(3):
            mod_o[0, f, j : j + 1] = md[j]
        n, _ = norm_stats(tok[0, f].astype(F32))
        first = (n * (1.0 + md[1]) + md[0]).astype(BF16)
        qkv_o[0, f] = nt(w_t[...], first).astype(BF16)
        mds.append(md)

    def scores(j, f):
        a = j * 2 * HD
        q = on_diagonal(qkv_o[0, f, a : a + 2 * HD] * BF16(0.125))
        k = qkv_o[0, f, D + a : D + a + 2 * HD]
        return (nn(k.T, q),)

    def mix(j, f, s):
        a = j * 2 * HD
        mx = jnp.max(s, axis=0, keepdims=True)
        p = jnp.exp(s - mx)
        total = jnp.sum(p, axis=0, keepdims=True)
        tot_o[0, f, j : j + 1] = mx + jnp.log(total)
        p = p.astype(BF16)
        scale = 1.0 / total
        cut = p.shape[1] // 2
        for e in range(2):
            v = qkv_o[0, f, 2 * D + a + e * HD : 2 * D + a + (e + 1) * HD]
            cols = slice(e * cut, (e + 1) * cut)
            mix_o[0, f, a + e * HD : a + (e + 1) * HD] = (nn(v, p[:, cols]) * scale[:, cols]).astype(BF16)

    pipelined([(j, f) for j in range(HEADS // 2) for f in range(frames)], [scores, mix], 2)
    for f in range(frames):
        br = tn(mix_o[0, f], wo[...])
        br_o[0, f] = br.astype(BF16)
        scr[f] = (tok[0, f].astype(F32) + mds[f][2] * br).astype(BF16)
        for k, slot in enumerate(slots):
            slot[0, f] = scr[f, pl.ds(pl.multiple_of((i ^ k) * rows, GROUP), rows), :]


def call_spatial_fwd(idx, tok, cond, ada, w_t, wo, start, count, n):
    f = tok.shape[1]
    p = tok.shape[2]
    whole = lambda *s: pl.BlockSpec((1, f) + s, lambda b, i: (b + start, 0) + (0,) * len(s))
    part = lambda *s: pl.BlockSpec((1, f) + s, lambda b, i: (b, 0) + (0,) * len(s))
    fixed = lambda *s: pl.BlockSpec(s, lambda b, i: (0,) * len(s), pipeline_mode=pl.Buffered(1))
    sd = lambda s, d: jax.ShapeDtypeStruct((count, f) + s, d)
    own = tok.shape[0] * f
    return pl.pallas_call(
        functools.partial(spatial_fwd, start),
        grid_spec=pltpu.PrefetchScalarGridSpec(
            num_scalar_prefetch=1,
            grid=(count,),
            in_specs=[whole(p, D), fixed(own, D), fixed(D, 3 * D), fixed(3 * D, D), fixed(D, D)],
            out_specs=[part(3 * D, p), part(D, p), part(p, D), part(HEADS // 2, 2 * p), part(3, D)]
            + [part(p // n, D)] * n,
            scratch_shapes=[pltpu.VMEM((f, p, D), BF16), pltpu.VMEM((own, 3 * D), F32)],
        ),
        out_shape=[sd((3 * D, p), BF16), sd((D, p), BF16), sd((p, D), BF16)]
        + [sd((HEADS // 2, 2 * p), F32), sd((3, D), F32)]
        + [sd((p // n, D), BF16)] * n,
        compiler_params=pltpu.CompilerParams(vmem_limit_bytes=VMEM),
        cost_estimate=cost(4 * count),
        name="spatial_fwd",
    )(idx, tok, cond.reshape(-1, D), ada, w_t, wo)


def tile_places(n, f, rows):
    return [
        (k, j * rows + g * GROUP)
        for g in range(rows // GROUP)
        for k in range(n)
        for j in range(f)
    ]


def divide(mine, acc, sent, kept, kinds):
    at = 0
    base = 0
    for kind, blocks in kinds:
        for out, who in ((sent, 1 - mine), (kept, mine)):
            row = at
            if kind == "rows":
                half = D // 2
                for j in range(blocks):
                    part = acc[base + j, pl.ds(pl.multiple_of(who * half, GROUP), half), :]
                    out[row : row + half] = part.astype(BF16)
                    row += half
            else:
                for j in range(blocks // 2):
                    out[row : row + D] = acc[base + who * (blocks // 2) + j].astype(BF16)
                    row += D
        at = row
        base += blocks


EARLY = (("rows", 4), ("blocks", 4), ("rows", 4))
LATE = (("rows", 4),)


def sum_specs(last_chunk, kinds):
    const = lambda *s: pl.BlockSpec(s, lambda *g: (0,) * len(s))
    sd = jax.ShapeDtypeStruct
    blocks = sum(k[1] for k in kinds)
    if not last_chunk:
        return [const(blocks, D, D)], [sd((blocks, D, D), F32)], []
    half = (blocks * D // 2, D)
    return [const(*half)] * 2, [sd(half, BF16)] * 2, [pltpu.VMEM((blocks, D, D), F32)]


def middle(n, f, start, first_chunk, last_chunk, once, idx, seg, *refs):
    refs = list(refs)
    take = lambda c: [refs.pop(0) for _ in range(c)]
    a1, ct, conds = take(n), take(n), take(n)
    ada_a, ada_b, tq_t, tq, to, up, down = take(7)
    if not first_chunk:
        init = take(1 + n)[0]
    dl = take(n)
    ou = take(n)
    sums = take(2 if last_chunk else 1)
    acc, init_sem = refs.pop(), refs.pop()
    mod_s, sum_s, qkv_s, p_s, mix_s, dg_s, hid_s, dqkv_s = refs
    rows = a1[0].shape[2]
    groups = rows // GROUP
    frames = n * f
    span = frames * GROUP
    tokens = span * groups
    places = tile_places(n, f, rows)
    b = pl.program_id(0)
    fresh = first_chunk and once

    @pl.when(b == 0)
    def _():
        if not first_chunk:
            pltpu.make_async_copy(init, acc, init_sem).start()
        elif not fresh:
            acc[...] = jnp.zeros_like(acc)
        sum_s[...] = jnp.zeros_like(sum_s)
        act = silu_low(jnp.concatenate([c[...] for c in conds], axis=0))
        mod_s[:, : 3 * D] = nn(act, ada_a[...])
        mod_s[:, 3 * D :] = nn(act, ada_b[...])

    pad = conds[0].shape[0]
    units = a1[0].shape[0]

    def tile(u):
        pack = b * units + u

        def per_frame(piece, plus=0.0):
            cols = slice(piece * D, (piece + 1) * D)
            at = [k * pad + (pack + start) * f + j for k in range(n) for j in range(f)]
            rows_ = [mod_s[pl.ds(t, 1), cols] + plus for t in at]
            one = jnp.concatenate([jnp.broadcast_to(r, (GROUP, D)) for r in rows_], axis=0)
            return jnp.concatenate([one] * groups, axis=0)

        def frame_sum(piece, v):
            total = jnp.sum(jnp.sum(v.reshape(groups, frames, GROUP, D), axis=0), axis=1)
            for k in range(n):
                for j in range(f):
                    sum_s[u, k, j * 6 + piece : j * 6 + piece + 1] = total[k * f + j : k * f + j + 1]

        def add(base, col, value):
            for j in range(value.shape[1] // D):
                part = value[:, j * D : (j + 1) * D]
                at = base + col // D + j
                acc[at] = part if fresh and u == 0 else acc[at] + part

        x1 = jnp.concatenate(
            [a1[k][u, r // rows, r % rows : r % rows + GROUP] for k, r in places], axis=0
        ).astype(F32)
        n2, r2 = norm_stats(x1)
        second = (n2 * per_frame(1, 1.0) + per_frame(0)).astype(BF16)
        yield
        qkv_s[u] = nt(tq_t[...], second).astype(BF16)
        lane = lax.broadcasted_iota(jnp.int32, (span, span), 0) % GROUP
        other = lax.broadcasted_iota(jnp.int32, (span, span), 1) % GROUP
        segs = [seg[pack + start, t] for t in range(frames)]

        def segment_of(axis):
            at = lax.broadcasted_iota(jnp.int32, (span, span), axis) // GROUP
            value = jnp.zeros((span, span), jnp.int32)
            for t in range(frames):
                value = jnp.where(at == t, segs[t], value)
            return value

        allowed = (segment_of(0) == segment_of(1)) & (lane == other)
        bias = jnp.where(allowed, 0.0, -1e30)
        bias = jnp.concatenate([bias, bias], axis=1)
        items = [(g, j) for g in range(groups) for j in range(HEADS // 2)]

        def pair(ref, kind, g, j):
            a = kind * D + j * 2 * HD
            return ref[u, a : a + 2 * HD, g * span : (g + 1) * span]

        def scores(g, j):
            q = on_diagonal(pair(qkv_s, 0, g, j) * BF16(0.125))
            return (nn(pair(qkv_s, 1, g, j).T, q),)

        def mix(g, j, s):
            s = s + bias
            p = jnp.exp(s - jnp.max(s, axis=0, keepdims=True))
            p = p * (1.0 / jnp.sum(p, axis=0, keepdims=True))
            p_s[u, g * (HEADS // 2) + j] = p
            o = nn(pair(qkv_s, 2, g, j), p.astype(BF16)).astype(BF16)
            a, cols = j * 2 * HD, slice(g * span, (g + 1) * span)
            mix_s[u, a : a + HD, cols] = o[:HD, :span]
            mix_s[u, a + HD : a + 2 * HD, cols] = o[HD:, span:]

        pipelined(items, [scores, mix], 2 if span <= 256 else 0)
        yield
        br2 = tn(mix_s[u], to[...])
        x2 = x1 + per_frame(2) * br2
        n3, r3 = norm_stats(x2)
        third = (n3 * per_frame(4, 1.0) + per_frame(3)).astype(BF16)
        yield
        step = STEP
        br3 = []

        def mlp_in(c):
            return (nn(third, up[:, c : c + step]),)

        def mlp_out(c, pre):
            sq = pre * pre
            t = jnp.tanh(pre * (0.7978845608028654 + (0.7978845608028654 * 0.044715) * sq))
            half = 0.5 + 0.5 * t
            hid = (pre * half).astype(BF16)
            hid_s[u, :, c : c + step] = hid
            inner = 0.7978845608028654 + (3 * 0.7978845608028654 * 0.044715) * sq
            dg_s[u, :, c : c + step] = (half + 0.5 * pre * (1.0 - t * t) * inner).astype(BF16)
            br3[:] = [sum(br3, nn(hid, down[c : c + step, :]))]

        pipelined([(c,) for c in range(0, MLP, step)], [mlp_in, mlp_out], 1)
        br3 = br3[0]
        yield
        gate3 = per_frame(5)
        value = (x2 + gate3 * br3).astype(BF16)
        for t, (k, r) in enumerate(places):
            ou[k][u, r // rows, r % rows : r % rows + GROUP] = value[t * GROUP : (t + 1) * GROUP]
        cot = jnp.concatenate([ct[k][u * f * rows + r : u * f * rows + r + GROUP] for k, r in places], axis=0).astype(F32)
        frame_sum(5, cot * br3)
        gb3 = (gate3 * cot).astype(BF16)
        if not first_chunk and u == 0:

            @pl.when(b == 0)
            def _():
                pltpu.make_async_copy(init, acc, init_sem).wait()

        gb3_t = gb3.T
        third_t = third.T
        yield
        g3 = []

        def back_in(c):
            return (nt(gb3, down[c : c + step, :]),)

        def back_out(c, gh):
            gp = (gh * dg_s[u, :, c : c + step]).astype(BF16)
            add(4, c, nn(gb3_t, hid_s[u, :, c : c + step]))
            add(0, c, nn(third_t, gp))
            g3[:] = [sum(g3, nt(gp, up[:, c : c + step]))]

        pipelined([(c,) for c in range(0, MLP, step)], [back_in, back_out], 1)
        g3 = g3[0]
        yield
        frame_sum(3, g3)
        frame_sum(4, g3 * n3)
        dx3 = norm_back(g3 * per_frame(4, 1.0), n3, r3)
        ga2 = cot + dx3
        frame_sum(2, ga2 * br2)
        gb2 = (per_frame(2) * ga2).astype(BF16)
        add(11, 0, nn(mix_s[u], gb2))
        gm_t = nt(to[...], gb2).astype(BF16)
        yield

        def grads_in(g, j):
            go = on_diagonal(gm_t[j * 2 * HD : (j + 1) * 2 * HD, g * span : (g + 1) * span])
            return (go, nn(pair(qkv_s, 2, g, j).T, go))

        def grads_mid(g, j, go, dp):
            p = p_s[u, g * (HEADS // 2) + j]
            ds = (p * (dp - jnp.sum(p * dp, axis=0, keepdims=True))).astype(BF16)
            return (go, p.astype(BF16), ds)

        def grads_out(g, j, go, p, ds):
            a, cols = j * 2 * HD, slice(g * span, (g + 1) * span)
            q = on_diagonal(pair(qkv_s, 0, g, j) * BF16(0.125))
            dqkv_s[u, 2 * D + a : 2 * D + a + 2 * HD, cols] = nt(go, p).astype(BF16)
            dqkv_s[u, D + a : D + a + 2 * HD, cols] = nt(q, ds).astype(BF16)
            dq = (nn(pair(qkv_s, 1, g, j), ds) * 0.125).astype(BF16)
            dqkv_s[u, a : a + HD, cols] = dq[:HD, :span]
            dqkv_s[u, a + HD : a + 2 * HD, cols] = dq[HD:, span:]

        pipelined(items, [grads_in, grads_mid, grads_out], 1 if span <= 256 else 0)
        yield
        dqkv = dqkv_s[u]
        add(8, 0, nt(second.T, dqkv))
        g2 = nn(tq[...], dqkv).T
        yield
        frame_sum(0, g2)
        frame_sum(1, g2 * n2)
        dx2 = norm_back(g2 * per_frame(1, 1.0), n2, r2)
        value = (dx3 + dx2).astype(BF16)
        for t, (k, r) in enumerate(places):
            dl[k][u, r : r + GROUP] = value[t * GROUP : (t + 1) * GROUP]
        for k in range(n):
            dl[k][u, f * rows :] = sum_s[u, k].astype(BF16)

    tiles = [tile(u) for u in range(units)]
    turn = 0
    while tiles:
        for t in list(tiles[: turn + 1]):
            if next(t, True):
                tiles.remove(t)
                turn -= 1
        turn += 1
    if last_chunk:

        @pl.when(b == pl.num_programs(0) - 1)
        def _():
            divide(idx[0] & 1, acc, sums[0], sums[1], EARLY)

    else:

        @pl.when(b == pl.num_programs(0) - 1)
        def _():
            copy = pltpu.make_async_copy(acc, sums[0], init_sem)
            copy.start()
            copy.wait()


STEP = 2 * D


def sum_rows(f):
    return -(-6 * f // GROUP) * GROUP


def call_middle(idx, seg, a1, ct, ada, tq_t, tq, to, up, down, init, start, last_chunk, packs):
    n = len(a1)
    count, f, rows = a1[0].shape[:3]
    frames = n * f
    span = frames * GROUP
    tokens = frames * rows
    groups = rows // GROUP
    pad = ct[0].shape[0] - packs * f * rows
    extra = sum_rows(f)
    units = count if span <= 256 else 1
    at = start // units
    part = lambda *s: pl.BlockSpec((units,) + s, lambda b, *i: (b,) + (0,) * len(s))
    fixed = lambda *s: pl.BlockSpec(s, lambda b, *i: (0,) * len(s), pipeline_mode=pl.Buffered(1))
    column = lambda j: pl.BlockSpec((D, 3 * D), lambda b, *i: (0, j), pipeline_mode=pl.Buffered(1))
    sd = jax.ShapeDtypeStruct
    sum_out, sum_shape, sum_scratch = sum_specs(last_chunk, EARLY)
    if not last_chunk:
        sum_out, sum_scratch = [pl.BlockSpec(memory_space=pl.ANY)], [pltpu.VMEM((12, D, D), F32)]
    whole = pl.BlockSpec((units, f, rows, D), lambda b, *i: (b + at, 0, 0, 0))
    return pl.pallas_call(
        functools.partial(middle, n, f, start, not init, last_chunk, units == count),
        grid_spec=pltpu.PrefetchScalarGridSpec(
            num_scalar_prefetch=2,
            grid=(count // units,),
            in_specs=[part(f, rows, D)] * n
            + [pl.BlockSpec((units * f * rows, D), lambda b, *i: (b + at, 0))] * n
            + [pl.BlockSpec((pad, D), lambda b, *i: (packs * f * rows // pad, 0))] * n
            + [column(1), column(2), fixed(3 * D, D), fixed(D, 3 * D)]
            + [fixed(D, D), fixed(D, MLP), fixed(MLP, D)]
            + [pl.BlockSpec(memory_space=pl.ANY)] * len(init),
            out_specs=[part(f * rows + extra, D)] * n + [whole] * n + sum_out,
            scratch_shapes=[
                pltpu.VMEM((n * pad, 6 * D), F32),
                pltpu.VMEM((units, n, extra, D), F32),
                pltpu.VMEM((units, 3 * D, tokens), BF16),
                pltpu.VMEM((units, groups * HEADS // 2, span, 2 * span), F32),
                pltpu.VMEM((units, D, tokens), BF16),
                pltpu.VMEM((units, tokens, MLP), BF16),
                pltpu.VMEM((units, tokens, MLP), BF16),
                pltpu.VMEM((units, 3 * D, tokens), BF16),
                pltpu.SemaphoreType.DMA,
            ]
            + sum_scratch,
        ),
        out_shape=[sd((count, f * rows + extra, D), BF16)] * n
        + [sd((packs, f, rows, D), BF16)] * n
        + sum_shape,
        input_output_aliases={2 + 3 * n + 8 + j: n + j for j in range(n)} if init else {},
        compiler_params=pltpu.CompilerParams(vmem_limit_bytes=VMEM),
        cost_estimate=cost(14 * count),
        name="middle",
    )(idx, seg, *a1, *ct, *ct, ada, ada, tq_t, tq, to, up, down, *init)


def spatial_bwd(n, first_chunk, last_chunk, idx, tok, cot, mod, qkv, mix, br, tot, wo, *rest):
    rest = list(rest)
    take = lambda c: [rest.pop(0) for _ in range(c)]
    if not first_chunk:
        init = take(1)[0]
    dl = take(n)
    dqkv_o, ga_o, gm_o, *sums = take(3 + (2 if last_chunk else 1))
    scr = rest.pop(0)
    acc = rest.pop() if last_chunk else sums[0]
    b = pl.program_id(0)

    @pl.when(b == 0)
    def _():
        acc[...] = jnp.zeros_like(acc) if first_chunk else init[...]
        gm_o[...] = jnp.zeros_like(gm_o)

    frames = tok.shape[1]
    rows = tok.shape[2] // n
    i = idx[0]
    total = sum(d[0, frames * rows :].astype(F32) for d in dl)
    gms = []
    for f in range(frames):
        for k in range(n):
            scr[pl.ds(pl.multiple_of((i ^ k) * rows, GROUP), rows), :] = dl[k][0, f * rows : (f + 1) * rows]
        ga = cot[0, f].astype(F32) + scr[...].astype(F32)
        ga_o[0, f] = ga
        gm_o[0, f * 7 : f * 7 + 1] = jnp.sum(ga * br[0, f].astype(F32), axis=0, keepdims=True)
        gm_o[0, f * 7 + 1 : f * 7 + 7] = total[f * 6 : f * 6 + 6]
        gb = (mod[0, f, 2:3] * ga).astype(BF16)
        acc[3] += nn(mix[0, f], gb)
        gms.append(nt(wo[...], gb).astype(BF16))

    def products(j, f):
        a = j * 2 * HD
        q = on_diagonal(qkv[0, f, a : a + 2 * HD] * BF16(0.125))
        go = on_diagonal(gms[f][a : a + 2 * HD])
        s = nn(qkv[0, f, D + a : D + a + 2 * HD].T, q)
        return s, nn(qkv[0, f, 2 * D + a : 2 * D + a + 2 * HD].T, go)

    def weights(j, f, s, dp):
        p = jnp.exp(s - tot[0, f, j : j + 1])
        ds = (p * (dp - jnp.sum(p * dp, axis=0, keepdims=True))).astype(BF16)
        return p.astype(BF16), ds

    def grads(j, f, p, ds):
        cut = p.shape[1] // 2
        for e in range(2):
            cols = slice(e * cut, (e + 1) * cut)
            at = j * 2 * HD + e * HD
            q = qkv[0, f, at : at + HD] * BF16(0.125)
            k = qkv[0, f, D + at : D + at + HD]
            dqkv_o[0, f, 2 * D + at : 2 * D + at + HD] = nt(gms[f][at : at + HD], p[:, cols]).astype(BF16)
            dqkv_o[0, f, D + at : D + at + HD] = nt(q, ds[:, cols]).astype(BF16)
            dqkv_o[0, f, at : at + HD] = (nn(k, ds[:, cols]) * 0.125).astype(BF16)

    pipelined([(j, f) for j in range(HEADS // 2) for f in range(frames)], [products, weights, grads], 1)
    for f in range(frames):
        nrm, _ = norm_stats(tok[0, f].astype(F32))
        first = (nrm * (1.0 + mod[0, f, 1:2]) + mod[0, f, 0:1]).astype(BF16)
        value = nt(first.T, dqkv_o[0, f])
        for j in range(3):
            acc[j] += value[:, j * D : (j + 1) * D]
    if last_chunk:

        @pl.when(b == pl.num_programs(0) - 1)
        def _():
            divide(i & 1, acc, sums[0], sums[1], LATE)


def call_spatial_bwd(idx, tok, cot, mod, qkv, mix, br, tot, wo, init, dl, start, last_chunk):
    n = len(dl)
    count = dl[0].shape[0]
    f, p = tok.shape[1:3]
    whole = lambda *s: pl.BlockSpec((1, f) + s, lambda b, i: (b + start, 0) + (0,) * len(s))
    part = lambda *s: pl.BlockSpec((1, f) + s, lambda b, i: (b, 0) + (0,) * len(s))
    pack = lambda *s: pl.BlockSpec((1,) + s, lambda b, i: (b,) + (0,) * len(s))
    fixed = lambda *s: pl.BlockSpec(s, lambda b, i: (0,) * len(s), pipeline_mode=pl.Buffered(1))
    sd = lambda s, d: jax.ShapeDtypeStruct((count,) + s, d)
    sum_out, sum_shape, sum_scratch = sum_specs(last_chunk, LATE)
    gm_rows = -(-7 * f // 8) * 8
    return pl.pallas_call(
        functools.partial(spatial_bwd, n, not init, last_chunk),
        grid_spec=pltpu.PrefetchScalarGridSpec(
            num_scalar_prefetch=1,
            grid=(count,),
            in_specs=[whole(p, D), whole(p, D), part(3, D), part(3 * D, p), part(D, p)]
            + [part(p, D), part(HEADS // 2, 2 * p), fixed(D, D)]
            + [fixed(4, D, D)] * len(init)
            + [pack(*dl[0].shape[1:])] * n,
            out_specs=[part(3 * D, p), part(p, D), pack(gm_rows, D)] + sum_out,
            scratch_shapes=[pltpu.VMEM((p, D), BF16)] + sum_scratch,
        ),
        out_shape=[sd((f, 3 * D, p), BF16), sd((f, p, D), F32), sd((gm_rows, D), F32)] + sum_shape,
        compiler_params=pltpu.CompilerParams(vmem_limit_bytes=VMEM),
        cost_estimate=cost(5 * count),
        name="spatial_bwd",
    )(idx, tok, cot, mod, qkv, mix, br, tot, wo, *init, *dl)


def last_step(n, start, last_chunk, idx, tok, mod, w, dqkv, ga, *rest):
    rest = list(rest)
    take = lambda c: [rest.pop(0) for _ in range(c)]
    pieces = take(n)
    rows = pieces[0].shape[2]
    frames = tok.shape[1]
    b = pl.program_id(0)
    i = idx[0]
    if last_chunk:
        cond = take(1)[0]
        gates = take(start // pl.num_programs(0) + 1)
        norms = take(len(gates) - 1)
        take(2)
        grad_o, out_o, gs_o, all_s = rest
        count = gates[0].shape[0]

        @pl.when(b == 0)
        def _():
            all_s[:, 9 * D :] = cond[...].astype(F32)
            for c, gate in enumerate(gates):
                for p in range(count):
                    for f in range(frames):
                        at = (c * count + p) * frames + f
                        for j in range(7):
                            all_s[at : at + 1, (2 + j) * D : (3 + j) * D] = gate[p, f * 7 + j : f * 7 + j + 1]
                        if c < len(norms):
                            for j in range(2):
                                all_s[at : at + 1, j * D : (j + 1) * D] = norms[c][p, f * 2 + j : f * 2 + j + 1]

    else:
        grad_o, out_o, gs_o = rest
        gs_o[...] = jnp.zeros_like(gs_o)

    def product(f):
        for k, piece in enumerate(pieces):
            out_o[0, f, pl.ds(pl.multiple_of((i ^ k) * rows, GROUP), rows), :] = piece[0, f]
        return (nt(dqkv[0, f].T, w[...]),)

    def finish(f, g):
        nrm, r = norm_stats(tok[0, f].astype(F32))
        for j, v in enumerate((g, g * nrm)):
            total = jnp.sum(v, axis=0, keepdims=True)
            if last_chunk:
                all_s[pl.ds((start + b) * frames + f, 1), j * D : (j + 1) * D] = total
            else:
                gs_o[0, f * 2 + j : f * 2 + j + 1] = total
        grad_o[0, f] = ga[0, f] + norm_back(g * (1.0 + mod[0, f, 1:2]), nrm, r)

    pipelined([(f,) for f in range(frames)], [product, finish], 1)
    if last_chunk:

        @pl.when(b == pl.num_programs(0) - 1)
        def _():
            gs_o[...] = all_s[...].astype(BF16)


def call_last(idx, tok, mod, w, dqkv, ga, ou, start, more, held):
    n = len(ou)
    count, f = dqkv.shape[:2]
    rows = ou[0].shape[2]
    packs, _, p = tok.shape[:3]
    gs_rows = -(-2 * f // 8) * 8
    whole = lambda *s: pl.BlockSpec((1, f) + s, lambda b, i: (b + start, 0) + (0,) * len(s))
    part = lambda *s: pl.BlockSpec((1, f) + s, lambda b, i: (b, 0) + (0,) * len(s))
    fixed = lambda *s: pl.BlockSpec(s, lambda b, i: (0,) * len(s), pipeline_mode=pl.Buffered(1))
    sd = jax.ShapeDtypeStruct
    more = more or []
    sums = sd((packs * f, 10 * D), BF16) if more else sd((count, gs_rows, D), F32)
    return pl.pallas_call(
        functools.partial(last_step, n, start, bool(more)),
        grid_spec=pltpu.PrefetchScalarGridSpec(
            num_scalar_prefetch=1,
            grid=(count,),
            in_specs=[whole(p, D), part(3, D), fixed(D, 3 * D), part(3 * D, p), part(p, D)]
            + [whole(rows, D)] * n
            + [fixed(*m.shape) for m in more]
            + [pl.BlockSpec(memory_space=pl.ANY)] * len(held),
            out_specs=[whole(p, D), whole(p, D)]
            + [
                pl.BlockSpec(sums.shape, lambda b, i: (0, 0))
                if more
                else pl.BlockSpec((1, gs_rows, D), lambda b, i: (b, 0, 0))
            ],
            scratch_shapes=[pltpu.VMEM(sums.shape, F32)] if more else [],
        ),
        out_shape=[sd(tok.shape, F32), sd(tok.shape, BF16), sums],
        input_output_aliases={6 + n + len(more) + j: j for j in range(len(held))},
        compiler_params=pltpu.CompilerParams(vmem_limit_bytes=VMEM),
        cost_estimate=cost(3 * count),
        name="last_step",
    )(idx, tok, mod, w, dqkv, ga, *ou, *more, *held)


def finish_early(idx, data, *refs):
    up_o, down_o, qkv_o, out_o = refs[-4:]
    half = D // 2
    for j in range(4):
        cols = slice(j * D, (j + 1) * D)
        up_o[:, cols] = data[j * half : (j + 1) * half].astype(F32)
        if j < 3:
            qkv_o[:, cols] = data[4 * D + j * half : 4 * D + (j + 1) * half].astype(F32)
    out_o[...] = data[4 * D + 3 * half :].astype(F32)
    for j in range(2):
        down_o[j * D : (j + 1) * D] = data[2 * D + j * D : 2 * D + (j + 1) * D].T.astype(F32)


def finish_late(idx, data, *refs):
    qkv_o, out_o = refs[-2:]
    half = D // 2
    for j in range(3):
        qkv_o[:, j * D : (j + 1) * D] = data[j * half : (j + 1) * half].astype(F32)
    out_o[...] = data[3 * half :].astype(F32)


def call_finish(kernel, shapes, idx, data, flip, held):
    spec = lambda s: pl.BlockSpec((s[0] // 2, s[1]), lambda j, i: ((i[0] & 1) ^ flip, 0))
    return pl.pallas_call(
        kernel,
        grid_spec=pltpu.PrefetchScalarGridSpec(
            num_scalar_prefetch=1,
            grid=(1,),
            in_specs=[pl.BlockSpec(data.shape, lambda j, i: (0, 0))]
            + [pl.BlockSpec(memory_space=pl.ANY)] * len(held),
            out_specs=[spec(s) for s in shapes],
        ),
        out_shape=[jax.ShapeDtypeStruct(s, F32) for s in shapes],
        input_output_aliases={2 + j: j for j in range(len(held))},
        compiler_params=pltpu.CompilerParams(vmem_limit_bytes=VMEM),
        cost_estimate=cost(2),
        name=kernel.__name__,
    )(idx, data, *held)


def ada_grad(turn, idx, own_act, other_act, own, other, out, act):
    first = (idx[0] & 1) == 0
    size = own.shape[0] // len(turn)
    block = lambda v, j: v[j * size : (j + 1) * size]

    def join(a, b):
        zero = [jnp.where(first, block(a, j), block(b, j)) for j in range(len(turn))]
        one = [jnp.where(first, block(b, j), block(a, j)) for j in turn]
        return jnp.concatenate(zero + one, axis=0)

    @pl.when(pl.program_id(0) == 0)
    def _():
        act[...] = silu_low(join(own_act, other_act)).T

    out[...] = nn(act[...], join(own, other))


def call_ada_grad(turn, idx, own, other):
    step = 3 * D
    act = pl.BlockSpec((own.shape[0], D), lambda j, i: (0, 9))
    mod = pl.BlockSpec((own.shape[0], step), lambda j, i: (0, j))
    return pl.pallas_call(
        functools.partial(ada_grad, turn),
        grid_spec=pltpu.PrefetchScalarGridSpec(
            num_scalar_prefetch=1,
            grid=(3,),
            in_specs=[act, act, mod, mod],
            out_specs=pl.BlockSpec((D, step), lambda j, i: (0, j)),
            scratch_shapes=[pltpu.VMEM((D, 2 * own.shape[0]), BF16)],
        ),
        out_shape=jax.ShapeDtypeStruct((D, 9 * D), F32),
        compiler_params=pltpu.CompilerParams(vmem_limit_bytes=VMEM),
        cost_estimate=cost(3),
        name="ada_grad",
    )(idx, own, other, own, other)


def swap(x, axis, mask):
    size = lax.axis_size(axis)
    return lax.ppermute(x, axis, [(s, s ^ mask) for s in range(size)])


def bits_of(axis):
    return [(axis, b) for b in range(lax.axis_size(axis).bit_length() - 1)]


def bit_of(axis, b):
    return (lax.axis_index(axis) >> b) & 1


def orders():
    pack, frame = bits_of("pack"), bits_of("frame")[1:]
    path = pack[:2]
    pack = pack[2:]
    while pack or frame:
        path += frame[:1] + pack[:1]
        pack, frame = pack[1:], frame[1:]
    turned = []
    for j in range(0, len(path), 2):
        turned += path[j : j + 2][::-1]
    return path, turned


def swap_by_core(x, step):
    nf, npk = lax.axis_size("frame"), lax.axis_size("pack")
    perm = []
    for pack in range(npk):
        for frame in range(nf):
            axis, b = step[frame & 1]
            to = (pack ^ (1 << b), frame) if axis == "pack" else (pack, frame ^ (1 << b))
            perm.append((frame * npk + pack, to[1] * npk + to[0]))
    return lax.ppermute(x, ("frame", "pack"), perm)


def bit_by_core(step):
    core = bit_of("frame", 0)
    return jnp.where(core == 0, bit_of(*step[0]), bit_of(*step[1]))


def doubled(g, other, mine):
    first = jnp.arange(2).reshape(2, 1, 1) == mine.astype(jnp.int32)
    return jnp.where(first, g[None], other[None]).reshape(-1, g.shape[1])


def tie_all(values, *deps):
    return list(lax.optimization_barrier((*values, *deps))[: len(values)])


def tie(value, *deps):
    return lax.optimization_barrier((value, *deps))[0]


class Order:
    def __init__(self):
        self.last = []

    def start(self, x):
        return tie(x, *self.last) if self.last else x

    def waited(self, x):
        self.last = [x]
        return x


class Gathering:
    def __init__(self, rows, steps):
        self.rows = rows
        self.steps = steps

    def start(self, step):
        self.moving = swap_by_core(self.rows, step)

    def end(self, step, after):
        self.rows = doubled(self.rows, tie(self.moving, after), bit_by_core(step))

    def sort(self, turn):
        size = self.rows.shape[0] // len(turn)
        turned = jnp.concatenate([self.rows[j * size : (j + 1) * size] for j in turn], axis=0)
        self.rows = jnp.where(bit_of("frame", 0) == 0, self.rows, turned)


def turned_blocks(steps):
    turn = []
    for j in range(1 << len(steps)):
        at = {s[0]: (j >> b) & 1 for b, s in enumerate(steps)}
        turn.append(sum(at[s[1]] << b for b, s in enumerate(steps)))
    return turn


class Summing:
    def __init__(self, order, send, keep, halvings):
        self.order = order
        self.keep = keep
        self.steps = list(zip(*orders()))
        self.halvings = halvings
        self.at = 0
        self.back = []
        self.beside = self.beside_step = None
        self.moving = swap(order.start(send), "frame", 1)

    def advance(self, after=None):
        moving = self.moving if after is None else tie(self.moving, after)
        moving = self.order.waited(moving)
        keep = self.keep
        if self.beside and self.beside_step:
            self.beside.end(self.beside_step, moving)
            if self.at == len(self.steps):
                self.beside.sort(turned_blocks(self.steps[self.halvings :]))
        total = lambda a, b: (a.astype(F32) + b.astype(F32)).astype(BF16)
        if self.at < len(self.steps):
            step = self.steps[self.at]
            if self.at < self.halvings:
                mine = bit_by_core(step)
                half = keep.shape[0] // 2
                part = lambda v, m: lax.dynamic_slice_in_dim(v, m * half, half, 0)
                send = total(part(keep, 1 - mine), part(moving, 1 - mine))
                self.keep = total(part(keep, mine), part(moving, mine))
                self.back.append(step)
            else:
                send = self.keep = total(keep, moving)
        else:
            if self.at == len(self.steps):
                self.keep = total(keep, moving)
            else:
                self.keep = doubled(keep, moving, bit_by_core(self.back.pop()))
            send = self.keep
            step = self.back[-1] if self.back else None
        self.at += 1
        send = self.order.start(send)
        self.sent = send
        if step is None:
            self.other = swap(send, "frame", 1)
            if self.beside:
                self.beside.other = swap(self.beside.rows, "frame", 1)
            return False
        self.moving = swap_by_core(send, step)
        if self.beside and self.at > self.halvings:
            self.beside.start(step)
            self.beside_step = step
        return True


def local(
    tokens,
    condition,
    clip_lengths,
    ada_weight,
    spatial_qkv,
    spatial_out,
    temporal_qkv,
    temporal_out,
    mlp_up,
    mlp_down,
    cotangent,
):
    n = lax.axis_size("frame")
    i = lax.axis_index("frame")
    idx = i.reshape(1).astype(jnp.int32)
    packs, f, patches = tokens.shape[:3]
    rows = patches // n
    count = packs // CHUNKS
    top = n // 2
    send = lambda parts: [parts[0]] + [swap(parts[k], "frame", k) for k in range(1, n)]

    own_cond = condition.reshape(packs * f, D)
    pad = -(-packs * f // GROUP) * GROUP
    cond_rows = jnp.concatenate([own_cond, jnp.zeros((pad - packs * f, D), BF16)], axis=0)

    def cut(k):
        v = lax.dynamic_slice_in_dim(cotangent, (i ^ k) * rows, rows, 2)
        return jnp.concatenate([v.reshape(-1, D), cond_rows], axis=0)

    ct = send([cut(k) for k in range(n)])
    sq_t = spatial_qkv.T
    tq_t = temporal_qkv.T
    frame_ids = jnp.concatenate([(i ^ k) * f + jnp.arange(f, dtype=jnp.int32) for k in range(n)])
    ends = [jnp.sum(clip_lengths[:, : j + 1], axis=1) for j in range(clip_lengths.shape[1])]
    segment = sum((e[:, None] <= frame_ids[None, :]).astype(jnp.int32) for e in ends)

    fwd = []
    source = tokens
    for c in range(CHUNKS):
        res = call_spatial_fwd(idx, source, condition, ada_weight, sq_t, spatial_out, c * count, count, n)
        slots = list(res[5:])
        if c:
            slots = tie_all(slots, *fwd[-1][1][1:])
        fwd.append((res[:5], send(slots)))
        if c == 0:
            source = tie(tokens, segment, tq_t, *ct[1:-1])

    init, mids = [], []
    for c in range(CHUNKS):
        last = c == CHUNKS - 1
        res = call_middle(
            idx, segment, fwd[c][1], ct, ada_weight, tq_t, temporal_qkv, temporal_out, mlp_up, mlp_down,
            init, c * count, last, packs,
        )
        init = [res[2 * n], *res[n : 2 * n]]
        res = list(res)
        if c:
            res = tie_all(res, *mids[-1][1:])
        mids.append(send(res[:n]))
    order = Order()
    early = Summing(order, res[2 * n], res[2 * n + 1], 3)
    outs = res[n : 2 * n]
    outs[top] = swap(outs[top], "frame", top)

    acc, backs = [], []
    for c in range(CHUNKS):
        last = c == CHUNKS - 1
        qkv, mix, br, tot, mod = fwd[c][0]
        dl = mids[c]
        if c:
            early.advance(after=backs[-1][2])
            dl = tie_all(dl, early.sent)
            for k in range(1, n):
                if k != top:
                    outs[k] = swap(tie(outs[k], early.sent), "frame", k)
        res = call_spatial_bwd(
            idx, tokens, cotangent, mod, qkv, mix, br, tot, spatial_out, acc, dl, c * count, last
        )
        acc = list(res[3:])
        backs.append(res)
    early.advance(after=backs[-1][2])
    late = Summing(order, acc[0], acc[1], 2)
    lasts, held = [], []
    for c in range(CHUNKS):
        last = c == CHUNKS - 1
        dqkv, ga = backs[c][:2]
        if c:
            early.advance(after=lasts[-1][2])
            late.advance(after=lasts[-1][2])
        ga = tie(ga, early.sent, late.moving if c == 0 else late.sent) if c else tie(ga, early.sent)
        more = [own_cond, *[b[2] for b in backs], *[v[2] for v in lasts]] if last else None
        res = call_last(idx, tokens, fwd[c][0][4], spatial_qkv, dqkv, ga, outs, c * count, more, held)
        held = list(res[:2])
        lasts.append(res)
    grad_tokens, output = held
    rows_of = lasts[-1][2]
    early.advance(after=rows_of)
    late.advance(after=rows_of)
    gather = late.beside = Gathering(rows_of, late.steps)
    early_shapes = [(D, MLP), (MLP, D), (D, 3 * D), (D, D)]
    late_shapes = [(D, 3 * D), (D, D)]
    half = None
    live = {"late": late, "early": early}
    skipped = False
    while live:
        for name in list(live):
            if name == "early" and len(early.back) == 0 and not skipped:
                skipped = True
            elif not live[name].advance():
                del live[name]
        if half is None and "early" not in live:
            half = call_finish(finish_early, early_shapes, idx, early.keep, 0, [])
            late.moving = tie(late.moving, half[3])
    own = rows_of[:, : 9 * D]
    back = jnp.einsum("tj,ij->ti", own, ada_weight, preferred_element_type=F32).reshape(packs, f, D)
    cf = condition.astype(F32)
    sig = 1.0 / (1.0 + jnp.exp(-cf))
    grad_condition = back * (sig * (1.0 + cf * (1.0 - sig)))

    late_half = call_finish(finish_late, late_shapes, idx, tie(late.keep, half[3]), 0, [])
    turn = turned_blocks(late.steps[: late.halvings][::-1])
    grad_ada = call_ada_grad(turn, idx, gather.rows, tie(gather.other, late_half[1]))
    late_other = tie(late.other, grad_ada)
    s_qkv, s_out = call_finish(finish_late, late_shapes, idx, late_other, 1, list(late_half))
    early_other = tie(early.other, s_out)
    up, down, t_qkv, t_out = call_finish(finish_early, early_shapes, idx, early_other, 1, list(half))
    return (output, grad_tokens, grad_condition, grad_ada, s_qkv, s_out, t_qkv, t_out, up, down)


def solution(mesh):
    tok = P("pack", "frame", None, None)
    cond = P("pack", "frame", None)
    return jax.shard_map(
        local,
        mesh=mesh,
        in_specs=(tok, cond, P("pack", None), P(), P(), P(), P(), P(), P(), P(), tok),
        out_specs=(tok, tok, cond, P(), P(), P(), P(), P(), P(), P()),
        check_vma=False,
    )
```
